32 devices in a mesh: grp: 4 (over y, x), dp: 8 (over z, core).
Axes of the slice: x: 2, y: 2, z: 4, core: 2. Of those that a mesh axis runs over, the one named last changes fastest.
Arguments:
- features: bfloat16 [32, 1024, 512], P(('grp', 'dp')), may hold values from -6 to 6
- segment_lengths: int32 [32, 4], P(('grp', 'dp')), may hold values from 1 to 512, 1024 in all within a row
- subnet_config: int32 [4, 3], P('grp'), may hold values from 8 to 3072, as said below
- cotangent: bfloat16 [32, 1024, 768], P(('grp', 'dp')), may hold values from -6 to 6
- projection_weight: float32 [512, 768], P(('grp', 'dp')), may hold values from -0.25 to 0.25
- projection_moment: float32 [512, 768], P(('grp', 'dp')), may hold values from -80 to 80
- projection_square: float32 [512, 768], P(('grp', 'dp')), may hold values from 16.384 to 65.536
- attention_weight: float32 [3, 768, 768], P(None, ('grp', 'dp')), may hold values from -0.21875 to 0.21875
- attention_moment: float32 [3, 768, 768], P(None, ('grp', 'dp')), may hold values from -28 to 28
- attention_square: float32 [3, 768, 768], P(None, ('grp', 'dp')), may hold values from 1.6384 to 6.5536
- output_weight: float32 [768, 768], P(('grp', 'dp')), may hold values from -1.75 to 1.75
- output_moment: float32 [768, 768], P(('grp', 'dp')), may hold values from -12 to 12
- output_square: float32 [768, 768], P(('grp', 'dp')), may hold values from 0.32768 to 1.31072
- feedforward_weight: float32 [2, 768, 3072], P(None, ('grp', 'dp')), may hold values from -0.21875 to 0.21875
- feedforward_moment: float32 [2, 768, 3072], P(None, ('grp', 'dp')), may hold values from -48 to 48
- feedforward_square: float32 [2, 768, 3072], P(None, ('grp', 'dp')), may hold values from 4.9152 to 19.6608
- small_params: float32 [11008], P(('grp', 'dp')), may hold values from -0.4 to 1.3, as said below
- small_moment: float32 [11008], P(('grp', 'dp')), may hold values from -80 to 80
- small_square: float32 [11008], P(('grp', 'dp')), may hold values from 16.384 to 65.536
Outputs:
- activations: bfloat16 [32, 1024, 768], P(('grp', 'dp'))
- input_gradient: float32 [32, 1024, 512], P(('grp', 'dp'))
- projection_gradient: float32 [512, 768], P(('grp', 'dp'))
- projection_moment_new: float32 [512, 768], P(('grp', 'dp'))
- projection_square_new: float32 [512, 768], P(('grp', 'dp'))
- projection_updated: float32 [512, 768], P(('grp', 'dp'))
- attention_gradient: float32 [3, 768, 768], P(None, ('grp', 'dp'))
- attention_moment_new: float32 [3, 768, 768], P(None, ('grp', 'dp'))
- attention_square_new: float32 [3, 768, 768], P(None, ('grp', 'dp'))
- attention_updated: float32 [3, 768, 768], P(None, ('grp', 'dp'))
- output_gradient: float32 [768, 768], P(('grp', 'dp'))
- output_moment_new: float32 [768, 768], P(('grp', 'dp'))
- output_square_new: float32 [768, 768], P(('grp', 'dp'))
- output_updated: float32 [768, 768], P(('grp', 'dp'))
- feedforward_gradient: float32 [2, 768, 3072], P(None, ('grp', 'dp'))
- feedforward_moment_new: float32 [2, 768, 3072], P(None, ('grp', 'dp'))
- feedforward_square_new: float32 [2, 768, 3072], P(None, ('grp', 'dp'))
- feedforward_updated: float32 [2, 768, 3072], P(None, ('grp', 'dp'))
- small_gradient: float32 [11008], P(('grp', 'dp'))
- small_moment_new: float32 [11008], P(('grp', 'dp'))
- small_square_new: float32 [11008], P(('grp', 'dp'))
- small_updated: float32 [11008], P(('grp', 'dp'))
The draws below stay inside these ranges and needn't reach their ends.
Inputs may be any that keep to these rules, and one draw needn't show every extreme that they name: `subnet_config`: each row is (E, H, F) with E one of 512, 640, 768; H one of 8, 10, 12; F = E * k // 2 with k one of 6, 7, 8. Some group has (768, 12, 3072) and some other group (512, 8, 1536). `small_params`: the three gains g0, g1, g2 lie in 0.7 to 1.3, all biases in -0.4 to 0.4.
All inputs are finite; a program needn't handle non-finite values.
Results may differ from the reference program's by a relative error of at most 0.017.
The reference program's roundings to bfloat16 on the way count: a program that leaves them out, or rounds other values in their place, can miss the bound.
Values may be sent and summed in bfloat16 or wider, within the bound.
A program may use at most 256 MiB of HBM per device.

```python
import math
import jax
import jax.numpy as jnp
import numpy as np
from jax import lax

D = 768
HEADS = 12
FF = 3072
FEAT = 512
HDIM = 64
ROW_LEN = 1024
NSEG = 4
STEP = 10
SEG_MOST = 512
QBLK = 512
GROUPS = 4
GROUP_ROWS = 8
ROWS = 32
TOKENS = 32768
VEC = 11008


def draw_subnet_config(key, part):
    keys = jax.random.split(key, 4)
    pick_width = jax.random.randint(keys[0], (GROUPS,), 0, 3)
    pick_heads = jax.random.randint(keys[1], (GROUPS,), 0, 3)
    pick_ratio = jax.random.randint(keys[2], (GROUPS,), 0, 3)
    order = jax.random.permutation(keys[3], GROUPS)
    places = jnp.arange(GROUPS)
    largest = places == order[0]
    smallest = places == order[1]
    pick_width = jnp.where(largest, 2, jnp.where(smallest, 0, pick_width))
    pick_heads = jnp.where(largest, 2, jnp.where(smallest, 0, pick_heads))
    pick_ratio = jnp.where(largest, 2, jnp.where(smallest, 0, pick_ratio))
    width_table = jnp.array([D * 2 // 3, D * 5 // 6, D], dtype=jnp.int32)
    heads_table = jnp.array([HEADS * 2 // 3, HEADS * 5 // 6, HEADS], dtype=jnp.int32)
    widths = width_table[pick_width]
    heads = heads_table[pick_heads]
    hidden = widths * (6 + pick_ratio.astype(jnp.int32)) // 2
    return jnp.stack([widths, heads, hidden], axis=1).astype(jnp.int32)


def draw_small_params(key, part):
    keys = jax.random.split(key, 2)
    biases = jax.random.uniform(keys[0], (VEC,), jnp.float32, -0.4, 0.4)
    gains = 1.0 + jax.random.uniform(keys[1], (VEC,), jnp.float32, -0.3, 0.3)
    position = jnp.arange(VEC)
    attn_start = 2 * FEAT + 4 * D
    final_start = 2 * FEAT + 7 * D + FF
    is_gain = (position < FEAT) | (position >= attn_start) & (position < attn_start + D) | (position >= final_start) & (position < final_start + D)
    return jnp.where(is_gain, gains, biases).astype(jnp.float32)


def steps_of(rng, dims, cuts, least, high):
    def one(dim, parts):
        heights = jax.random.uniform(jax.random.fold_in(jax.random.fold_in(rng, 6), dim), (parts,), jnp.float32, least / len(cuts), high / len(cuts))
        return jnp.repeat(jnp.exp(heights), dims[dim] // parts).reshape((-1,) + (1,) * (len(dims) - dim - 1))

    level = one(*cuts[0])
    for cut in cuts[1:]:
        level = level * one(*cut)
    return level


def profile(count, total, bound, skew):
    loads = [(1 << 20) // math.isqrt(grade ** skew) + 1 for grade in range(2, count + 1)]
    surplus, given = total - bound - (count - 1), [1] * (count - 1)
    while surplus > 0:
        candidates = [i for i in range(count - 1) if given[i] < bound]
        whole, budget = sum([loads[i] for i in candidates]), surplus
        for i in candidates:
            addition = min(bound - given[i], max(1, budget * loads[i] // whole), surplus)
            given[i] = given[i] + addition
            surplus = surplus - addition
    return np.array([bound] + given)


def uneven(stream_key, count, total, most, lean):
    if count == 2:
        one = jax.random.randint(stream_key, (), max(1, total - most), min(most, total - 1) + 1)
        return jnp.stack([one, total - one])
    sizes = jnp.asarray(profile(count, total, most, lean), jnp.int32)
    couples = (count - 1) // 2
    giver, taker = sizes[1:1 + 2 * couples:2], sizes[2:2 + 2 * couples:2]
    slack = jnp.minimum(giver - 1, most - taker)
    shifted = jax.random.randint(jax.random.fold_in(stream_key, 1), (couples,), 0, 1 << 20) % (slack + 1)
    sizes = sizes.at[1:1 + 2 * couples:2].set(giver - shifted).at[2:2 + 2 * couples:2].set(taker + shifted)
    return sizes[jax.random.permutation(jax.random.fold_in(stream_key, 2), count)]


def scatter_about(key, shape, scale, most, cuts=(), held_as=jnp.bfloat16):
    values = scale * jax.random.normal(key, shape, jnp.float32)
    if cuts:
        values = values * steps_of(key, shape, cuts, -0.22, 0.18)
    return jnp.clip(values, -most, most).astype(held_as)


def setup_inputs(seed: int = 0) -> dict:
    key_of = jax.random.split(jax.random.key(seed), 20)
    return {
        "features": scatter_about(key_of[0], (ROWS, ROW_LEN, FEAT), 1.0, 6.0, ((0, 32),)),
        "segment_lengths": jax.vmap(lambda own: uneven(own, NSEG, ROW_LEN, SEG_MOST, 1))(jax.random.split(key_of[1], ROWS)).reshape((ROWS, NSEG)).astype(jnp.int32),
        "subnet_config": draw_subnet_config(jax.random.fold_in(key_of[19], 71), 0),
        "cotangent": scatter_about(key_of[3], (ROWS, ROW_LEN, D), 1.0, 6.0, ((0, 32),)),
        "projection_weight": scatter_about(key_of[4], (FEAT, D), FEAT ** -0.5, 0.25, ((0, 32),), jnp.float32),
        "projection_moment": scatter_about(key_of[5], (FEAT, D), (0.08 * TOKENS ** 0.5), 80.0, ((0, 32),), jnp.float32),
        "projection_square": jnp.clip(jnp.exp(math.log(65.536) - 1.3862944 * jax.random.uniform(key_of[6], (FEAT, D), jnp.float32) ** steps_of(key_of[6], (FEAT, D), ((0, 32),), -0.2, 0.2)), 16.384, 65.536),
        "attention_weight": scatter_about(key_of[7], (3, D, D), D ** -0.5, 0.21875, ((1, 32),), jnp.float32),
        "attention_moment": scatter_about(key_of[8], (3, D, D), (0.025 * TOKENS ** 0.5), 28.0, ((1, 32),), jnp.float32),
        "attention_square": jnp.clip(jnp.exp(math.log(6.5536) - 1.3862944 * jax.random.uniform(key_of[9], (3, D, D), jnp.float32) ** steps_of(key_of[9], (3, D, D), ((1, 32),), -0.2, 0.2)), 1.6384, 6.5536),
        "output_weight": scatter_about(key_of[10], (D, D), HEADS ** -0.5, 1.75, ((0, 32),), jnp.float32),
        "output_moment": scatter_about(key_of[11], (D, D), (0.011 * TOKENS ** 0.5), 12.0, ((0, 32),), jnp.float32),
        "output_square": jnp.clip(jnp.exp(math.log(1.31072) - 1.3862944 * jax.random.uniform(key_of[12], (D, D), jnp.float32) ** steps_of(key_of[12], (D, D), ((0, 32),), -0.2, 0.2)), 0.32768, 1.31072),
        "feedforward_weight": scatter_about(key_of[13], (2, D, FF), D ** -0.5, 0.21875, ((1, 32),), jnp.float32),
        "feedforward_moment": scatter_about(key_of[14], (2, D, FF), (0.045 * TOKENS ** 0.5), 48.0, ((1, 32),), jnp.float32),
        "feedforward_square": jnp.clip(jnp.exp(math.log(19.6608) - 1.3862944 * jax.random.uniform(key_of[15], (2, D, FF), jnp.float32) ** steps_of(key_of[15], (2, D, FF), ((1, 32),), -0.2, 0.2)), 4.9152, 19.6608),
        "small_params": draw_small_params(jax.random.fold_in(key_of[19], 71), 0),
        "small_moment": scatter_about(key_of[17], (VEC,), (0.08 * TOKENS ** 0.5), 80.0, ((0, 32),), jnp.float32),
        "small_square": jnp.clip(jnp.exp(math.log(65.536) - 1.3862944 * jax.random.uniform(key_of[18], (VEC,), jnp.float32) ** steps_of(key_of[18], (VEC,), ((0, 32),), -0.2, 0.2)), 16.384, 65.536),
    }


@jax.custom_vjp
def low(v):
    return lax.optimization_barrier(v.astype(jnp.bfloat16)).astype(jnp.float32)

@jax.custom_vjp
def low_back(v):
    return v

def low_keep(v):
    return (low(v), None)

def low_pass(kept, grad):
    return (grad,)

def back_keep(v):
    return (v, None)

def back_low(kept, grad):
    return (low(grad),)
low.defvjp(low_keep, low_pass)
low_back.defvjp(back_keep, back_low)
NORM_EPS = 1e-05
RATE = 0.08
SMALL_RATE = 0.3
BETA_ONE = 0.9
BETA_TWO = 0.999
ADAM_EPS = 1e-08
DECAY = 0.01
FULL_PRECISION = lax.Precision.HIGHEST

def vector_pieces(vector):
    widths = [FEAT, FEAT, D, D, D, D, D, D, FF, D, D, D]
    pieces = []
    offset = 0
    for width in widths:
        pieces.append(vector[offset:offset + width])
        offset = offset + width
    return pieces

def plain_norm(value, gain, shift):
    centre = lax.optimization_barrier(jnp.mean(value, -1, keepdims=True))
    centred = value - centre
    spread = lax.optimization_barrier(jnp.mean(centred * centred, -1, keepdims=True))
    return centred * lax.rsqrt(spread + NORM_EPS) * gain + shift

def masked_norm(value, gain, shift, keep, count):
    centre = lax.optimization_barrier(jnp.sum(value * keep, -1, keepdims=True)) / count
    centred = (value - centre) * keep
    spread = lax.optimization_barrier(jnp.sum(centred * centred, -1, keepdims=True)) / count
    return (centred * lax.rsqrt(spread + NORM_EPS) * gain + shift) * keep

def matmul(left, right):
    return jnp.dot(left, right, precision=FULL_PRECISION)

def attend(query, key, value, segment):
    scale = 1.0 / math.sqrt(HDIM)
    query_blocks = query.reshape(ROW_LEN // QBLK, QBLK, HEADS, HDIM)
    segment_blocks = segment.reshape(ROW_LEN // QBLK, QBLK)
    keys = key.reshape(ROW_LEN, HEADS, HDIM)
    values = value.reshape(ROW_LEN, HEADS, HDIM)

    def block(inputs):
        block_query, block_segment = inputs
        raw = low_back(jnp.einsum('qhd,khd->hqk', block_query, keys, precision=FULL_PRECISION))
        same = block_segment[:, None] == segment[None, :]
        scores = jnp.where(same[None], raw * scale, -1e+30)
        weights = low(jax.nn.softmax(scores, axis=-1))
        mixed = jnp.einsum('hqk,khd->qhd', weights, values, precision=FULL_PRECISION)
        return mixed.reshape(QBLK, D)
    return lax.map(jax.checkpoint(block), (query_blocks, segment_blocks)).reshape(ROW_LEN, D)

def forward_row(params, feat_row, segment, keep_width, keep_heads, keep_hidden, count):
    input_matrix, triple_matrix, output_matrix, feedforward, vector = [low(item) for item in params]
    feat_gain, feat_bias, proj_bias, query_bias, value_bias, out_bias, attn_gain, attn_shift, hidden_bias, down_bias, final_gain, final_shift = vector_pieces(vector)
    normed = plain_norm(feat_row, feat_gain, feat_bias)
    hidden = low_back((matmul(low(normed), input_matrix) + proj_bias) * keep_width)
    hidden_low = low(hidden)
    query = low(low_back((matmul(hidden_low, triple_matrix[0]) + query_bias) * keep_heads))
    key = low(low_back(matmul(hidden_low, triple_matrix[1]) * keep_heads))
    value = low(low_back((matmul(hidden_low, triple_matrix[2]) + value_bias) * keep_heads))
    mixed = low(low_back(attend(query, key, value, segment)))
    branch = low_back((matmul(mixed, output_matrix) + out_bias) * keep_width)
    first = masked_norm(hidden + branch, attn_gain, attn_shift, keep_width, count)
    inner = low_back((matmul(low(first), feedforward[0]) + hidden_bias) * keep_hidden)
    active = low(jax.nn.gelu(inner, approximate=False))
    down = low_back((matmul(active, feedforward[1].T) + down_bias) * keep_width)
    return masked_norm(first + down, final_gain, final_shift, keep_width, count)

def adam(weight, moment, square, grad, rate):
    moment_new = BETA_ONE * moment + (1.0 - BETA_ONE) * grad
    square_new = BETA_TWO * square + (1.0 - BETA_TWO) * grad * grad
    fix_one = 1.0 - BETA_ONE ** STEP
    fix_two = 1.0 - BETA_TWO ** STEP
    direction = moment_new / fix_one / (jnp.sqrt(square_new / fix_two) + ADAM_EPS)
    return (moment_new, square_new, weight - rate * (direction + DECAY * weight))

def reference(features, segment_lengths, subnet_config, cotangent, projection_weight, projection_moment, projection_square, attention_weight, attention_moment, attention_square, output_weight, output_moment, output_square, feedforward_weight, feedforward_moment, feedforward_square, small_params, small_moment, small_square):
    params = (projection_weight, attention_weight, output_weight, feedforward_weight, small_params)
    row_configs = jnp.repeat(subnet_config, GROUP_ROWS, axis=0)
    positions = jnp.arange(ROW_LEN, dtype=jnp.int32)
    columns = jnp.arange(D, dtype=jnp.int32)
    units = jnp.arange(FF, dtype=jnp.int32)

    def per_row(totals, inputs):
        feat_row, lengths, config, cot_row = inputs
        ends = jnp.cumsum(lengths)
        segment = lax.optimization_barrier(jnp.sum((positions[:, None] >= ends[None, :]).astype(jnp.int32), -1))
        keep_width = (columns < config[0]).astype(jnp.float32)
        keep_heads = (columns < config[1] * HDIM).astype(jnp.float32)
        keep_hidden = (units < config[2]).astype(jnp.float32)
        count = config[0].astype(jnp.float32)

        def run(weights, feats):
            return forward_row(weights, feats, segment, keep_width, keep_heads, keep_hidden, count)
        out_row, pull = jax.vjp(run, params, feat_row.astype(jnp.float32))
        grads, feat_grad = pull(cot_row.astype(jnp.float32))
        totals = jax.tree.map(jnp.add, totals, grads)
        return (totals, (out_row.astype(jnp.bfloat16), 0.1 * feat_grad))
    start = jax.tree.map(jnp.zeros_like, params)
    totals, (activations, input_gradient) = lax.scan(per_row, start, (features, segment_lengths, row_configs, cotangent))
    proj_m, proj_v, proj_w = adam(projection_weight, projection_moment, projection_square, totals[0], RATE)
    attn_m, attn_v, attn_w = adam(attention_weight, attention_moment, attention_square, totals[1], RATE)
    out_m, out_v, out_w = adam(output_weight, output_moment, output_square, totals[2], RATE)
    ffn_m, ffn_v, ffn_w = adam(feedforward_weight, feedforward_moment, feedforward_square, totals[3], RATE)
    small_m, small_v, small_w = adam(small_params, small_moment, small_square, totals[4], SMALL_RATE)
    return (activations, input_gradient, totals[0], proj_m, proj_v, proj_w, totals[1], attn_m, attn_v, attn_w, totals[2], out_m, out_v, out_w, totals[3], ffn_m, ffn_v, ffn_w, totals[4], small_m, small_v, small_w)
```

```python
import functools
import math

import jax
import jax.numpy as jnp
from jax import lax
from jax.experimental import pallas as pl
from jax.experimental.pallas import tpu as pltpu
from jax.sharding import PartitionSpec as P

D = 768
FF = 3072
FEAT = 512
HDIM = 64
HEADS = 12
PAIRS = HEADS // 2
LEN = 1024
STEP = 10
TILE = 256
NT = LEN // TILE
VEC = 11008

NORM_EPS = 1e-05
RATE = 0.08
SMALL_RATE = 0.3
BETA_ONE = 0.9
BETA_TWO = 0.999
ADAM_EPS = 1e-08
DECAY = 0.01

F32 = jnp.float32
BF16 = jnp.bfloat16
BIG = 2.0**100
VMEM_LIMIT = 63 << 20

WIDTHS = dict(
    g0=FEAT, b0=FEAT, bp=D, bq=D, bv=D, bo=D, g1=D, c1=D, b1=FF, b2=D, g2=D, c2=D
)
OFFSETS = {}
_at = 0
for _name, _width in WIDTHS.items():
    OFFSETS[_name] = _at
    _at += _width

KEY_RANGE = [
    (max(0, (i * TILE - 511) // TILE * TILE), min(LEN, -(-(i * TILE + TILE + 511) // TILE) * TILE))
    for i in range(NT)
]


def mm(a, b):
    return jnp.dot(a, b, preferred_element_type=F32)


def mm_nt(a, b):
    return lax.dot_general(a, b, (((1,), (1,)), ((), ())), preferred_element_type=F32)


def piece(ref, name, start=0, width=None):
    begin = OFFSETS[name] + start
    return ref[0:1, begin : begin + (width or WIDTHS[name])]


def put(ref, name, value, start=0):
    begin = OFFSETS[name] + start
    ref[0:1, begin : begin + value.shape[1]] = value


def keep_row(width, limit, start=0):
    lane = lax.broadcasted_iota(jnp.int32, (1, width), 1) + start
    return (lane < limit).astype(F32)


def col_sum(value):
    return jnp.sum(value, 0, keepdims=True)


def row_sum(value):
    return jnp.sum(value, 1, keepdims=True)


def rows_of(t):
    return pl.ds(pl.multiple_of(t * TILE, TILE), TILE)


def lanes_of(p, width=128):
    return pl.ds(pl.multiple_of(p * width, width), width)


def gelu_both(u):
    half = jnp.exp(-0.5 * u * u)
    t = 1.0 / (1.0 + (0.3275911 * 0.7071067811865476) * jnp.abs(u))
    poly = 0.5 * 1.061405429
    for c in (-1.453152027, 1.421413741, -0.284496736, 0.254829592):
        poly = poly * t + 0.5 * c
    tail = poly * t * half
    cdf = jnp.where(u >= 0.0, 1.0 - tail, tail)
    return u * cdf, cdf + u * (half * 0.3989422804014327)


def fill_patterns(seg_ref, kpat, qpat):
    e0 = seg_ref[0, 0]
    e1 = e0 + seg_ref[0, 1]
    e2 = e1 + seg_ref[0, 2]

    @pl.loop(0, NT)
    def _(t):
        pos = lax.broadcasted_iota(jnp.int32, (TILE, 128), 0) + t * TILE
        lane = lax.broadcasted_iota(jnp.int32, (TILE, 128), 1)
        seg = (
            (pos >= e0).astype(jnp.int32)
            + (pos >= e1).astype(jnp.int32)
            + (pos >= e2).astype(jnp.int32)
        )
        for e in range(2):
            slot = lane - (64 if e == 0 else 0)
            valid = (slot >= 0) & (slot < 4)
            same = slot == seg
            kpat[e, rows_of(t), :] = jnp.where(same, 1.0, 0.0).astype(BF16)
            qpat[e, rows_of(t), :] = jnp.where(valid & (slot != seg), -BIG, 0.0).astype(BF16)


def half_mask(e):
    lane = lax.broadcasted_iota(jnp.int32, (1, 128), 1)
    return ((lane < 64) if e == 0 else (lane >= 64)).astype(F32).astype(BF16)


def norm0(feat, svec, rows):
    x = feat[rows, :].astype(F32)
    centred = x - row_sum(x) * (1.0 / FEAT)
    inv = lax.rsqrt(row_sum(centred * centred) * (1.0 / FEAT) + NORM_EPS)
    hat = centred * inv
    normed = (hat * piece(svec, "g0") + piece(svec, "b0")).astype(BF16)
    return hat, inv, normed


def forward_kernel(
    upto,
    seg_ref, cfg_ref, feat_hbm, cot_hbm, wg_hbm, wp_hbm, svec_in,
    act_out, hl_out, hlt_out, qkv_out, kt_out, mixed_out, mixedt_out, xh1_out, inv1_out, flt_out,
    active_out, gp_out, d2_out, dg_out, dgt_out, lse_out, sg_out,
    feat, cot, wg, wp, hid, hl, hlt, qkv, kt, vt, mixed, mixedt, xh1, fl, flt, active, gp, dg, dgt, act,
    kpat, qpat, sem_in, sem_out,
):
    svec = svec_in
    outs = []

    def load(i, src, dst):
        copy = pltpu.make_async_copy(src, dst, sem_in.at[i])
        copy.start()
        return copy

    def save(src, dst):
        copy = pltpu.make_async_copy(src, dst, sem_out.at[len(outs)])
        copy.start()
        outs.append(copy)

    c_feat = load(0, feat_hbm, feat)
    c_wp = load(1, wp_hbm, wp)
    c_w = [load(2 + u, wg_hbm.at[u], wg.at[u]) for u in range(12)]
    c_cot = load(14, cot_hbm, cot)

    width = cfg_ref[0, 0]
    count = 1.0 / width.astype(F32)
    fill_patterns(seg_ref, kpat, qpat)
    c_feat.wait()
    c_wp.wait()

    @pl.loop(0, NT)
    def _(t):
        rows = rows_of(t)
        normed = norm0(feat, svec, rows)[2]
        h = (mm(normed, wp[...]) + piece(svec, "bp")) * keep_row(D, width)
        hid[rows, :] = h
        low = h.astype(BF16)
        hl[rows, :] = low
        hlt[:, rows] = low.T

    save(hl, hl_out)
    save(hlt, hlt_out)
    for u in range(3):
        c_w[u].wait()

    @pl.loop(0, NT)
    def _(t):
        rows = rows_of(t)
        keep = keep_row(D, cfg_ref[0, 1] * HDIM)
        low = hl[rows, :]
        qkv[0, rows, :] = ((mm(low, wg[0]) + piece(svec, "bq")) * keep).astype(BF16)
        k = (mm(low, wg[1]) * keep).astype(BF16)
        qkv[1, rows, :] = k
        kt[:, rows] = k.T
        v = ((mm(low, wg[2]) + piece(svec, "bv")) * keep).astype(BF16)
        qkv[2, rows, :] = v
        vt[:, rows] = v.T

    save(qkv, qkv_out)
    save(kt, kt_out)

    if upto >= 2:

        @pl.loop(0, PAIRS)
        def _(p):
            lanes = lanes_of(p)
            for e in range(2):
                kaug = qkv[1, :, lanes] * half_mask(e) + kpat[e]
                head_rows = pl.ds(pl.multiple_of(p * 128 + 64 * e, 64), 64)
                for b in range(NT):
                    lo, hi = KEY_RANGE[b]
                    cols = slice(b * TILE, (b + 1) * TILE)
                    qaug = qkv[0, cols, lanes] * (half_mask(e) * 0.125) + qpat[e, cols, :]
                    st = mm_nt(kaug[lo:hi], qaug)
                    peak = jnp.max(st, 0, keepdims=True)
                    power = jnp.exp(st - peak)
                    total = col_sum(power)
                    ot = mm(vt[head_rows, lo:hi], power.astype(BF16))
                    mixedt[head_rows, cols] = (ot * (1.0 / total)).astype(BF16)
                    lse_out[pl.ds(2 * p + e, 1), cols] = peak + jnp.log(total)

    save(mixedt, mixedt_out)
    c_w[3].wait()

    if upto >= 3:

        @pl.loop(0, NT)
        def _(t):
            rows = rows_of(t)
            keep = keep_row(D, width)
            mix = mixedt[:, rows].T
            mixed[rows, :] = mix
            z = hid[rows, :] + (mm(mix, wg[3]) + piece(svec, "bo")) * keep
            centred = (z - row_sum(z * keep) * count) * keep
            inv = lax.rsqrt(row_sum(centred * centred) * count + NORM_EPS)
            hat = centred * inv
            first = (hat * piece(svec, "g1") + piece(svec, "c1")) * keep
            xh1[rows, :] = hat.astype(BF16)
            inv1_out[rows, :] = jnp.broadcast_to(inv, (TILE, 128))
            hid[rows, :] = first + piece(svec, "b2") * keep
            low = first.astype(BF16)
            fl[rows, :] = low
            flt[:, rows] = low.T

    save(mixed, mixed_out)
    save(xh1, xh1_out)
    save(flt, flt_out)

    if upto >= 4:
        for q in range(4):
            c_w[4 + q].wait()
            c_w[8 + q].wait()

            @pl.loop(0, NT)
            def _(t, q=q):
                rows = rows_of(t)
                u = (mm(fl[rows, :], wg[4 + q]) + piece(svec, "b1", q * D, D)) * keep_row(
                    D, cfg_ref[0, 2], q * D
                )
                g, slope = gelu_both(u)
                low = g.astype(BF16)
                active[q, rows, :] = low
                gp[q, rows, :] = slope.astype(BF16)
                hid[rows, :] += mm_nt(low, wg[8 + q]) * keep_row(D, width)

            save(active.at[q], active_out.at[q])
            save(gp.at[q], gp_out.at[q])
    c_cot.wait()
    if upto < 4:
        for q in range(8):
            c_w[4 + q].wait()

    zero = jnp.zeros((1, D), F32)

    def last(t, sums):
        gain_sum, shift_sum, bias_sum = sums
        rows = rows_of(t)
        keep = keep_row(D, width)
        z = hid[rows, :]
        centred = (z - row_sum(z * keep) * count) * keep
        inv = lax.rsqrt(row_sum(centred * centred) * count + NORM_EPS)
        hat = centred * inv
        gain = piece(svec, "g2")
        act[rows, :] = ((hat * gain + piece(svec, "c2")) * keep).astype(BF16)
        g = cot[rows, :].astype(F32) * keep
        gain_sum = gain_sum + col_sum(g * hat)
        shift_sum = shift_sum + col_sum(g)
        a = g * gain
        d2 = inv * (a - keep * (row_sum(a) * count) - hat * (row_sum(a * hat) * count))
        hid[rows, :] = d2
        low = d2.astype(BF16)
        dg[rows, :] = low
        dgt[:, rows] = low.T
        return gain_sum, shift_sum, bias_sum + col_sum(low.astype(F32))

    gain_sum, shift_sum, bias_sum = lax.fori_loop(0, NT, last, (zero, zero, zero))
    sg_out[...] = jnp.zeros((1, VEC), F32)
    put(sg_out, "g2", gain_sum)
    put(sg_out, "c2", shift_sum)
    put(sg_out, "b2", bias_sum)
    save(act, act_out)
    save(hid, d2_out)
    save(dg, dg_out)
    save(dgt, dgt_out)
    for copy in outs:
        copy.wait()


def backward_kernel(
    upto,
    seg_ref, cfg_ref, feat_hbm, wg_hbm, wp_hbm, svec,
    hlt_hbm, qkv_hbm, kt_hbm, mixed_hbm, mixedt_hbm, xh1_hbm, inv1_hbm, flt_hbm,
    active_hbm, gp_hbm, d2_hbm, dg_hbm, dgt_hbm, lse, sg_in,
    dx_out, gu_out, gwp_out, sg,
    feat, w2q, w1q, wo, wa, wp, hlt, qkv, kt, mixed, mixedt, xh1, inv1, flt, actq, gpq, ig, fg, dg, dgt,
    go, tg, delta, dqt, pbuf, dsbuf, gslot, dxs, kpat, qpat, nrmt, sem_in, sem_q, sem_g, sem_dx,
):
    def load(i, src, dst):
        copy = pltpu.make_async_copy(src, dst, sem_in.at[i])
        copy.start()
        return copy

    n_put = [0]

    def slot_wait(i):
        pltpu.make_async_copy(gslot.at[i], gu_out.at[0], sem_g.at[i]).wait()

    def new_slot():
        i = n_put[0] % 2
        if n_put[0] >= 2:
            slot_wait(i)
        return i

    def send_slot(i, dst):
        pltpu.make_async_copy(gslot.at[i], dst, sem_g.at[i]).start()
        n_put[0] += 1

    def quarter(q):
        s = q % 2
        copies = [
            pltpu.make_async_copy(src, dst, sem_q.at[s, i])
            for i, (src, dst) in enumerate(
                [
                    (active_hbm.at[q], actq.at[s]),
                    (wg_hbm.at[8 + q], w2q.at[s]),
                    (gp_hbm.at[q], gpq.at[s]),
                    (wg_hbm.at[4 + q], w1q.at[s]),
                ]
            )
        ]
        return copies

    c_dgt = load(0, dgt_hbm, dgt)
    for copy in quarter(0):
        copy.start()
    c_dg = load(1, dg_hbm, dg)
    c_flt = load(2, flt_hbm, flt)
    c_d2 = load(3, d2_hbm, fg)
    for copy in quarter(1):
        copy.start()
    c_xh1 = load(4, xh1_hbm, xh1)
    c_inv1 = load(5, inv1_hbm, inv1)
    c_mixed = load(6, mixed_hbm, mixed)
    c_mixedt = load(7, mixedt_hbm, mixedt)
    c_wo = load(8, wg_hbm.at[3], wo)
    c_qkv = load(9, qkv_hbm, qkv)
    c_kt = load(10, kt_hbm, kt)
    c_hlt = load(11, hlt_hbm, hlt)
    c_wa = [load(12 + i, wg_hbm.at[i], wa.at[i]) for i in range(3)]
    c_wp = load(15, wp_hbm, wp)
    c_feat = load(16, feat_hbm, feat)

    width = cfg_ref[0, 0]
    count = 1.0 / width.astype(F32)
    sg[...] = sg_in[...]
    fill_patterns(seg_ref, kpat, qpat)

    def weight_grad(left, right, dst, steps=D // TILE):
        @pl.loop(0, steps)
        def _(m):
            rows = rows_of(m)
            dst[rows, :] = mm(left[rows, :], right[...])

    c_dgt.wait()
    for q in range(4):
        s = q % 2
        copies = quarter(q)
        copies[0].wait()
        i = new_slot()
        weight_grad(dgt, actq.at[s], gslot.at[i])
        send_slot(i, gu_out.at[8 + q])
        if q == 0:
            c_dg.wait()
        copies[1].wait()
        copies[2].wait()

        def inner(t, bias, q=q, s=s):
            rows = rows_of(t)
            low = (
                mm(dg[rows, :], w2q[s])
                * gpq[s, rows, :].astype(F32)
                * keep_row(D, cfg_ref[0, 2], q * D)
            ).astype(BF16)
            ig[rows, :] = low
            return bias + col_sum(low.astype(F32))

        put(sg, "b1", lax.fori_loop(0, NT, inner, jnp.zeros((1, D), F32)), q * D)
        if q == 0:
            c_flt.wait()
            c_d2.wait()
        copies[3].wait()
        i = new_slot()
        weight_grad(flt, ig, gslot.at[i])
        send_slot(i, gu_out.at[4 + q])

        @pl.loop(0, NT)
        def _(t, s=s):
            rows = rows_of(t)
            fg[rows, :] += mm_nt(ig[rows, :], w1q[s])

        if q < 2:
            for copy in quarter(q + 2):
                copy.start()

    for copy in (c_xh1, c_inv1, c_mixed, c_mixedt, c_wo):
        copy.wait()
    zero = jnp.zeros((1, D), F32)

    def middle(t, sums):
        gain_sum, shift_sum, bias_sum = sums
        rows = rows_of(t)
        keep = keep_row(D, width)
        hat = xh1[rows, :].astype(F32)
        g = fg[rows, :] * keep
        gain_sum = gain_sum + col_sum(g * hat)
        shift_sum = shift_sum + col_sum(g)
        a = g * piece(svec, "g1")
        d1 = inv1[rows, 0:1] * (a - keep * (row_sum(a) * count) - hat * (row_sum(a * hat) * count))
        fg[rows, :] = d1
        low = d1.astype(BF16)
        dg[rows, :] = low
        mg = mm_nt(low, wo[...]).astype(BF16)
        go[rows, :] = mg
        product = mg.astype(F32) * mixed[rows, :].astype(F32)
        high = product.astype(BF16)
        rest = (product - high.astype(F32)).astype(BF16)
        lane = lax.broadcasted_iota(jnp.int32, (16, D), 1)
        head = lax.broadcasted_iota(jnp.int32, (16, D), 0)
        pick = ((lane >= head * HDIM) & (lane < head * HDIM + HDIM)).astype(F32).astype(BF16)
        delta[:, rows] = mm_nt(pick, high) + mm_nt(pick, rest)
        return gain_sum, shift_sum, bias_sum + col_sum(low.astype(F32))

    gain_sum, shift_sum, bias_sum = lax.fori_loop(0, NT, middle, (zero, zero, zero))
    put(sg, "g1", gain_sum)
    put(sg, "c1", shift_sum)
    put(sg, "bo", bias_sum)
    i = new_slot()
    weight_grad(mixedt, dg, gslot.at[i])
    send_slot(i, gu_out.at[3])

    c_qkv.wait()
    c_kt.wait()
    c_hlt.wait()
    for copy in c_wa:
        copy.wait()
    for j in range(3):
        if upto >= 2:

            @pl.loop(0, 2)
            def _(pp, j=j):
                p = j * 2 + pp
                lanes = lanes_of(p)
                vpair = qkv[2, :, lanes]
                for e in range(2):
                    kaug = qkv[1, :, lanes] * half_mask(e) + kpat[e]
                    head_rows = pl.ds(pl.multiple_of(p * 128 + 64 * e, 64), 64)
                    for b in range(NT):
                        lo, hi = KEY_RANGE[b]
                        cols = slice(b * TILE, (b + 1) * TILE)
                        qaug = qkv[0, cols, lanes] * (half_mask(e) * 0.125) + qpat[e, cols, :]
                        st = mm_nt(kaug[lo:hi], qaug)
                        weights = jnp.exp(st - lse[pl.ds(2 * p + e, 1), cols])
                        pbuf[e, lo:hi, cols] = weights.astype(BF16)
                        goe = go[cols, lanes] * half_mask(e)
                        dp = mm_nt(vpair[lo:hi], goe)
                        ds = (weights * (dp - delta[pl.ds(2 * p + e, 1), cols])).astype(BF16)
                        dsbuf[e, lo:hi, cols] = ds
                        dqt[64 * e : 64 * e + 64, cols] = mm(kt[head_rows, lo:hi], ds)
                        if b == 0:
                            pbuf[e, hi:LEN, cols] = jnp.zeros((LEN - hi, TILE), BF16)
                            dsbuf[e, hi:LEN, cols] = jnp.zeros((LEN - hi, TILE), BF16)
                        if b == NT - 1:
                            pbuf[e, 0:lo, cols] = jnp.zeros((lo, TILE), BF16)
                            dsbuf[e, 0:lo, cols] = jnp.zeros((lo, TILE), BF16)
                keep = keep_row(128, cfg_ref[0, 1] * HDIM - p * 128)
                out_lanes = lanes_of(pp)
                for t in range(NT):
                    rows = slice(t * TILE, (t + 1) * TILE)
                    tg[rows, out_lanes] = (dqt[:, rows].T * (keep * 0.125)).astype(BF16)
                    dk = jnp.zeros((TILE, 128), F32)
                    dv = jnp.zeros((TILE, 128), F32)
                    for e in range(2):
                        dk = dk + mm(dsbuf[e, rows, :], qkv[0, :, lanes] * half_mask(e))
                        dv = dv + mm(pbuf[e, rows, :], go[:, lanes] * half_mask(e))
                    tg[rows, pl.ds(pl.multiple_of(256 + pp * 128, 128), 128)] = (
                        dk * (keep * 0.125)
                    ).astype(BF16)
                    tg[rows, pl.ds(pl.multiple_of(512 + pp * 128, 128), 128)] = (dv * keep).astype(
                        BF16
                    )

        i = new_slot()
        weight_grad(hlt, tg, gslot.at[i])
        send_slot(i, gu_out.at[j])
        span = slice(256 * j, 256 * j + 256)

        def back(t, bias, span=span):
            rows = rows_of(t)
            total = fg[rows, :]
            for i in range(3):
                total = total + mm_nt(tg[rows, 256 * i : 256 * i + 256], wa[i, :, span])
            fg[rows, :] = total
            return bias + col_sum(tg[rows, :].astype(F32))

        bias = lax.fori_loop(0, NT, back, zero)
        put(sg, "bq", bias[:, 0:256], 256 * j)
        put(sg, "bv", bias[:, 512:768], 256 * j)

    c_wp.wait()
    c_feat.wait()
    zero_feat = jnp.zeros((1, FEAT), F32)

    def first(t, sums):
        gain_sum, shift_sum, bias_sum = sums
        rows = rows_of(t)
        hat, inv, normed = norm0(feat, svec, rows)
        nrmt[:, rows] = normed.T
        low = (fg[rows, :] * keep_row(D, width)).astype(BF16)
        dg[rows, :] = low
        g = mm_nt(low, wp[...])
        gain_sum = gain_sum + col_sum(g * hat)
        shift_sum = shift_sum + col_sum(g)
        a = g * piece(svec, "g0")
        dx = inv * (a - row_sum(a) * (1.0 / FEAT) - hat * (row_sum(a * hat) * (1.0 / FEAT)))
        dxs[rows, :] = 0.1 * dx
        return gain_sum, shift_sum, bias_sum + col_sum(low.astype(F32))

    gain_sum, shift_sum, bias_sum = lax.fori_loop(0, NT, first, (zero_feat, zero_feat, zero))
    put(sg, "g0", gain_sum)
    put(sg, "b0", shift_sum)
    put(sg, "bp", bias_sum)
    c_dx = pltpu.make_async_copy(dxs, dx_out, sem_dx)
    c_dx.start()
    i = new_slot()
    weight_grad(nrmt, dg, gslot.at[i], FEAT // TILE)
    c_gp = pltpu.make_async_copy(gslot.at[i, 0:FEAT, :], gwp_out, sem_g.at[i])
    c_gp.start()
    c_dx.wait()
    slot_wait(1 - i)
    c_gp.wait()


def any_spec():
    return pl.BlockSpec(memory_space=pl.ANY)


def vmem_spec():
    return pl.BlockSpec(memory_space=pltpu.VMEM)


def smem_spec():
    return pl.BlockSpec(memory_space=pltpu.SMEM)


def forward_call(seg, cfg, feat, cot, wg, wp, svec, upto=9):
    shape = jax.ShapeDtypeStruct
    outs = [
        (shape((LEN, D), BF16), any_spec()),
        (shape((LEN, D), BF16), any_spec()),
        (shape((D, LEN), BF16), any_spec()),
        (shape((3, LEN, D), BF16), any_spec()),
        (shape((D, LEN), BF16), any_spec()),
        (shape((LEN, D), BF16), any_spec()),
        (shape((D, LEN), BF16), any_spec()),
        (shape((LEN, D), BF16), any_spec()),
        (shape((LEN, 128), F32), vmem_spec()),
        (shape((D, LEN), BF16), any_spec()),
        (shape((4, LEN, D), BF16), any_spec()),
        (shape((4, LEN, D), BF16), any_spec()),
        (shape((LEN, D), F32), any_spec()),
        (shape((LEN, D), BF16), any_spec()),
        (shape((D, LEN), BF16), any_spec()),
        (shape((16, LEN), F32), vmem_spec()),
        (shape((1, VEC), F32), vmem_spec()),
    ]
    bf = lambda *s: pltpu.VMEM(s, BF16)
    scratch = [
        bf(LEN, FEAT), bf(LEN, D), bf(12, D, D), bf(FEAT, D), pltpu.VMEM((LEN, D), F32),
        bf(LEN, D), bf(D, LEN), bf(3, LEN, D), bf(D, LEN), bf(D, LEN), bf(LEN, D), bf(D, LEN),
        bf(LEN, D), bf(LEN, D), bf(D, LEN), bf(4, LEN, D), bf(4, LEN, D), bf(LEN, D), bf(D, LEN),
        bf(LEN, D), bf(2, LEN, 128), bf(2, LEN, 128),
        pltpu.SemaphoreType.DMA((15,)), pltpu.SemaphoreType.DMA((24,)),
    ]
    return pl.pallas_call(
        functools.partial(forward_kernel, upto),
        out_shape=[o[0] for o in outs],
        in_specs=[smem_spec(), smem_spec()] + [any_spec()] * 4 + [vmem_spec()],
        out_specs=[o[1] for o in outs],
        scratch_shapes=scratch,
        compiler_params=pltpu.CompilerParams(vmem_limit_bytes=VMEM_LIMIT),
        name="forward",
    )(seg, cfg, feat, cot, wg, wp, svec)


def backward_call(seg, cfg, feat, wg, wp, svec, saved, upto=9):
    shape = jax.ShapeDtypeStruct
    bf = lambda *s: pltpu.VMEM(s, BF16)
    scratch = [
        bf(LEN, FEAT), bf(2, D, D), bf(2, D, D), bf(D, D), bf(3, D, D), bf(FEAT, D), bf(D, LEN),
        bf(3, LEN, D), bf(D, LEN), bf(LEN, D), bf(D, LEN), bf(LEN, D), pltpu.VMEM((LEN, 128), F32),
        bf(D, LEN), bf(2, LEN, D), bf(2, LEN, D), bf(LEN, D), pltpu.VMEM((LEN, D), F32),
        bf(LEN, D), bf(D, LEN), bf(LEN, D), bf(LEN, D), pltpu.VMEM((16, LEN), F32),
        pltpu.VMEM((128, LEN), F32), bf(2, LEN, LEN), bf(2, LEN, LEN), pltpu.VMEM((2, D, D), F32),
        pltpu.VMEM((LEN, FEAT), F32), bf(2, LEN, 128), bf(2, LEN, 128), bf(FEAT, LEN),
        pltpu.SemaphoreType.DMA((17,)), pltpu.SemaphoreType.DMA((2, 4)),
        pltpu.SemaphoreType.DMA((2,)), pltpu.SemaphoreType.DMA,
    ]
    return pl.pallas_call(
        functools.partial(backward_kernel, upto),
        out_shape=[
            shape((LEN, FEAT), F32), shape((12, D, D), F32), shape((FEAT, D), F32), shape((1, VEC), F32),
        ],
        in_specs=[smem_spec(), smem_spec()] + [any_spec()] * 3 + [vmem_spec()]
        + [any_spec()] * 13 + [vmem_spec()] * 2,
        out_specs=[any_spec()] * 3 + [vmem_spec()],
        scratch_shapes=scratch,
        compiler_params=pltpu.CompilerParams(vmem_limit_bytes=VMEM_LIMIT),
        name="backward",
    )(seg, cfg, feat, wg, wp, svec, *saved)


def adam(weight, moment, square, grad, rate):
    moment_new = BETA_ONE * moment + (1.0 - BETA_ONE) * grad
    square_new = BETA_TWO * square + (1.0 - BETA_TWO) * grad * grad
    fix_one = 1.0 - BETA_ONE**STEP
    fix_two = 1.0 - BETA_TWO**STEP
    direction = moment_new / fix_one / (jnp.sqrt(square_new / fix_two) + ADAM_EPS)
    return (moment_new, square_new, weight - rate * (direction + DECAY * weight))


AXES = ("grp", "dp")


def layer(features, lengths, config, cotangent, wg, wp, svec, upto=9, back_upto=9):
    feat = features.reshape(LEN, FEAT)
    cot = cotangent.reshape(LEN, D)
    saved = forward_call(lengths, config, feat, cot, wg, wp, svec, upto)
    activations = saved[0]
    dx, gu, gwp, sg = backward_call(lengths, config, feat, wg, wp, svec, saved[2:], back_upto)
    return activations, dx, gu, gwp, sg


def per_device(
    features, segment_lengths, subnet_config, cotangent,
    projection_weight, projection_moment, projection_square,
    attention_weight, attention_moment, attention_square,
    output_weight, output_moment, output_square,
    feedforward_weight, feedforward_moment, feedforward_square,
    small_params, small_moment, small_square,
):
    gather = lambda w, axis: lax.all_gather(w.astype(BF16), AXES, axis=axis, tiled=True)
    wp = gather(projection_weight, 0)
    wa = gather(attention_weight, 1)
    wo = gather(output_weight, 0)
    wf = gather(feedforward_weight, 1)
    svec = gather(small_params, 0).astype(F32).reshape(1, VEC)
    quarters = wf.reshape(2, D, 4, D).transpose(0, 2, 1, 3).reshape(8, D, D)
    wg = jnp.concatenate([wa, wo[None], quarters], 0)
    activations, dx, gu, gwp, sg = layer(
        features, segment_lengths, subnet_config, cotangent, wg, wp, svec
    )
    ga = gu[0:3].reshape(3, D, 3, 256).transpose(2, 1, 0, 3).reshape(3, D, D)
    gf = gu[4:12].reshape(2, 4, D, D).transpose(0, 2, 1, 3).reshape(2, D, FF)
    scatter = lambda g, dim: lax.psum_scatter(g, AXES, scatter_dimension=dim, tiled=True)
    gp = scatter(gwp, 0)
    ga = scatter(ga, 1)
    go = scatter(gu[3], 0)
    gf = scatter(gf, 1)
    gs = scatter(sg.reshape(VEC), 0)
    out = [activations.reshape(1, LEN, D), dx.reshape(1, LEN, FEAT)]
    for w, m, v, g, rate in (
        (projection_weight, projection_moment, projection_square, gp, RATE),
        (attention_weight, attention_moment, attention_square, ga, RATE),
        (output_weight, output_moment, output_square, go, RATE),
        (feedforward_weight, feedforward_moment, feedforward_square, gf, RATE),
        (small_params, small_moment, small_square, gs, SMALL_RATE),
    ):
        out.append(g)
        out.extend(adam(w, m, v, g, rate))
    return tuple(out)


def solution(mesh):
    rows3, rows2, stacked, flat = (
        P(AXES, None, None), P(AXES, None), P(None, AXES, None), P(AXES),
    )
    return jax.shard_map(
        per_device,
        mesh=mesh,
        in_specs=(
            rows3, rows2, P("grp", None), rows3, rows2, rows2, rows2, stacked, stacked, stacked,
            rows2, rows2, rows2, stacked, stacked, stacked, flat, flat, flat,
        ),
        out_specs=(rows3, rows3) + (rows2,) * 4 + (stacked,) * 4 + (rows2,) * 4 + (stacked,) * 4 + (flat,) * 4,
        check_vma=False,
    )
```

```python
import functools
import math

import jax
import jax.numpy as jnp
from jax import lax
from jax.experimental import pallas as pl
from jax.experimental.pallas import tpu as pltpu
from jax.sharding import PartitionSpec as P

D = 768
FF = 3072
FEAT = 512
HDIM = 64
HEADS = 12
PAIRS = HEADS // 2
LEN = 1024
STEP = 10
TILE = 256
NT = LEN // TILE
VEC = 11008

NORM_EPS = 1e-05
RATE = 0.08
SMALL_RATE = 0.3
BETA_ONE = 0.9
BETA_TWO = 0.999
ADAM_EPS = 1e-08
DECAY = 0.01

F32 = jnp.float32
BF16 = jnp.bfloat16
BIG = 2.0**100
VMEM_LIMIT = 63 << 20

WIDTHS = dict(
    g0=FEAT, b0=FEAT, bp=D, bq=D, bv=D, bo=D, g1=D, c1=D, b1=FF, b2=D, g2=D, c2=D
)
OFFSETS = {}
_at = 0
for _name, _width in WIDTHS.items():
    OFFSETS[_name] = _at
    _at += _width

KEY_RANGE = [
    (max(0, (i * TILE - 511) // TILE * TILE), min(LEN, -(-(i * TILE + TILE + 511) // TILE) * TILE))
    for i in range(NT)
]


def mm(a, b):
    return jnp.dot(a, b, preferred_element_type=F32)


def mm_nt(a, b):
    return lax.dot_general(a, b, (((1,), (1,)), ((), ())), preferred_element_type=F32)


def piece(ref, name, start=0, width=None):
    begin = OFFSETS[name] + start
    return ref[0:1, begin : begin + (width or WIDTHS[name])]


def put(ref, name, value, start=0):
    begin = OFFSETS[name] // 128 + start // 128
    for i in range(value.shape[1] // 128):
        ref[pl.ds(begin + i, 1), :] = value[:, 128 * i : 128 * i + 128]


def keep_row(width, limit, start=0):
    lane = lax.broadcasted_iota(jnp.int32, (1, width), 1) + start
    return (lane < limit).astype(F32)


def col_sum(value):
    return jnp.sum(value, 0, keepdims=True)


def row_sum(value):
    return jnp.sum(value, 1, keepdims=True)


def rows_of(t):
    return pl.ds(pl.multiple_of(t * TILE, TILE), TILE)


def lanes_of(p, width=128):
    return pl.ds(pl.multiple_of(p * width, width), width)


def gelu_both(u):
    half = jnp.exp(-0.5 * u * u)
    t = 1.0 / (1.0 + (0.3275911 * 0.7071067811865476) * jnp.abs(u))
    poly = 0.5 * 1.061405429
    for c in (-1.453152027, 1.421413741, -0.284496736, 0.254829592):
        poly = poly * t + 0.5 * c
    tail = poly * t * half
    cdf = jnp.where(u >= 0.0, 1.0 - tail, tail)
    return u * cdf, cdf + u * (half * 0.3989422804014327)


def fill_patterns(seg_ref, kpat, qpat):
    e0 = seg_ref[0, 0]
    e1 = e0 + seg_ref[0, 1]
    e2 = e1 + seg_ref[0, 2]

    @pl.loop(0, NT)
    def _(t):
        pos = lax.broadcasted_iota(jnp.int32, (TILE, 128), 0) + t * TILE
        lane = lax.broadcasted_iota(jnp.int32, (TILE, 128), 1)
        seg = (
            (pos >= e0).astype(jnp.int32)
            + (pos >= e1).astype(jnp.int32)
            + (pos >= e2).astype(jnp.int32)
        )
        for e in range(2):
            slot = lane - (64 if e == 0 else 0)
            valid = (slot >= 0) & (slot < 4)
            same = slot == seg
            kpat[e, rows_of(t), :] = jnp.where(same, 1.0, 0.0).astype(BF16)
            qpat[e, rows_of(t), :] = jnp.where(valid & (slot != seg), -BIG, 0.0).astype(BF16)


def half_mask(e):
    lane = lax.broadcasted_iota(jnp.int32, (1, 128), 1)
    return ((lane < 64) if e == 0 else (lane >= 64)).astype(F32).astype(BF16)


def norm0(feat, svec, rows):
    x = feat[rows, :].astype(F32)
    centred = x - row_sum(x) * (1.0 / FEAT)
    inv = lax.rsqrt(row_sum(centred * centred) * (1.0 / FEAT) + NORM_EPS)
    hat = centred * inv
    normed = (hat * piece(svec, "g0") + piece(svec, "b0")).astype(BF16)
    return hat, inv, normed


DIMS = ("y", "x", "z1", "z0")
CUBE = (2, 2, 2, 2)


def here():
    g = lax.axis_index("grp")
    d = lax.axis_index("dp")
    return dict(
        y=g // 2, x=g % 2, z1=d // 4, z0=(d // 2) % 2, c=d % 2,
    )


def partner(pos, dim):
    near = {k: (1 - v if k == dim else v) for k, v in pos.items()}
    return (near["y"] * 2 + near["x"], near["z1"] * 4 + near["z0"] * 2 + near["c"])


def cube(pos, full, other=()):
    return tuple(
        slice(None) if dim in full else (1 - pos[dim] if dim in other else pos[dim])
        for dim in DIMS
    )


def greet(pos):
    barrier = pltpu.get_barrier_semaphore()
    for dim in DIMS + ("c",):
        pl.semaphore_signal(
            barrier, inc=1, device_id=partner(pos, dim), device_id_type=pl.DeviceIdType.MESH
        )
    pl.semaphore_wait(barrier, len(DIMS) + 1)


def remote(src, dst, send_sem, recv_sem, device):
    return pltpu.make_async_remote_copy(
        src_ref=src, dst_ref=dst, send_sem=send_sem, recv_sem=recv_sem,
        device_id=device, device_id_type=pl.DeviceIdType.MESH,
    )


def by_core(pos, action):
    for c in range(2):
        pl.when(pos["c"] == c)(functools.partial(action, c))


def half(c):
    return slice(384 * c, 384 * c + 384)


PARTS = [("p", 0), ("h", 0), ("h", 1), ("h", 2), ("h", 3), ("u", 4), ("u", 6), ("u", 8), ("u", 10)]
GATHER_ORDER = [(("z1", "z0", "x", "y"), ("z1", "z0", "y", "x"))] * 8 + [
    (("x", "y", "z1", "z0"), ("y", "x", "z1", "z0"))
]


class Gather:
    def __init__(self, pos, wg, wp, stage, stage_p, send, recv):
        self.pos, self.wg, self.wp = pos, wg, wp
        self.stage, self.stage_p = stage, stage_p
        self.send, self.recv = send, recv

    def view(self, i, c, index):
        kind, u = PARTS[i]
        if kind == "p":
            return self.wp.at[index + (slice(None), half(c))]
        if kind == "h":
            return self.wg.at[(u,) + index + (slice(None), half(c))]
        return self.wg.at[(u + c,) + index]

    def staged(self, i, c, rows):
        kind, u = PARTS[i]
        if kind == "p":
            return self.stage_p.at[rows, half(c)]
        if kind == "h":
            return self.stage.at[u, rows, half(c)]
        return self.stage.at[u + c, rows, :]

    def swap(self, i, c):
        own = pl.ds(16 * c, 16) if PARTS[i][0] == "p" else pl.ds(24 * c, 24)
        view = self.staged(i, 1 - c, own)
        return remote(view, view, self.send.at[i, 4], self.recv.at[i, 4], partner(self.pos, "c"))

    def hop(self, i, s, c):
        order = GATHER_ORDER[i][c]
        view = self.view(i, c, cube(self.pos, order[:s]))
        return remote(view, view, self.send.at[i, s], self.recv.at[i, s], partner(self.pos, order[s]))

    def give(self, i, far, c):
        order = GATHER_ORDER[i][c]
        view = self.view(i, c, cube(self.pos, order[:3], order[3:] if far else ()))
        return remote(
            view, view, self.send.at[i, 5 + far], self.recv.at[i, 5 + far], partner(self.pos, "c")
        )

    def begin(self, i):
        def action(c):
            other = pl.ds(16 * (1 - c), 16) if PARTS[i][0] == "p" else pl.ds(24 * (1 - c), 24)
            view = self.staged(i, c, other)
            remote(
                view, view, self.send.at[i, 4], self.recv.at[i, 4], partner(self.pos, "c")
            ).wait_recv()
            rows = slice(0, 32 if PARTS[i][0] == "p" else 48)
            block = self.view(i, c, cube(self.pos, ()))
            block[...] = self.staged(i, c, rows)[...].astype(BF16)
            self.hop(i, 0, c).start()

        by_core(self.pos, action)

    def step(self, i, s):
        def action(c):
            self.hop(i, s, c).wait_recv()
            if s < 3:
                self.hop(i, s + 1, c).start()
            if s >= 2:
                self.give(i, s - 2, c).start()

        by_core(self.pos, action)

    def need(self, i):
        def action(c):
            for far in range(2):
                self.give(i, far, 1 - c).wait_recv()

        by_core(self.pos, action)

    def finish(self):
        def action(c):
            for i in range(len(PARTS)):
                self.swap(i, c).wait_send()
                for s in range(4):
                    self.hop(i, s, c).wait_send()
                for far in range(2):
                    self.give(i, far, c).wait_send()

        by_core(self.pos, action)


class VectorSum:
    ORDER = ("c", "z0", "z1", "x", "y")

    def __init__(self, pos, held, got, send, recv):
        self.pos, self.held, self.got, self.send, self.recv = pos, held, got, send, recv

    def copy(self, s):
        return remote(
            self.held.at[s], self.got.at[s], self.send.at[s], self.recv.at[s],
            partner(self.pos, self.ORDER[s]),
        )

    def start(self, s):
        self.copy(s).start()

    def step(self, s):
        self.copy(s).wait_recv()
        self.held[s + 1] = self.held[s] + self.got[s]
        if s < 4:
            self.start(s + 1)

    def finish(self):
        for s in range(5):
            self.copy(s).wait_send()


def square(ref, u):
    return ref[u].reshape(D, D)


def forward_kernel(
    fast,
    *refs,
):
    refs = list(refs)
    take = lambda n: [refs.pop(0) for _ in range(n)]
    seg_ref, cfg_ref, feat_hbm, cot_hbm = take(4)
    if fast:
        own_p, own_a, own_o, own_f, own_s = take(5)
        wg_out, wp_out, svec = None, None, None
    else:
        wg_hbm, wp_hbm, svec = take(3)
    (
        act_out, hlt_out, qkv_out, kt_out, mixed_out, mixedt_out, xh1_out, inv1_out, flt_out,
        active_out, gp_out, d2_out, dg_out, dgt_out, lse_out, sg_out,
    ) = take(16)
    if fast:
        wg_out, wp_out, svec = take(3)
    (
        feat, cot, wg, wp, hid, hl, hlt, qkv, kt, vt, mixed, mixedt, xh1, fl, flt, active, gp, dg, dgt,
        kpat, qpat, sem_in, sem_out,
    ) = take(23)
    if fast:
        raw_p, raw_a, raw_o, raw_f, stage, stage_p, sem_raw, g_send, g_recv, sv_held, sv_got, v_send, v_recv = take(13)
    act = hl
    outs = []

    def load(i, src, dst):
        copy = pltpu.make_async_copy(src, dst, sem_in.at[i])
        copy.start()
        return copy

    def save(src, dst, part=None):
        i = len(outs)
        pick = lambda ref: ref if part is None else ref.at[part]
        make = lambda: pltpu.make_async_copy(pick(src), pick(dst), sem_out.at[i])
        make().start()
        outs.append(make)

    def need(i):
        kind, u = PARTS[i]
        if fast:
            gather.need(i)
            if kind == "p":
                save(wp, wp_out)
            elif kind == "h":
                save(wg, wg_out, u)
            else:
                save(wg, wg_out, pl.ds(u, 2))
        elif kind == "p":
            c_wp.wait()
        else:
            for v in range(u, u + (2 if kind == "u" else 1)):
                c_w[v].wait()

    def run(*steps):
        if fast:
            for i, s in steps:
                if i == "v":
                    vector.step(s)
                else:
                    gather.step(i, s)

    width = cfg_ref[0, 0]
    count = 1.0 / width.astype(F32)
    c_feat = load(0, feat_hbm, feat)
    if fast:
        pos = here()
        raws = [
            pltpu.make_async_copy(src, dst, sem_raw.at[i])
            for i, (src, dst) in enumerate(
                [(own_p, raw_p), (own_a, raw_a), (own_o, raw_o), (own_f, raw_f), (own_s, sv_held.at[0])]
            )
        ]
        for copy in raws:
            copy.start()
        gather = Gather(pos, wg, wp, stage, stage_p, g_send, g_recv)
        vector = VectorSum(pos, sv_held, sv_got, v_send, v_recv)
        for copy in raws:
            copy.wait()

        def arrange(c):
            rows = slice(24 * c, 24 * c + 24)
            stage_p[16 * c : 16 * c + 16, :] = raw_p[...]
            for j in range(3):
                for i in range(3):
                    stage[j, rows, 256 * i : 256 * i + 256] = raw_a[i, :, 256 * j : 256 * j + 256]
            stage[3, rows, :] = raw_o[...]
            for i in range(2):
                for q in range(4):
                    stage[4 + 4 * i + q, rows, :] = raw_f[i, :, D * q : D * q + D]

        by_core(pos, arrange)
        greet(pos)
        by_core(pos, lambda c: gather.swap(0, c).start())
        vector.start(0)
        for i in range(1, len(PARTS)):
            by_core(pos, lambda c, i=i: gather.swap(i, c).start())
        for i in (0, 1, 8, 2, 3, 4, 5, 6, 7):
            gather.begin(i)
    else:
        c_wp = load(1, wp_hbm, wp)
        c_w = [load(2 + u, wg_hbm.at[u], wg.at[u]) for u in range(12)]
    c_cot = load(14, cot_hbm, cot)
    run((0, 0), ("v", 0), (1, 0), (0, 1), ("v", 1), (2, 0), ("v", 2), (1, 1), (0, 2), ("v", 3), (3, 0), (8, 0))
    fill_patterns(seg_ref, kpat, qpat)
    run((2, 1), ("v", 4), (0, 3), (1, 2), (8, 1), (4, 0))
    if fast:
        for i in range(VEC // 128):
            svec[0:1, 128 * i : 128 * i + 128] = sv_held[5, i : i + 1, :]
    c_feat.wait()
    need(0)

    @pl.loop(0, NT)
    def _(t):
        rows = rows_of(t)
        normed = norm0(feat, svec, rows)[2]
        h = (mm(normed, wp[...].reshape(FEAT, D)) + piece(svec, "bp")) * keep_row(D, width)
        hid[rows, :] = h
        low = h.astype(BF16)
        hl[rows, :] = low
        hlt[:, rows] = low.T

    save(hlt, hlt_out)
    run((1, 3))
    need(1)

    slots = [
        [(2, 2), (3, 1), (5, 0)],
        [(2, 3)],
        [(3, 2), (4, 1), (6, 0)],
        [(3, 3), (8, 2)],
        [(4, 2), (5, 1), (7, 0)],
        [(4, 3)],
        [(5, 2), (6, 1)],
        [],
        [(5, 3), (6, 2)],
        [(7, 1)],
        [(8, 3)],
        [(6, 3)],
    ]

    def at_slot(p, e):
        if fast:
            for i in range(PAIRS):
                if slots[2 * i + e]:

                    @pl.when(p == i)
                    def _(i=i):
                        run(*slots[2 * i + e])

    @pl.loop(0, PAIRS)
    def _(p):
        at_slot(p, 0)
        for j in range(3):

            @pl.when(p == 2 * j)
            def _(j=j):
                if j:
                    need(1 + j)

        @pl.when(lax.rem(p, 2) == 0)
        def _():
            j = lax.div(p, 2)
            group = lanes_of(j, 256)

            @pl.loop(0, NT)
            def _(t):
                rows = rows_of(t)
                keep = keep_row(256, cfg_ref[0, 1] * HDIM - j * 256)
                o = mm(hl[rows, :], square(wg, j))
                bias = lambda name: svec[0:1, pl.ds(pl.multiple_of(OFFSETS[name] + j * 256, 128), 256)]
                qkv[0, rows, group] = ((o[:, 0:256] + bias("bq")) * keep).astype(BF16)
                k = (o[:, 256:512] * keep).astype(BF16)
                qkv[1, rows, group] = k
                v = ((o[:, 512:768] + bias("bv")) * keep).astype(BF16)
                qkv[2, rows, group] = v
                down = pl.ds(pl.multiple_of(j * 256, 256), 256)
                kt[down, rows] = k.T
                vt[down, rows] = v.T

        lanes = lanes_of(p)
        for e in range(2):
            if e:
                at_slot(p, 1)
            kaug = qkv[1, :, lanes] * half_mask(e) + kpat[e]
            head_rows = pl.ds(pl.multiple_of(p * 128 + 64 * e, 64), 64)
            for b in range(NT):
                lo, hi = KEY_RANGE[b]
                cols = slice(b * TILE, (b + 1) * TILE)
                qaug = qkv[0, cols, lanes] * (half_mask(e) * 0.125) + qpat[e, cols, :]
                st = mm_nt(kaug[lo:hi], qaug)
                peak = jnp.max(st, 0, keepdims=True)
                power = jnp.exp(st - peak)
                total = col_sum(power)
                ot = mm(vt[head_rows, lo:hi], power.astype(BF16))
                mixedt[head_rows, cols] = (ot * (1.0 / total)).astype(BF16)
                lse_out[pl.ds(2 * p + e, 1), cols] = peak + jnp.log(total)

    save(qkv, qkv_out)
    save(kt, kt_out)
    save(mixedt, mixedt_out)
    need(4)

    @pl.loop(0, NT)
    def _(t):
        rows = rows_of(t)
        keep = keep_row(D, width)
        mix = mixedt[:, rows].T
        mixed[rows, :] = mix
        z = hid[rows, :] + (mm(mix, square(wg, 3)) + piece(svec, "bo")) * keep
        centred = (z - row_sum(z * keep) * count) * keep
        inv = lax.rsqrt(row_sum(centred * centred) * count + NORM_EPS)
        hat = centred * inv
        first = (hat * piece(svec, "g1") + piece(svec, "c1")) * keep
        xh1[rows, :] = hat.astype(BF16)
        inv1_out[rows, :] = jnp.broadcast_to(inv, (TILE, 128))
        hid[rows, :] = first + piece(svec, "b2") * keep
        low = first.astype(BF16)
        fl[rows, :] = low
        flt[:, rows] = low.T

    save(mixed, mixed_out)
    save(xh1, xh1_out)
    save(flt, flt_out)
    need(5)

    def up(q):
        @pl.loop(0, NT)
        def _(t):
            rows = rows_of(t)
            u = (mm(fl[rows, :], square(wg, 4 + q)) + piece(svec, "b1", q * D, D)) * keep_row(
                D, cfg_ref[0, 2], q * D
            )
            g, slope = gelu_both(u)
            active[q, rows, :] = g.astype(BF16)
            gp[q, rows, :] = slope.astype(BF16)

        save(active, active_out, q)
        save(gp, gp_out, q)

    def down(q):
        @pl.loop(0, NT)
        def _(t):
            rows = rows_of(t)
            hid[rows, :] += mm_nt(active[q, rows, :], square(wg, 8 + q)) * keep_row(D, width)

    up(0)
    up(1)
    run((7, 2))
    need(6)
    up(2)
    run((7, 3))
    up(3)
    need(7)
    down(0)
    down(1)
    need(8)
    down(2)
    down(3)
    c_cot.wait()
    zero = jnp.zeros((1, D), F32)

    def last(t, sums):
        gain_sum, shift_sum, bias_sum = sums
        rows = rows_of(t)
        keep = keep_row(D, width)
        z = hid[rows, :]
        centred = (z - row_sum(z * keep) * count) * keep
        inv = lax.rsqrt(row_sum(centred * centred) * count + NORM_EPS)
        hat = centred * inv
        gain = piece(svec, "g2")
        act[rows, :] = ((hat * gain + piece(svec, "c2")) * keep).astype(BF16)
        g = cot[rows, :].astype(F32) * keep
        gain_sum = gain_sum + col_sum(g * hat)
        shift_sum = shift_sum + col_sum(g)
        a = g * gain
        d2 = inv * (a - keep * (row_sum(a) * count) - hat * (row_sum(a * hat) * count))
        hid[rows, :] = d2
        low = d2.astype(BF16)
        dg[rows, :] = low
        dgt[:, rows] = low.T
        return gain_sum, shift_sum, bias_sum + col_sum(low.astype(F32))

    gain_sum, shift_sum, bias_sum = lax.fori_loop(0, NT, last, (zero, zero, zero))
    sg_out[...] = jnp.zeros((88, 128), F32)
    put(sg_out, "g2", gain_sum)
    put(sg_out, "c2", shift_sum)
    put(sg_out, "b2", bias_sum)
    save(act, act_out)
    save(hid, d2_out)
    save(dg, dg_out)
    save(dgt, dgt_out)
    if fast:
        gather.finish()
        vector.finish()
    for make in outs:
        make().wait()


R_PARTS = [("u", 8), ("u", 4), ("u", 10), ("u", 6), ("h", 3), ("h", 0), ("h", 1), ("h", 2), ("p", 0)]
R_ORDER = (("x", "y", "z0", "z1"), ("y", "x", "z0", "z1"))


class Scatter:
    def __init__(self, pos, acc, got, given, first, fin, gout, goutp, send, recv, local, credit):
        self.pos, self.acc, self.got, self.given, self.first = pos, acc, got, given, first
        self.fin, self.gout, self.goutp = fin, gout, goutp
        self.send, self.recv, self.local, self.credit = send, recv, local, credit

    def trim(self, i):
        kind = R_PARTS[i][0]
        if kind == "u":
            return ()
        return (slice(0, 32 if kind == "p" else 48), slice(0, 384))

    def held(self, bufs, i, index):
        kind = R_PARTS[i][0]
        if kind == "p":
            return bufs[2].at[index]
        if kind == "h":
            return bufs[1].at[(i - 4,) + index]
        return bufs[0].at[(i,) + index]

    def slot(self, buf, i):
        full = (slice(None),) * 4
        return buf.at[(i % 2,) + full + self.trim(i)]

    def hand(self, i):
        return remote(
            self.slot(self.given, i), self.slot(self.first, i), self.send.at[i, 4], self.recv.at[i, 4],
            partner(self.pos, "c"),
        )

    def hop(self, i, s, c):
        order = R_ORDER[c]
        src = self.held(self.acc, i, cube(self.pos, order[s + 1 :], order[s : s + 1]))
        dst = self.held(self.got, i, cube(self.pos, order[s + 1 :], order[: s + 1]))
        return remote(src, dst, self.send.at[i, s], self.recv.at[i, s], partner(self.pos, order[s]))

    def offer(self, i):
        if i >= 2:
            pl.semaphore_wait(self.credit, 1)
        self.hand(i).start()

    def reuse(self, i):
        if i >= 2:
            self.hand(i - 2).wait_send()

    def begin(self, i):
        self.hand(i).wait_recv()
        mine = self.held(self.acc, i, (slice(None),) * 4)
        mine[...] = mine[...] + self.slot(self.first, i)[...]
        if i < len(R_PARTS) - 2:
            pl.semaphore_signal(
                self.credit, inc=1, device_id=partner(self.pos, "c"),
                device_id_type=pl.DeviceIdType.MESH,
            )
        by_core(self.pos, lambda c: self.hop(i, 0, c).start())

    def ends(self, i, c, own):
        kind, u = R_PARTS[i]
        rows = 16 if kind == "p" else 24
        fin = self.held(self.fin, i, ())
        if kind == "p":
            dst = self.goutp.at[:, half(c)]
        elif kind == "h":
            dst = self.gout.at[u, :, half(c)]
        else:
            dst = self.gout.at[u + c]
        if own:
            return pltpu.make_async_copy(fin.at[pl.ds(rows * c, rows)], dst, self.local.at[i])
        return remote(
            fin.at[pl.ds(rows * (1 - c), rows)], dst, self.send.at[i, 5], self.recv.at[i, 5],
            partner(self.pos, "c"),
        )

    def step(self, i, s):
        def action(c):
            order = R_ORDER[c]
            self.hop(i, s, c).wait_recv()
            mine = self.held(self.acc, i, cube(self.pos, order[s + 1 :]))
            came = list(cube(self.pos, order[s + 1 :], order[:s]))
            came = self.held(self.got, i, tuple(came))
            if s < 3:
                mine[...] = mine[...] + came[...]
                self.hop(i, s + 1, c).start()
            else:
                fin = self.held(self.fin, i, ())
                fin[...] = mine[...].astype(F32) + came[...].astype(F32)
                for own in (True, False):
                    self.ends(i, c, own).start()

        by_core(self.pos, action)

    def finish(self):
        n = len(R_PARTS)
        for i in range(n - 2, n):
            self.hand(i).wait_send()

        def action(c):
            for i in range(n):
                for s in range(4):
                    self.hop(i, s, c).wait_send()
                self.ends(i, c, True).wait()
                self.ends(i, c, False).wait_send()
                self.ends(i, 1 - c, False).wait_recv()

        by_core(self.pos, action)


def backward_kernel(fast, *refs):
    refs = list(refs)
    take = lambda n: [refs.pop(0) for _ in range(n)]
    seg_ref, cfg_ref, feat_hbm, wg_hbm, wp_hbm, svec = take(6)
    (
        hlt_hbm, qkv_hbm, kt_hbm, mixed_hbm, mixedt_hbm, xh1_hbm, inv1_hbm, flt_hbm,
        active_hbm, gp_hbm, d2_hbm, dg_hbm, dgt_hbm, lse, sg_in,
    ) = take(15)
    dx_out, gu_out, gwp_out, sg = take(4)
    (
        feat, wbuf, wp, pool, tr, kt, qkv, go, inv1, fg, dg, tg, delta, dqt, kpat, qpat,
        acc_u, acc_h, acc_p, given, sem_in, sem_q, sem_dx,
    ) = take(23)
    if fast:
        (
            got_u, got_h, got_p, first_in, fin_u, fin_h, fin_p, r_send, r_recv, r_local, credit,
            sv_held, sv_got, v_send, v_recv,
        ) = take(15)
        pos = here()
        core = pos["c"]
        small = sv_held.at[0]
        scatter = Scatter(
            pos, (acc_u, acc_h, acc_p), (got_u, got_h, got_p), given, first_in, (fin_u, fin_h, fin_p),
            gu_out, gwp_out, r_send, r_recv, r_local, credit,
        )
        vector = VectorSum(pos, sv_held, sv_got, v_send, v_recv)
    else:
        sem_out = take(1)[0]
        core = lax.axis_index("dp") % 2
        small = sg
        holder = Scatter(None, (acc_u, acc_h, acc_p), *[None] * 10)

    def load(i, src, dst):
        copy = pltpu.make_async_copy(src, dst, sem_in.at[i])
        copy.start()
        return copy

    def run(*steps):
        if fast:
            for i, s in steps:
                if s < 0:
                    scatter.begin(i)
                else:
                    scatter.step(i, s)

    def columns(h):
        return pl.ds(pl.multiple_of(384 * h, 128), 384)

    def plain_copy(i, mine):
        kind, u = R_PARTS[i]
        which = core if mine else 1 - core
        full = (slice(None),) * 4
        if mine:
            src = holder.held(holder.acc, i, full)
        else:
            src = given.at[(i % 2,) + full + holder.trim(i)]
        if kind == "p":
            dst = gwp_out.at[full + (slice(None), columns(which))]
        elif kind == "h":
            dst = gu_out.at[(u,) + full + (slice(None), columns(which))]
        else:
            dst = gu_out.at[u + which]
        return pltpu.make_async_copy(src, dst, sem_out.at[i, 1 if mine else 0])

    def make(i, mine, left, right):
        kind = R_PARTS[i][0]
        rows, width = (32, 384) if kind == "p" else (48, 384 if kind == "h" else D)
        if not mine:
            if fast:
                scatter.reuse(i)
            elif i >= 2:
                plain_copy(i - 2, False).wait()

        @pl.loop(0, 2)
        def _(y):
            span = pl.ds(pl.multiple_of(y * 8 * rows, 8 * rows), 8 * rows)
            value = mm(left[span, :], right[...]).astype(BF16).reshape(2, 2, 2, rows, width)
            if not mine:
                trim = (slice(0, rows), slice(0, width))
                given[(i % 2, y) + (slice(None),) * 3 + trim] = value
            elif kind == "p":
                acc_p[y] = value
            elif kind == "h":
                acc_h[i - 4, y] = value
            else:
                acc_u[i, y] = value

        if fast:
            if not mine:
                scatter.offer(i)
        else:
            plain_copy(i, mine).start()

    def quarter(k):
        s = k % 2
        q = 2 * (k // 2) + (core if k % 2 else 1 - core)
        pairs = [
            (active_hbm.at[q], pool.at[s]),
            (wg_hbm.at[8 + q], wbuf.at[s]),
            (gp_hbm.at[q], pool.at[2 + s]),
            (wg_hbm.at[4 + q], wbuf.at[2 + s]),
        ]
        return q, [
            pltpu.make_async_copy(src, dst, sem_q.at[s, i]) for i, (src, dst) in enumerate(pairs)
        ]

    dgt, flt, ig = tr.at[0], tr.at[1], pool.at[4]
    c_dgt = load(0, dgt_hbm, dgt)
    for copy in quarter(0)[1]:
        copy.start()
    c_dg = load(1, dg_hbm, dg)
    c_flt = load(2, flt_hbm, flt)
    c_d2 = load(3, d2_hbm, fg)
    for copy in quarter(1)[1]:
        copy.start()
    c_xh1 = load(4, xh1_hbm, go)
    c_inv1 = load(5, inv1_hbm, inv1)
    c_mixed = load(6, mixed_hbm, pool.at[5])
    c_qkv = load(9, qkv_hbm, qkv)
    c_kt = load(10, kt_hbm, kt)
    c_wp = load(15, wp_hbm, wp)
    c_feat = load(16, feat_hbm, feat)

    width = cfg_ref[0, 0]
    count = 1.0 / width.astype(F32)
    if fast:
        greet(pos)
    small[...] = sg_in[...]
    fill_patterns(seg_ref, kpat, qpat)
    c_dgt.wait()
    events = {
        (1, 0): [(0, -1)],
        (1, 2): [(1, -1)],
        (2, 3): [(0, 0)],
        (3, 0): [(2, -1), (1, 0)],
        (3, 2): [(3, -1), (0, 1)],
        (3, 3): [(1, 1), (0, 2)],
    }
    for k in range(4):
        s = k % 2
        mine = bool(k % 2)
        q, copies = quarter(k)
        at = lambda n: run(*events.get((k, n), []))
        copies[0].wait()
        make(2 * (k // 2), mine, dgt, pool.at[s])
        at(0)
        if k == 0:
            c_dg.wait()
        copies[1].wait()
        copies[2].wait()

        def inner(t, bias, q=q, s=s):
            rows = rows_of(t)
            low = (
                mm(dg[rows, :], square(wbuf, s))
                * pool[2 + s, rows, :].astype(F32)
                * keep_row(D, cfg_ref[0, 2] - q * D)
            ).astype(BF16)
            ig[rows, :] = low
            return bias + col_sum(low.astype(F32))

        put(small, "b1", lax.fori_loop(0, NT, inner, jnp.zeros((1, D), F32)), q * D)
        at(1)
        if k == 0:
            c_flt.wait()
            c_d2.wait()
        make(2 * (k // 2) + 1, mine, flt, ig)
        at(2)
        copies[3].wait()

        @pl.loop(0, NT)
        def _(t, s=s):
            rows = rows_of(t)
            fg[rows, :] += mm_nt(ig[rows, :], square(wbuf, 2 + s))

        at(3)
        if k < 2:
            for copy in quarter(k + 2)[1]:
                copy.start()
        if k == 2:
            c_wo = load(8, wg_hbm.at[3], wbuf.at[0])
            c_wa = [load(12, wg_hbm.at[0], wbuf.at[2])]

    mixedt, hlt, mixed = tr.at[0], tr.at[1], pool.at[5]
    c_mixedt = load(7, mixedt_hbm, mixedt)
    c_hlt = load(11, hlt_hbm, hlt)
    c_wa.append(load(13, wg_hbm.at[1], wbuf.at[1]))
    c_wa.append(load(14, wg_hbm.at[2], wbuf.at[3]))
    wa_slot = (2, 1, 3)
    for copy in (c_xh1, c_inv1, c_mixed, c_wo):
        copy.wait()
    zero = jnp.zeros((1, D), F32)

    def middle(t, sums):
        gain_sum, shift_sum, bias_sum = sums
        rows = rows_of(t)
        keep = keep_row(D, width)
        hat = go[rows, :].astype(F32)
        g = fg[rows, :] * keep
        gain_sum = gain_sum + col_sum(g * hat)
        shift_sum = shift_sum + col_sum(g)
        a = g * piece(svec, "g1")
        d1 = inv1[rows, 0:1] * (a - keep * (row_sum(a) * count) - hat * (row_sum(a * hat) * count))
        fg[rows, :] = d1
        low = d1.astype(BF16)
        dg[rows, :] = low
        mg = mm_nt(low, square(wbuf, 0)).astype(BF16)
        go[rows, :] = mg
        product = mg.astype(F32) * mixed[rows, :].astype(F32)
        high = product.astype(BF16)
        rest = (product - high.astype(F32)).astype(BF16)
        lane = lax.broadcasted_iota(jnp.int32, (16, D), 1)
        head = lax.broadcasted_iota(jnp.int32, (16, D), 0)
        pick = ((lane >= head * HDIM) & (lane < head * HDIM + HDIM)).astype(F32).astype(BF16)
        delta[:, rows] = mm_nt(pick, high) + mm_nt(pick, rest)
        return gain_sum, shift_sum, bias_sum + col_sum(low.astype(F32))

    gain_sum, shift_sum, bias_sum = lax.fori_loop(0, NT, middle, (zero, zero, zero))
    put(small, "g1", gain_sum)
    put(small, "c1", shift_sum)
    put(small, "bo", bias_sum)
    run((2, 0), (0, 3), (1, 2))
    c_mixedt.wait()
    make(4, False, mixedt, dg.at[:, columns(1 - core)])
    make(4, True, mixedt, dg.at[:, columns(core)])

    c_qkv.wait()
    c_kt.wait()
    c_hlt.wait()
    for copy in c_wa:
        copy.wait()
    slots = [
        [[(2, 1), (1, 3), (3, 0)], [(4, -1), (2, 2), (3, 1)], [(2, 3), (4, 0), (3, 2)], [(4, 1), (3, 3)]],
        [[(5, -1), (4, 2)], [(5, 0), (4, 3)], [(5, 1)], [(5, 2)]],
        [[(6, -1), (5, 3)], [(6, 0)], [(6, 1)], [(6, 2)]],
    ]

    def chunk(n):
        return n // 3, slice(256 * (n % 3), 256 * (n % 3) + 256)

    for j in range(3):

        def at_slot(pp, e, j=j):
            if fast:
                for i in range(2):
                    steps = slots[j][2 * i + e]

                    @pl.when(pp == i)
                    def _(steps=steps):
                        run(*steps)

        @pl.loop(0, 2)
        def _(pp, j=j):
            p = j * 2 + pp
            lanes = lanes_of(p)
            for e in range(2):
                at_slot(pp, e)
                kaug = qkv[1, :, lanes] * half_mask(e) + kpat[e]
                head_rows = pl.ds(pl.multiple_of(p * 128 + 64 * e, 64), 64)
                for b in range(NT):
                    lo, hi = KEY_RANGE[b]
                    cols = slice(b * TILE, (b + 1) * TILE)
                    qaug = qkv[0, cols, lanes] * (half_mask(e) * 0.125) + qpat[e, cols, :]
                    st = mm_nt(kaug[lo:hi], qaug)
                    weights = jnp.exp(st - lse[pl.ds(2 * p + e, 1), cols])
                    n, span = chunk(4 * e + b)
                    pool[n, lo:hi, span] = weights.astype(BF16)
                    goe = go[cols, lanes] * half_mask(e)
                    dp = mm_nt(qkv[2, lo:hi, lanes], goe)
                    ds = (weights * (dp - delta[pl.ds(2 * p + e, 1), cols])).astype(BF16)
                    n, span = chunk(8 + 4 * e + b)
                    pool[n, lo:hi, span] = ds
                    dqt[64 * e : 64 * e + 64, cols] = mm(kt[head_rows, lo:hi], ds)
            keep = keep_row(128, cfg_ref[0, 1] * HDIM - p * 128)
            for t in range(NT):
                rows = slice(t * TILE, (t + 1) * TILE)
                dk = jnp.zeros((TILE, 128), F32)
                dv = jnp.zeros((TILE, 128), F32)
                for b in range(NT):
                    if not KEY_RANGE[b][0] <= t * TILE < KEY_RANGE[b][1]:
                        continue
                    cols = slice(b * TILE, (b + 1) * TILE)
                    for e in range(2):
                        n, span = chunk(8 + 4 * e + b)
                        dk = dk + mm(pool[n, rows, span], qkv[0, cols, lanes] * half_mask(e))
                        n, span = chunk(4 * e + b)
                        dv = dv + mm(pool[n, rows, span], go[cols, lanes] * half_mask(e))
                dq = dqt[:, rows].T
                for i, value in enumerate((dq * (keep * 0.125), dk * (keep * 0.125), dv * keep)):
                    tg[rows, pl.ds(pl.multiple_of(256 * i + pp * 128, 128), 128)] = value.astype(BF16)

        make(5 + j, False, hlt, tg.at[:, columns(1 - core)])
        make(5 + j, True, hlt, tg.at[:, columns(core)])

        def back(t, bias, j=j):
            rows = rows_of(t)
            fg[rows, :] += mm_nt(tg[rows, :], square(wbuf, wa_slot[j]))
            return bias + col_sum(tg[rows, :].astype(F32))

        bias = lax.fori_loop(0, NT, back, zero)
        put(small, "bq", bias[:, 0:256], 256 * j)
        put(small, "bv", bias[:, 512:768], 256 * j)

    run((7, -1), (6, 3))
    c_wp.wait()
    c_feat.wait()
    zero_feat = jnp.zeros((1, FEAT), F32)
    nrmt = tr.at[0]

    def first(t, sums):
        gain_sum, shift_sum, bias_sum = sums
        rows = rows_of(t)
        hat, inv, normed = norm0(feat, svec, rows)
        nrmt[0:FEAT, rows] = normed.T
        low = (fg[rows, :] * keep_row(D, width)).astype(BF16)
        dg[rows, :] = low
        g = mm_nt(low, wp[...].reshape(FEAT, D))
        gain_sum = gain_sum + col_sum(g * hat)
        shift_sum = shift_sum + col_sum(g)
        a = g * piece(svec, "g0")
        dx = inv * (a - row_sum(a) * (1.0 / FEAT) - hat * (row_sum(a * hat) * (1.0 / FEAT)))
        fg[rows, 0:FEAT] = 0.1 * dx
        return gain_sum, shift_sum, bias_sum + col_sum(low.astype(F32))

    gain_sum, shift_sum, bias_sum = lax.fori_loop(0, NT, first, (zero_feat, zero_feat, zero))
    put(small, "g0", gain_sum)
    put(small, "b0", shift_sum)
    put(small, "bp", bias_sum)
    c_dx = pltpu.make_async_copy(fg.at[:, 0:FEAT], dx_out, sem_dx)
    c_dx.start()
    if fast:
        vector.start(0)
    make(8, False, nrmt, dg.at[:, columns(1 - core)])
    make(8, True, nrmt, dg.at[:, columns(core)])
    if fast:
        run((7, 0))
        vector.step(0)
        run((8, -1), (7, 1))
        vector.step(1)
        run((8, 0), (7, 2))
        vector.step(2)
        run((8, 1), (7, 3))
        vector.step(3)
        run((8, 2))
        vector.step(4)
        run((8, 3))
        sg[...] = sv_held[5]
        vector.finish()
        scatter.finish()
    else:
        for i in range(len(R_PARTS)):
            plain_copy(i, True).wait()
        for i in range(len(R_PARTS) - 2, len(R_PARTS)):
            plain_copy(i, False).wait()
    c_dx.wait()


def adam_rule(weight, moment, square_in, grad, rate):
    moment_new = BETA_ONE * moment + (1.0 - BETA_ONE) * grad
    square_new = BETA_TWO * square_in + (1.0 - BETA_TWO) * grad * grad
    fix_one = 1.0 - BETA_ONE**STEP
    fix_two = 1.0 - BETA_TWO**STEP
    direction = moment_new / fix_one / (jnp.sqrt(square_new / fix_two) + ADAM_EPS)
    return (moment_new, square_new, weight - rate * (direction + DECAY * weight))


def adam_kernel(*refs):
    gu, gp, gs = refs[0:3]
    ins, outs = refs[3:18], refs[18:]

    def update(k, index, grad, rate):
        w, m, v = (ref[index] for ref in ins[3 * k : 3 * k + 3])
        for ref, value in zip(outs[4 * k : 4 * k + 4], (grad,) + adam_rule(w, m, v, grad, rate)):
            ref[index] = value

    everything = (slice(None), slice(None))
    update(0, everything, gp[...], RATE)
    for i in range(3):
        for j in range(3):
            span = slice(256 * j, 256 * j + 256)
            update(1, (i, slice(None), span), gu[j, :, 256 * i : 256 * i + 256], RATE)
    update(2, everything, gu[3], RATE)
    for i in range(2):
        for q in range(4):
            update(3, (i, slice(None), slice(D * q, D * q + D)), gu[4 + 4 * i + q], RATE)
    update(4, everything, gs[...], SMALL_RATE)


def adam_call(gu, gp, gs, state):
    shape = jax.ShapeDtypeStruct
    outs = [shape(state[3 * k].shape, F32) for k in range(5) for _ in range(4)]
    return pl.pallas_call(
        adam_kernel,
        out_shape=outs,
        in_specs=[vmem_spec()] * 18,
        out_specs=[vmem_spec()] * 20,
        compiler_params=pltpu.CompilerParams(vmem_limit_bytes=32 << 20),
        name="adam",
    )(gu, gp, gs, *state)


def any_spec():
    return pl.BlockSpec(memory_space=pl.ANY)


def vmem_spec():
    return pl.BlockSpec(memory_space=pltpu.VMEM)


def smem_spec():
    return pl.BlockSpec(memory_space=pltpu.SMEM)


def forward_call(fast, seg, cfg, feat, cot, weights):
    shape = jax.ShapeDtypeStruct
    outs = [
        (shape((LEN, D), BF16), any_spec()),
        (shape((D, LEN), BF16), any_spec()),
        (shape((3, LEN, D), BF16), any_spec()),
        (shape((D, LEN), BF16), any_spec()),
        (shape((LEN, D), BF16), any_spec()),
        (shape((D, LEN), BF16), any_spec()),
        (shape((LEN, D), BF16), any_spec()),
        (shape((LEN, 128), F32), vmem_spec()),
        (shape((D, LEN), BF16), any_spec()),
        (shape((4, LEN, D), BF16), any_spec()),
        (shape((4, LEN, D), BF16), any_spec()),
        (shape((LEN, D), F32), any_spec()),
        (shape((LEN, D), BF16), any_spec()),
        (shape((D, LEN), BF16), any_spec()),
        (shape((16, LEN), F32), vmem_spec()),
        (shape((88, 128), F32), vmem_spec()),
    ]
    if fast:
        outs += [
            (shape((12,) + CUBE + (48, D), BF16), any_spec()),
            (shape(CUBE + (32, D), BF16), any_spec()),
            (shape((1, VEC), F32), vmem_spec()),
        ]
    bf = lambda *s: pltpu.VMEM(s, BF16)
    f32 = lambda *s: pltpu.VMEM(s, F32)
    dma = lambda *s: pltpu.SemaphoreType.DMA(s)
    scratch = [
        bf(LEN, FEAT), bf(LEN, D), bf(12, *CUBE, 48, D), bf(*CUBE, 32, D), f32(LEN, D),
        bf(LEN, D), bf(D, LEN), bf(3, LEN, D), bf(D, LEN), bf(D, LEN), bf(LEN, D), bf(D, LEN),
        bf(LEN, D), bf(LEN, D), bf(D, LEN), bf(4, LEN, D), bf(4, LEN, D), bf(LEN, D), bf(D, LEN),
        bf(2, LEN, 128), bf(2, LEN, 128), dma(15), dma(32),
    ]
    if fast:
        scratch += [
            f32(16, D), f32(3, 24, D), f32(24, D), f32(2, 24, FF), f32(12, 48, D), f32(32, D), dma(5),
            dma(len(PARTS), 7), dma(len(PARTS), 7), f32(6, 88, 128), f32(5, 88, 128), dma(5), dma(5),
        ]
        specs = [any_spec()] * len(weights)
        params = dict(collective_id=0, has_side_effects=True)
    else:
        specs = [any_spec()] * 2 + [vmem_spec()]
        params = {}
    return pl.pallas_call(
        functools.partial(forward_kernel, fast),
        out_shape=[o[0] for o in outs],
        in_specs=[smem_spec(), smem_spec()] + [any_spec()] * 2 + specs,
        out_specs=[o[1] for o in outs],
        scratch_shapes=scratch,
        compiler_params=pltpu.CompilerParams(vmem_limit_bytes=VMEM_LIMIT, **params),
        name="forward",
    )(seg, cfg, feat, cot, *weights)


def backward_call(fast, seg, cfg, feat, wg, wp, svec, saved):
    shape = jax.ShapeDtypeStruct
    bf = lambda *s: pltpu.VMEM(s, BF16)
    f32 = lambda *s: pltpu.VMEM(s, F32)
    dma = lambda *s: pltpu.SemaphoreType.DMA(s)
    n = len(R_PARTS)
    scratch = [
        bf(LEN, FEAT), bf(4, *CUBE, 48, D), bf(*CUBE, 32, D), bf(6, LEN, D), bf(2, D, LEN), bf(D, LEN),
        bf(3, LEN, D), bf(LEN, D), f32(LEN, 128), f32(LEN, D), bf(LEN, D), bf(LEN, D), f32(16, LEN),
        f32(128, LEN), bf(2, LEN, 128), bf(2, LEN, 128),
        bf(4, *CUBE, 48, D), bf(4, *CUBE, 48, 384), bf(*CUBE, 32, 384), bf(2, *CUBE, 48, D),
        dma(17), dma(2, 4), pltpu.SemaphoreType.DMA,
    ]
    if fast:
        scratch += [
            bf(4, *CUBE, 48, D), bf(4, *CUBE, 48, 384), bf(*CUBE, 32, 384), bf(2, *CUBE, 48, D),
            f32(4, 48, D), f32(4, 48, 384), f32(32, 384), dma(n, 6), dma(n, 6), dma(n),
            pltpu.SemaphoreType.REGULAR, f32(6, 88, 128), f32(5, 88, 128), dma(5), dma(5),
        ]
        grads = [shape((12, 24, D), F32), shape((16, D), F32)]
        params = dict(collective_id=1, has_side_effects=True)
    else:
        scratch += [dma(n, 2)]
        grads = [shape((12,) + CUBE + (48, D), BF16), shape(CUBE + (32, D), BF16)]
        params = {}
    return pl.pallas_call(
        functools.partial(backward_kernel, fast),
        out_shape=[shape((LEN, FEAT), F32)] + grads + [shape((88, 128), F32)],
        in_specs=[smem_spec(), smem_spec()] + [any_spec()] * 3 + [vmem_spec()]
        + [any_spec()] * 13 + [vmem_spec()] * 2,
        out_specs=[any_spec()] * 3 + [vmem_spec()],
        scratch_shapes=scratch,
        compiler_params=pltpu.CompilerParams(vmem_limit_bytes=VMEM_LIMIT, **params),
        name="backward",
    )(seg, cfg, feat, wg, wp, svec, *saved)


AXES = ("grp", "dp")


def gathered(projection_weight, attention_weight, output_weight, feedforward_weight, small_params):
    gather = lambda w, axis: lax.all_gather(w.astype(BF16), AXES, axis=axis, tiled=True)
    wp = gather(projection_weight, 0)
    wa = gather(attention_weight, 1)
    wo = gather(output_weight, 0)
    wf = gather(feedforward_weight, 1)
    svec = gather(small_params, 0).astype(F32).reshape(1, VEC)
    return units(wp, wa, wo, wf) + (svec,)


def units(wp, wa, wo, wf):
    groups = wa.reshape(3, D, 3, 256).transpose(2, 1, 0, 3).reshape(3, D, D)
    quarters = wf.reshape(2, D, 4, D).transpose(0, 2, 1, 3).reshape(8, D, D)
    wg = jnp.concatenate([groups, wo[None], quarters], 0)
    return wg.reshape((12,) + CUBE + (48, D)), wp.reshape(CUBE + (32, D))


def layer(fast, features, lengths, config, cotangent, weights):
    feat = features.reshape(LEN, FEAT)
    cot = cotangent.reshape(LEN, D)
    saved = forward_call(fast, lengths, config, feat, cot, weights)
    activations = saved[0]
    wg, wp, svec = saved[16:] if fast else weights
    dx, gu, gwp, sg = backward_call(fast, lengths, config, feat, wg, wp, svec, saved[1:16])
    return activations, dx, gu, gwp, sg


def per_device(
    fast,
    features, segment_lengths, subnet_config, cotangent,
    projection_weight, projection_moment, projection_square,
    attention_weight, attention_moment, attention_square,
    output_weight, output_moment, output_square,
    feedforward_weight, feedforward_moment, feedforward_square,
    small_params, small_moment, small_square,
):
    weights = (projection_weight, attention_weight, output_weight, feedforward_weight)
    if fast:
        me = lax.axis_index(AXES)
        low = small_params.astype(BF16).astype(F32)
        placed = lax.dynamic_update_slice(jnp.zeros((88 * 128,), F32), low, (me * low.shape[0],))
        weights = weights + (placed.reshape(88, 128),)
    else:
        weights = gathered(*weights, small_params)
    activations, dx, gu, gwp, sg = layer(
        fast, features, segment_lengths, subnet_config, cotangent, weights
    )
    state = (
        projection_weight, projection_moment, projection_square,
        attention_weight, attention_moment, attention_square,
        output_weight, output_moment, output_square,
        feedforward_weight, feedforward_moment, feedforward_square,
        small_params[None], small_moment[None], small_square[None],
    )
    out = [activations.reshape(1, LEN, D), dx.reshape(1, LEN, FEAT)]
    vec = sg.reshape(88 * 128)
    if fast:
        gs = lax.dynamic_slice(vec, (me * small_params.shape[0],), small_params.shape)
        done = adam_call(gu, gwp, gs[None], state)
        return tuple(out) + tuple(done[:16]) + tuple(x[0] for x in done[16:])
    gu = gu.reshape(12, D, D).astype(F32)
    scatter = lambda g, dim: lax.psum_scatter(g, AXES, scatter_dimension=dim, tiled=True)
    ga = gu[0:3].reshape(3, D, 3, 256).transpose(2, 1, 0, 3).reshape(3, D, D)
    gf = gu[4:12].reshape(2, 4, D, D).transpose(0, 2, 1, 3).reshape(2, D, FF)
    sums = (
        scatter(gwp.reshape(FEAT, D).astype(F32), 0), scatter(ga, 1), scatter(gu[3], 0), scatter(gf, 1),
        scatter(vec[:VEC], 0)[None],
    )
    for k, g in enumerate(sums):
        new = (g,) + adam_rule(*state[3 * k : 3 * k + 3], g, RATE if k < 4 else SMALL_RATE)
        out.extend(x[0] if k == 4 else x for x in new)
    return tuple(out)


def solution(mesh):
    rows3, rows2, stacked, flat = (
        P(AXES, None, None), P(AXES, None), P(None, AXES, None), P(AXES),
    )
    return jax.shard_map(
        functools.partial(per_device, dict(mesh.shape) == dict(grp=4, dp=8)),
        mesh=mesh,
        in_specs=(
            rows3, rows2, P("grp", None), rows3, rows2, rows2, rows2, stacked, stacked, stacked,
            rows2, rows2, rows2, stacked, stacked, stacked, flat, flat, flat,
        ),
        out_specs=(rows3, rows3) + (rows2,) * 4 + (stacked,) * 4 + (rows2,) * 4 + (stacked,) * 4 + (flat,) * 4,
        check_vma=False,
    )
```

```python
import functools
import math

import jax
import jax.numpy as jnp
from jax import lax
from jax.experimental import pallas as pl
from jax.experimental.pallas import tpu as pltpu
from jax.sharding import PartitionSpec as P

D = 768
FF = 3072
FEAT = 512
HDIM = 64
HEADS = 12
PAIRS = HEADS // 2
LEN = 1024
STEP = 10
TILE = 256
NT = LEN // TILE
VEC = 11008

NORM_EPS = 1e-05
RATE = 0.08
SMALL_RATE = 0.3
BETA_ONE = 0.9
BETA_TWO = 0.999
ADAM_EPS = 1e-08
DECAY = 0.01

F32 = jnp.float32
BF16 = jnp.bfloat16
BIG = 2.0**100
VMEM_LIMIT = 63 << 20

WIDTHS = dict(
    g0=FEAT, b0=FEAT, bp=D, bq=D, bv=D, bo=D, g1=D, c1=D, b1=FF, b2=D, g2=D, c2=D
)
OFFSETS = {}
_at = 0
for _name, _width in WIDTHS.items():
    OFFSETS[_name] = _at
    _at += _width

KEY_RANGE = [
    (max(0, (i * TILE - 511) // TILE * TILE), min(LEN, -(-(i * TILE + TILE + 511) // TILE) * TILE))
    for i in range(NT)
]


def mm(a, b):
    return jnp.dot(a, b, preferred_element_type=F32)


def mm_nt(a, b):
    return lax.dot_general(a, b, (((1,), (1,)), ((), ())), preferred_element_type=F32)


def piece(ref, name, start=0, width=None):
    begin = OFFSETS[name] + start
    return ref[0:1, begin : begin + (width or WIDTHS[name])]


def put(ref, name, value, start=0):
    begin = OFFSETS[name] // 128 + start // 128
    for i in range(value.shape[1] // 128):
        ref[pl.ds(begin + i, 1), :] = value[:, 128 * i : 128 * i + 128]


def keep_row(width, limit, start=0):
    lane = lax.broadcasted_iota(jnp.int32, (1, width), 1) + start
    return (lane < limit).astype(F32)


def col_sum(value):
    return jnp.sum(value, 0, keepdims=True)


def row_sum(value):
    return jnp.sum(value, 1, keepdims=True)


def rows_of(t):
    return pl.ds(pl.multiple_of(t * TILE, TILE), TILE)


def lanes_of(p, width=128):
    return pl.ds(pl.multiple_of(p * width, width), width)


def gelu_both(u):
    half = jnp.exp(-0.5 * u * u)
    t = 1.0 / (1.0 + (0.3275911 * 0.7071067811865476) * jnp.abs(u))
    poly = 0.5 * 1.061405429
    for c in (-1.453152027, 1.421413741, -0.284496736, 0.254829592):
        poly = poly * t + 0.5 * c
    tail = poly * t * half
    cdf = jnp.where(u >= 0.0, 1.0 - tail, tail)
    return u * cdf, cdf + u * (half * 0.3989422804014327)


def fill_patterns(seg_ref, kpat, qpat):
    e0 = seg_ref[0, 0]
    e1 = e0 + seg_ref[0, 1]
    e2 = e1 + seg_ref[0, 2]

    @pl.loop(0, NT)
    def _(t):
        pos = lax.broadcasted_iota(jnp.int32, (TILE, 128), 0) + t * TILE
        lane = lax.broadcasted_iota(jnp.int32, (TILE, 128), 1)
        seg = (
            (pos >= e0).astype(jnp.int32)
            + (pos >= e1).astype(jnp.int32)
            + (pos >= e2).astype(jnp.int32)
        )
        for e in range(2):
            slot = lane - (64 if e == 0 else 0)
            valid = (slot >= 0) & (slot < 4)
            same = slot == seg
            kpat[e, rows_of(t), :] = jnp.where(same, 1.0, 0.0).astype(BF16)
            qpat[e, rows_of(t), :] = jnp.where(valid & (slot != seg), -BIG, 0.0).astype(BF16)


def half_mask(e):
    lane = lax.broadcasted_iota(jnp.int32, (1, 128), 1)
    return ((lane < 64) if e == 0 else (lane >= 64)).astype(F32).astype(BF16)


def norm0(feat, svec, rows):
    x = feat[rows, :].astype(F32)
    centred = x - row_sum(x) * (1.0 / FEAT)
    inv = lax.rsqrt(row_sum(centred * centred) * (1.0 / FEAT) + NORM_EPS)
    hat = centred * inv
    normed = (hat * piece(svec, "g0") + piece(svec, "b0")).astype(BF16)
    return hat, inv, normed


DIMS = ("y", "x", "z1", "z0")
CUBE = (2, 2, 2, 2)


def here():
    g = lax.axis_index("grp")
    d = lax.axis_index("dp")
    return dict(
        y=g // 2, x=g % 2, z1=d // 4, z0=(d // 2) % 2, c=d % 2,
    )


def partner(pos, dims):
    near = {k: (1 - v if k in dims else v) for k, v in pos.items()}
    return (near["y"] * 2 + near["x"], near["z1"] * 4 + near["z0"] * 2 + near["c"])


def cube(pos, full, other=()):
    return tuple(
        slice(None) if dim in full else (1 - pos[dim] if dim in other else pos[dim])
        for dim in DIMS
    )


def subsets(dims):
    return [(d,) for d in dims] + ([tuple(dims)] if len(dims) == 2 else [])


NEAR = [("c",), ("x",), ("y",), ("x", "y"), ("z0",), ("z1",), ("z1", "z0")]


def greet(pos):
    barrier = pltpu.get_barrier_semaphore()
    for dims in NEAR:
        pl.semaphore_signal(
            barrier, inc=1, device_id=partner(pos, dims), device_id_type=pl.DeviceIdType.MESH
        )
    pl.semaphore_wait(barrier, len(NEAR))


def remote(src, dst, send_sem, recv_sem, device):
    return pltpu.make_async_remote_copy(
        src_ref=src, dst_ref=dst, send_sem=send_sem, recv_sem=recv_sem,
        device_id=device, device_id_type=pl.DeviceIdType.MESH,
    )


def by_core(pos, action):
    for c in range(2):
        pl.when(pos["c"] == c)(functools.partial(action, c))


def half(c):
    return slice(384 * c, 384 * c + 384)


PARTS = [("p", 0), ("h", 0), ("h", 1), ("h", 2), ("h", 3), ("u", 4), ("u", 6), ("u", 8), ("u", 10)]
Z = ("z1", "z0")
SHORT = ((Z, ("x", "y")),) * 2
PLAIN = ((Z, ("x",), ("y",)), (Z, ("y",), ("x",)))
ROUTES = [SHORT, SHORT] + [PLAIN] * 7


class Gather:
    def __init__(self, pos, wg, wp, stage, stage_p, send, recv):
        self.pos, self.wg, self.wp = pos, wg, wp
        self.stage, self.stage_p = stage, stage_p
        self.send, self.recv = send, recv

    def view(self, i, c, index):
        kind, u = PARTS[i]
        if kind == "p":
            return self.wp.at[index + (slice(None), half(c))]
        if kind == "h":
            return self.wg.at[(u,) + index + (slice(None), half(c))]
        return self.wg.at[(u + c,) + index]

    def staged(self, i, c, rows):
        kind, u = PARTS[i]
        if kind == "p":
            return self.stage_p.at[rows, half(c)]
        if kind == "h":
            return self.stage.at[u, rows, half(c)]
        return self.stage.at[u + c, rows, :]

    def swap(self, i, c):
        own = pl.ds(16 * c, 16) if PARTS[i][0] == "p" else pl.ds(24 * c, 24)
        view = self.staged(i, 1 - c, own)
        return remote(view, view, self.send.at[i, 10], self.recv.at[i, 10], partner(self.pos, ("c",)))

    def hops(self, i, s, c):
        route = ROUTES[i][c]
        first = sum(len(subsets(dims)) for dims in route[:s])
        view = self.view(i, c, cube(self.pos, sum(route[:s], ())))
        return [
            remote(view, view, self.send.at[i, first + n], self.recv.at[i, first + n], partner(self.pos, dims))
            for n, dims in enumerate(subsets(route[s]))
        ]

    def gives(self, i, late, c):
        route = ROUTES[i][c]
        full = sum(route[:-1], ())
        ways = subsets(route[-1]) if late else [()]
        views = [self.view(i, c, cube(self.pos, full, dims)) for dims in ways]
        return [
            remote(
                view, view, self.send.at[i, 6 + late + n], self.recv.at[i, 6 + late + n],
                partner(self.pos, ("c",)),
            )
            for n, view in enumerate(views)
        ]

    def begin(self, i):
        def action(c):
            other = pl.ds(16 * (1 - c), 16) if PARTS[i][0] == "p" else pl.ds(24 * (1 - c), 24)
            view = self.staged(i, c, other)
            remote(
                view, view, self.send.at[i, 10], self.recv.at[i, 10], partner(self.pos, ("c",))
            ).wait_recv()
            rows = slice(0, 32 if PARTS[i][0] == "p" else 48)
            block = self.view(i, c, cube(self.pos, ()))
            block[...] = self.staged(i, c, rows)[...].astype(BF16)
            for copy in self.hops(i, 0, c):
                copy.start()

        by_core(self.pos, action)

    def step(self, i, s):
        def action(c):
            last = len(ROUTES[i][c]) - 1
            for copy in self.hops(i, s, c):
                copy.wait_recv()
            if s < last:
                for copy in self.hops(i, s + 1, c):
                    copy.start()
            if s >= last - 1:
                for copy in self.gives(i, s - last + 1, c):
                    copy.start()

        by_core(self.pos, action)

    def need(self, i):
        def action(c):
            for late in range(2):
                for copy in self.gives(i, late, 1 - c):
                    copy.wait_recv()

        by_core(self.pos, action)

    def finish(self):
        def action(c):
            for i in range(len(PARTS)):
                self.swap(i, c).wait_send()
                for s in range(len(ROUTES[i][c])):
                    for copy in self.hops(i, s, c):
                        copy.wait_send()
                for late in range(2):
                    for copy in self.gives(i, late, c):
                        copy.wait_send()

        by_core(self.pos, action)


class VectorSum:
    PHASES = (("c",), ("x", "y"), Z)

    def __init__(self, pos, rows, held, got, send, recv):
        self.pos, self.rows, self.held, self.got, self.send, self.recv = pos, rows, held, got, send, recv

    def copies(self, s):
        first = sum(len(subsets(dims)) for dims in self.PHASES[:s])
        return [
            remote(
                self.held.at[s, self.rows], self.got.at[first + n, self.rows],
                self.send.at[first + n], self.recv.at[first + n], partner(self.pos, dims),
            )
            for n, dims in enumerate(subsets(self.PHASES[s]))
        ]

    def start(self, s=0):
        for copy in self.copies(s):
            copy.start()

    def step(self, s):
        first = sum(len(subsets(dims)) for dims in self.PHASES[:s])
        total = self.held[s, self.rows]
        for n, copy in enumerate(self.copies(s)):
            copy.wait_recv()
            total = total + self.got[first + n, self.rows]
        self.held[s + 1, self.rows] = total
        if s < 2:
            self.start(s + 1)

    def finish(self):
        for s in range(3):
            for copy in self.copies(s):
                copy.wait_send()


def square(ref, u):
    return ref[u].reshape(D, D)


def forward_kernel(
    fast,
    *refs,
):
    refs = list(refs)
    take = lambda n: [refs.pop(0) for _ in range(n)]
    seg_ref, cfg_ref, feat_hbm, cot_hbm = take(4)
    if fast:
        own_p, own_a, own_o, own_f, own_s = take(5)
        wg_out, wp_out, svec = None, None, None
    else:
        wg_hbm, wp_hbm, svec = take(3)
    (
        act_out, hlt_out, qkv_out, kt_out, mixed_out, mixedt_out, xh1_out, inv1_out, flt_out,
        active_out, gp_out, d2_out, dg_out, dgt_out, lse_out, sg_out,
    ) = take(16)
    if fast:
        wg_out, wp_out, svec = take(3)
    (
        feat, cot, wg, wp, hid, hl, hlt, qkv, kt, vt, mixed, mixedt, xh1, fl, flt, active, gp, dg, dgt,
        kpat, qpat, sem_in, sem_out,
    ) = take(23)
    if fast:
        raw_p, raw_a, raw_o, raw_f, stage, stage_p, sem_raw, g_send, g_recv, sv_held, sv_got, v_send, v_recv = take(13)
    act = hl
    outs = []

    def load(i, src, dst):
        copy = pltpu.make_async_copy(src, dst, sem_in.at[i])
        copy.start()
        return copy

    def save(src, dst, part=None):
        i = len(outs)
        pick = lambda ref: ref if part is None else ref.at[part]
        make = lambda: pltpu.make_async_copy(pick(src), pick(dst), sem_out.at[i])
        make().start()
        outs.append(make)

    def need(i):
        kind, u = PARTS[i]
        if fast:
            gather.need(i)
            if kind == "p":
                save(wp, wp_out)
            elif kind == "h":
                save(wg, wg_out, u)
            else:
                save(wg, wg_out, pl.ds(u, 2))
        elif kind == "p":
            c_wp.wait()
        else:
            for v in range(u, u + (2 if kind == "u" else 1)):
                c_w[v].wait()

    def run(*steps):
        if fast:
            for i, s in steps:
                if i == "v":
                    vector.step(s)
                elif s < 0:
                    gather.begin(i)
                else:
                    gather.step(i, s)

    width = cfg_ref[0, 0]
    count = 1.0 / width.astype(F32)
    c_feat = load(0, feat_hbm, feat)
    if fast:
        pos = here()
        raws = [
            pltpu.make_async_copy(src, dst, sem_raw.at[i])
            for i, (src, dst) in enumerate(
                [(own_p, raw_p), (own_a, raw_a), (own_o, raw_o), (own_f, raw_f), (own_s, sv_held.at[0])]
            )
        ]
        for copy in raws:
            copy.start()
        gather = Gather(pos, wg, wp, stage, stage_p, g_send, g_recv)
        vector = VectorSum(pos, slice(0, 88), sv_held, sv_got, v_send, v_recv)
        for copy in raws:
            copy.wait()

        def arrange(c):
            rows = slice(24 * c, 24 * c + 24)
            stage_p[16 * c : 16 * c + 16, :] = raw_p[...]
            for j in range(3):
                for i in range(3):
                    stage[j, rows, 256 * i : 256 * i + 256] = raw_a[i, :, 256 * j : 256 * j + 256]
            stage[3, rows, :] = raw_o[...]
            for i in range(2):
                for q in range(4):
                    stage[4 + 4 * i + q, rows, :] = raw_f[i, :, D * q : D * q + D]

        by_core(pos, arrange)
        greet(pos)
        by_core(pos, lambda c: gather.swap(0, c).start())
        vector.start(0)
        for i in range(1, len(PARTS)):
            by_core(pos, lambda c, i=i: gather.swap(i, c).start())
        run((0, -1), (1, -1))
    else:
        c_wp = load(1, wp_hbm, wp)
        c_w = [load(2 + u, wg_hbm.at[u], wg.at[u]) for u in range(12)]
    c_cot = load(14, cot_hbm, cot)
    fill_patterns(seg_ref, kpat, qpat)
    run(("v", 0), (0, 0), ("v", 1), (2, -1), (1, 0), (3, -1), ("v", 2), (0, 1))
    if fast:
        for i in range(VEC // 128):
            svec[0:1, 128 * i : 128 * i + 128] = sv_held[3, i : i + 1, :]
    c_feat.wait()
    need(0)

    @pl.loop(0, NT)
    def _(t):
        rows = rows_of(t)
        normed = norm0(feat, svec, rows)[2]
        h = (mm(normed, wp[...].reshape(FEAT, D)) + piece(svec, "bp")) * keep_row(D, width)
        hid[rows, :] = h
        low = h.astype(BF16)
        hl[rows, :] = low
        hlt[:, rows] = low.T

    save(hlt, hlt_out)
    run((2, 0), (1, 1), (3, 0), (4, -1), (5, -1))
    need(1)

    slots = [
        [[], [(2, 1), (3, 1)]],
        [[(4, 0), (6, -1)], [(5, 0), (7, -1), (4, 1), (2, 2)]],
        [[], [(6, 0), (8, -1)]],
        [[(4, 2), (5, 1), (7, 0)], []],
        [[], [(6, 1), (8, 0)]],
        [[(7, 1)], [(5, 2)]],
    ]

    def at_slot(p, e):
        if fast:
            for i in range(PAIRS):
                if slots[i][e]:

                    @pl.when(p == i)
                    def _(i=i):
                        run(*slots[i][e])

    @pl.loop(0, PAIRS)
    def _(p):
        for j in range(3):

            @pl.when(p == 2 * j)
            def _(j=j):
                if j:
                    need(1 + j)

        @pl.when(lax.rem(p, 2) == 0)
        def _():
            j = lax.div(p, 2)
            group = lanes_of(j, 256)

            @pl.loop(0, NT)
            def _(t):
                rows = rows_of(t)
                keep = keep_row(256, cfg_ref[0, 1] * HDIM - j * 256)
                o = mm(hl[rows, :], square(wg, j))
                bias = lambda name: svec[0:1, pl.ds(pl.multiple_of(OFFSETS[name] + j * 256, 128), 256)]
                qkv[0, rows, group] = ((o[:, 0:256] + bias("bq")) * keep).astype(BF16)
                k = (o[:, 256:512] * keep).astype(BF16)
                qkv[1, rows, group] = k
                v = ((o[:, 512:768] + bias("bv")) * keep).astype(BF16)
                qkv[2, rows, group] = v
                down = pl.ds(pl.multiple_of(j * 256, 256), 256)
                kt[down, rows] = k.T
                vt[down, rows] = v.T

        if fast:

            @pl.when(p == 2)
            def _():
                run((3, 2))

        lanes = lanes_of(p)
        for e in range(2):
            kaug = qkv[1, :, lanes] * half_mask(e) + kpat[e]
            head_rows = pl.ds(pl.multiple_of(p * 128 + 64 * e, 64), 64)
            for b in range(NT):
                lo, hi = KEY_RANGE[b]
                cols = slice(b * TILE, (b + 1) * TILE)
                qaug = qkv[0, cols, lanes] * (half_mask(e) * 0.125) + qpat[e, cols, :]
                st = mm_nt(kaug[lo:hi], qaug)
                peak = jnp.max(st, 0, keepdims=True)
                power = jnp.exp(st - peak)
                total = col_sum(power)
                ot = mm(vt[head_rows, lo:hi], power.astype(BF16))
                mixedt[head_rows, cols] = (ot * (1.0 / total)).astype(BF16)
                lse_out[pl.ds(2 * p + e, 1), cols] = peak + jnp.log(total)
            at_slot(p, e)

    save(qkv, qkv_out)
    save(kt, kt_out)
    save(mixedt, mixedt_out)
    need(4)

    @pl.loop(0, NT)
    def _(t):
        rows = rows_of(t)
        keep = keep_row(D, width)
        mix = mixedt[:, rows].T
        mixed[rows, :] = mix
        z = hid[rows, :] + (mm(mix, square(wg, 3)) + piece(svec, "bo")) * keep
        centred = (z - row_sum(z * keep) * count) * keep
        inv = lax.rsqrt(row_sum(centred * centred) * count + NORM_EPS)
        hat = centred * inv
        first = (hat * piece(svec, "g1") + piece(svec, "c1")) * keep
        xh1[rows, :] = hat.astype(BF16)
        inv1_out[rows, :] = jnp.broadcast_to(inv, (TILE, 128))
        hid[rows, :] = first + piece(svec, "b2") * keep
        low = first.astype(BF16)
        fl[rows, :] = low
        flt[:, rows] = low.T

    save(mixed, mixed_out)
    save(xh1, xh1_out)
    save(flt, flt_out)
    need(5)

    def up(q):
        @pl.loop(0, NT)
        def _(t):
            rows = rows_of(t)
            u = (mm(fl[rows, :], square(wg, 4 + q)) + piece(svec, "b1", q * D, D)) * keep_row(
                D, cfg_ref[0, 2], q * D
            )
            g, slope = gelu_both(u)
            active[q, rows, :] = g.astype(BF16)
            gp[q, rows, :] = slope.astype(BF16)

        save(active, active_out, q)
        save(gp, gp_out, q)

    def down(q):
        @pl.loop(0, NT)
        def _(t):
            rows = rows_of(t)
            hid[rows, :] += mm_nt(active[q, rows, :], square(wg, 8 + q)) * keep_row(D, width)

    up(0)
    run((8, 1), (6, 2))
    up(1)
    need(6)
    up(2)
    run((7, 2))
    up(3)
    need(7)
    down(0)
    down(1)
    run((8, 2))
    need(8)
    down(2)
    down(3)
    c_cot.wait()
    zero = jnp.zeros((1, D), F32)

    def last(t, sums):
        gain_sum, shift_sum, bias_sum = sums
        rows = rows_of(t)
        keep = keep_row(D, width)
        z = hid[rows, :]
        centred = (z - row_sum(z * keep) * count) * keep
        inv = lax.rsqrt(row_sum(centred * centred) * count + NORM_EPS)
        hat = centred * inv
        gain = piece(svec, "g2")
        act[rows, :] = ((hat * gain + piece(svec, "c2")) * keep).astype(BF16)
        g = cot[rows, :].astype(F32) * keep
        gain_sum = gain_sum + col_sum(g * hat)
        shift_sum = shift_sum + col_sum(g)
        a = g * gain
        d2 = inv * (a - keep * (row_sum(a) * count) - hat * (row_sum(a * hat) * count))
        hid[rows, :] = d2
        low = d2.astype(BF16)
        dg[rows, :] = low
        dgt[:, rows] = low.T
        return gain_sum, shift_sum, bias_sum + col_sum(low.astype(F32))

    gain_sum, shift_sum, bias_sum = lax.fori_loop(0, NT, last, (zero, zero, zero))
    sg_out[...] = jnp.zeros((88, 128), F32)
    put(sg_out, "g2", gain_sum)
    put(sg_out, "c2", shift_sum)
    put(sg_out, "b2", bias_sum)
    save(act, act_out)
    save(hid, d2_out)
    save(dg, dg_out)
    save(dgt, dgt_out)
    if fast:
        gather.finish()
        vector.finish()
    for make in outs:
        make().wait()


R_PARTS = [("u", 8), ("u", 4), ("u", 10), ("u", 6), ("h", 3), ("h", 0), ("h", 1), ("h", 2), ("p", 0)]
R_PLAIN = ((("x",), ("y",), Z), (("y",), ("x",), Z))
R_SHORT = ((("x", "y"), Z),) * 2
R_ROUTES = [R_PLAIN] * 7 + [R_SHORT] * 2


class Scatter:
    def __init__(self, pos, acc, got, given, first, fin, gout, goutp, send, recv, local, credit):
        self.pos, self.acc, self.got, self.given, self.first = pos, acc, got, given, first
        self.fin, self.gout, self.goutp = fin, gout, goutp
        self.send, self.recv, self.local, self.credit = send, recv, local, credit

    def trim(self, i):
        kind = R_PARTS[i][0]
        if kind == "u":
            return ()
        return (slice(0, 32 if kind == "p" else 48), slice(0, 384))

    def held(self, bufs, i, index):
        kind = R_PARTS[i][0]
        if kind == "p":
            return bufs[2].at[index]
        if kind == "h":
            return bufs[1].at[(i - 4,) + index]
        return bufs[0].at[(i,) + index]

    def slot(self, buf, i):
        full = (slice(None),) * 4
        return buf.at[(i % 2,) + full + self.trim(i)]

    def hand(self, i):
        return remote(
            self.slot(self.given, i), self.slot(self.first, i), self.send.at[i, 6], self.recv.at[i, 6],
            partner(self.pos, ("c",)),
        )

    def hops(self, i, s, c):
        route = R_ROUTES[i][c]
        first = sum(len(subsets(dims)) for dims in route[:s])
        rest = sum(route[s + 1 :], ())
        dst = self.held(self.got, i, cube(self.pos, rest, sum(route[: s + 1], ())))
        return [
            remote(
                self.held(self.acc, i, cube(self.pos, rest, dims)), dst,
                self.send.at[i, first + n], self.recv.at[i, first + n], partner(self.pos, dims),
            )
            for n, dims in enumerate(subsets(route[s]))
        ]

    def came(self, i, s, c):
        route = R_ROUTES[i][c]
        rest = sum(route[s + 1 :], ())
        before = sum(route[:s], ())
        return [
            self.held(self.got, i, cube(self.pos, rest, before + tuple(d for d in route[s] if d not in dims)))
            for dims in subsets(route[s])
        ]

    def offer(self, i):
        if i >= 2:
            pl.semaphore_wait(self.credit, 1)
        self.hand(i).start()

    def reuse(self, i):
        if i >= 2:
            self.hand(i - 2).wait_send()

    def begin(self, i):
        self.hand(i).wait_recv()
        mine = self.held(self.acc, i, (slice(None),) * 4)
        mine[...] = mine[...] + self.slot(self.first, i)[...]
        if i < len(R_PARTS) - 2:
            pl.semaphore_signal(
                self.credit, inc=1, device_id=partner(self.pos, ("c",)),
                device_id_type=pl.DeviceIdType.MESH,
            )

        def action(c):
            for copy in self.hops(i, 0, c):
                copy.start()

        by_core(self.pos, action)

    def ends(self, i, c, own):
        kind, u = R_PARTS[i]
        rows = 16 if kind == "p" else 24
        fin = self.held(self.fin, i, ())
        if kind == "p":
            dst = self.goutp.at[:, half(c)]
        elif kind == "h":
            dst = self.gout.at[u, :, half(c)]
        else:
            dst = self.gout.at[u + c]
        if own:
            return pltpu.make_async_copy(fin.at[pl.ds(rows * c, rows)], dst, self.local.at[i])
        return remote(
            fin.at[pl.ds(rows * (1 - c), rows)], dst, self.send.at[i, 7], self.recv.at[i, 7],
            partner(self.pos, ("c",)),
        )

    def step(self, i, s):
        def action(c):
            route = R_ROUTES[i][c]
            for copy in self.hops(i, s, c):
                copy.wait_recv()
            mine = self.held(self.acc, i, cube(self.pos, sum(route[s + 1 :], ())))
            total = mine[...].astype(F32)
            for came in self.came(i, s, c):
                total = total + came[...].astype(F32)
            if s < len(route) - 1:
                mine[...] = total.astype(BF16)
                for copy in self.hops(i, s + 1, c):
                    copy.start()
            else:
                self.held(self.fin, i, ())[...] = total
                for own in (True, False):
                    self.ends(i, c, own).start()

        by_core(self.pos, action)

    def finish(self):
        n = len(R_PARTS)
        for i in range(n - 2, n):
            self.hand(i).wait_send()

        def action(c):
            for i in range(n):
                for s in range(len(R_ROUTES[i][c])):
                    for copy in self.hops(i, s, c):
                        copy.wait_send()
                self.ends(i, c, True).wait()
                self.ends(i, c, False).wait_send()
                self.ends(i, 1 - c, False).wait_recv()

        by_core(self.pos, action)


def backward_kernel(fast, *refs):
    refs = list(refs)
    take = lambda n: [refs.pop(0) for _ in range(n)]
    seg_ref, cfg_ref, feat_hbm, wg_hbm, wp_hbm, svec = take(6)
    (
        hlt_hbm, qkv_hbm, kt_hbm, mixed_hbm, mixedt_hbm, xh1_hbm, inv1_hbm, flt_hbm,
        active_hbm, gp_hbm, d2_hbm, dg_hbm, dgt_hbm, lse, sg_in,
    ) = take(15)
    dx_out, gu_out, gwp_out, sg = take(4)
    (
        feat, wbuf, wp, pool, tr, kt, qkv, go, inv1, fg, dg, tg, delta, dqt, kpat, qpat,
        acc_u, acc_h, acc_p, given, sem_in, sem_q, sem_dx,
    ) = take(23)
    if fast:
        (
            got_u, got_h, got_p, first_in, fin_u, fin_h, fin_p, r_send, r_recv, r_local, credit,
            sv_held, sv_got, v_send, v_recv,
        ) = take(15)
        pos = here()
        core = pos["c"]
        small = sv_held.at[0]
        scatter = Scatter(
            pos, (acc_u, acc_h, acc_p), (got_u, got_h, got_p), given, first_in, (fin_u, fin_h, fin_p),
            gu_out, gwp_out, r_send, r_recv, r_local, credit,
        )
        late, early = (
            VectorSum(pos, rows, sv_held, sv_got, v_send.at[i], v_recv.at[i])
            for i, rows in enumerate((slice(0, 32), slice(32, 88)))
        )
    else:
        sem_out = take(1)[0]
        core = lax.axis_index("dp") % 2
        small = sg
        holder = Scatter(None, (acc_u, acc_h, acc_p), *[None] * 10)

    def load(i, src, dst):
        copy = pltpu.make_async_copy(src, dst, sem_in.at[i])
        copy.start()
        return copy

    def run(*steps):
        if fast:
            for i, s in steps:
                if i == "e":
                    early.step(s)
                elif i == "l":
                    late.step(s)
                elif s < 0:
                    scatter.begin(i)
                else:
                    scatter.step(i, s)

    def columns(h):
        return pl.ds(pl.multiple_of(384 * h, 128), 384)

    def plain_copy(i, mine):
        kind, u = R_PARTS[i]
        which = core if mine else 1 - core
        full = (slice(None),) * 4
        if mine:
            src = holder.held(holder.acc, i, full)
        else:
            src = given.at[(i % 2,) + full + holder.trim(i)]
        if kind == "p":
            dst = gwp_out.at[full + (slice(None), columns(which))]
        elif kind == "h":
            dst = gu_out.at[(u,) + full + (slice(None), columns(which))]
        else:
            dst = gu_out.at[u + which]
        return pltpu.make_async_copy(src, dst, sem_out.at[i, 1 if mine else 0])

    def make(i, mine, left, right):
        kind = R_PARTS[i][0]
        rows, width = (32, 384) if kind == "p" else (48, 384 if kind == "h" else D)
        if not mine:
            if fast:
                scatter.reuse(i)
            elif i >= 2:
                plain_copy(i - 2, False).wait()

        @pl.loop(0, 2)
        def _(y):
            span = pl.ds(pl.multiple_of(y * 8 * rows, 8 * rows), 8 * rows)
            value = mm(left[span, :], right[...]).astype(BF16).reshape(2, 2, 2, rows, width)
            if not mine:
                trim = (slice(0, rows), slice(0, width))
                given[(i % 2, y) + (slice(None),) * 3 + trim] = value
            elif kind == "p":
                acc_p[y] = value
            elif kind == "h":
                acc_h[i - 4, y] = value
            else:
                acc_u[i, y] = value

        if fast:
            if not mine:
                scatter.offer(i)
        else:
            plain_copy(i, mine).start()

    def quarter(k):
        s = k % 2
        q = 2 * (k // 2) + (core if k % 2 else 1 - core)
        pairs = [
            (active_hbm.at[q], pool.at[s]),
            (wg_hbm.at[8 + q], wbuf.at[s]),
            (gp_hbm.at[q], pool.at[2 + s]),
            (wg_hbm.at[4 + q], wbuf.at[2 + s]),
        ]
        return q, [
            pltpu.make_async_copy(src, dst, sem_q.at[s, i]) for i, (src, dst) in enumerate(pairs)
        ]

    dgt, flt, ig = tr.at[0], tr.at[1], pool.at[4]
    c_dgt = load(0, dgt_hbm, dgt)
    for copy in quarter(0)[1]:
        copy.start()
    c_dg = load(1, dg_hbm, dg)
    c_flt = load(2, flt_hbm, flt)
    c_d2 = load(3, d2_hbm, fg)
    for copy in quarter(1)[1]:
        copy.start()
    c_xh1 = load(4, xh1_hbm, go)
    c_inv1 = load(5, inv1_hbm, inv1)
    c_mixed = load(6, mixed_hbm, pool.at[5])
    c_qkv = load(9, qkv_hbm, qkv)
    c_kt = load(10, kt_hbm, kt)
    c_wp = load(15, wp_hbm, wp)
    c_feat = load(16, feat_hbm, feat)

    width = cfg_ref[0, 0]
    count = 1.0 / width.astype(F32)
    if fast:
        greet(pos)
    small[...] = sg_in[...]
    fill_patterns(seg_ref, kpat, qpat)
    c_dgt.wait()
    events = {
        (1, 0): [(0, -1)],
        (1, 2): [(1, -1)],
        (3, 0): [(2, -1), (0, 0)],
        (3, 2): [(3, -1), (1, 0)],
    }
    for k in range(4):
        s = k % 2
        mine = bool(k % 2)
        q, copies = quarter(k)
        at = lambda n: run(*events.get((k, n), []))
        copies[0].wait()
        make(2 * (k // 2), mine, dgt, pool.at[s])
        at(0)
        if k == 0:
            c_dg.wait()
        copies[1].wait()
        copies[2].wait()

        def inner(t, bias, q=q, s=s):
            rows = rows_of(t)
            low = (
                mm(dg[rows, :], square(wbuf, s))
                * pool[2 + s, rows, :].astype(F32)
                * keep_row(D, cfg_ref[0, 2] - q * D)
            ).astype(BF16)
            ig[rows, :] = low
            return bias + col_sum(low.astype(F32))

        put(small, "b1", lax.fori_loop(0, NT, inner, jnp.zeros((1, D), F32)), q * D)
        at(1)
        if k == 0:
            c_flt.wait()
            c_d2.wait()
        make(2 * (k // 2) + 1, mine, flt, ig)
        at(2)
        copies[3].wait()

        @pl.loop(0, NT)
        def _(t, s=s):
            rows = rows_of(t)
            fg[rows, :] += mm_nt(ig[rows, :], square(wbuf, 2 + s))

        at(3)
        if k < 2:
            for copy in quarter(k + 2)[1]:
                copy.start()
        if k == 2:
            c_wo = load(8, wg_hbm.at[3], wbuf.at[0])
            c_wa = [load(12, wg_hbm.at[0], wbuf.at[2])]

    mixedt, hlt, mixed = tr.at[0], tr.at[1], pool.at[5]
    c_mixedt = load(7, mixedt_hbm, mixedt)
    c_hlt = load(11, hlt_hbm, hlt)
    c_wa.append(load(13, wg_hbm.at[1], wbuf.at[1]))
    c_wa.append(load(14, wg_hbm.at[2], wbuf.at[3]))
    wa_slot = (2, 1, 3)
    for copy in (c_xh1, c_inv1, c_mixed, c_wo):
        copy.wait()
    zero = jnp.zeros((1, D), F32)

    def middle(t, sums):
        gain_sum, shift_sum, bias_sum = sums
        rows = rows_of(t)
        keep = keep_row(D, width)
        hat = go[rows, :].astype(F32)
        g = fg[rows, :] * keep
        gain_sum = gain_sum + col_sum(g * hat)
        shift_sum = shift_sum + col_sum(g)
        a = g * piece(svec, "g1")
        d1 = inv1[rows, 0:1] * (a - keep * (row_sum(a) * count) - hat * (row_sum(a * hat) * count))
        fg[rows, :] = d1
        low = d1.astype(BF16)
        dg[rows, :] = low
        mg = mm_nt(low, square(wbuf, 0)).astype(BF16)
        go[rows, :] = mg
        product = mg.astype(F32) * mixed[rows, :].astype(F32)
        high = product.astype(BF16)
        rest = (product - high.astype(F32)).astype(BF16)
        lane = lax.broadcasted_iota(jnp.int32, (16, D), 1)
        head = lax.broadcasted_iota(jnp.int32, (16, D), 0)
        pick = ((lane >= head * HDIM) & (lane < head * HDIM + HDIM)).astype(F32).astype(BF16)
        delta[:, rows] = mm_nt(pick, high) + mm_nt(pick, rest)
        return gain_sum, shift_sum, bias_sum + col_sum(low.astype(F32))

    gain_sum, shift_sum, bias_sum = lax.fori_loop(0, NT, middle, (zero, zero, zero))
    put(small, "g1", gain_sum)
    put(small, "c1", shift_sum)
    put(small, "bo", bias_sum)
    if fast:
        early.start()
    run((0, 1))
    c_mixedt.wait()
    make(4, False, mixedt, dg.at[:, columns(1 - core)])
    make(4, True, mixedt, dg.at[:, columns(core)])

    c_qkv.wait()
    c_kt.wait()
    c_hlt.wait()
    for copy in c_wa:
        copy.wait()
    slots = [
        [[], [(2, 0), (1, 1), (4, -1)], [("e", 0), (3, 0)], []],
        [[], [(5, -1), (1, 2), ("e", 2), (3, 1)], [], [(4, 1)]],
        [[], [(6, -1), (3, 2), (4, 2)], [], [(5, 1)]],
    ]
    after_loop = [[(0, 2), ("e", 1)], [], []]
    after_make = [[(4, 0)], [(5, 0), (2, 2)], [(6, 0)]]
    after_back = [[(2, 1)], [], [(7, -1)]]

    def chunk(n):
        return n // 3, slice(256 * (n % 3), 256 * (n % 3) + 256)

    for j in range(3):

        def at_slot(pp, e, j=j):
            if fast:
                for i in range(2):
                    steps = slots[j][2 * i + e]
                    if steps:

                        @pl.when(pp == i)
                        def _(steps=steps):
                            run(*steps)

        @pl.loop(0, 2)
        def _(pp, j=j):
            p = j * 2 + pp
            lanes = lanes_of(p)
            for e in range(2):
                at_slot(pp, e)
                kaug = qkv[1, :, lanes] * half_mask(e) + kpat[e]
                head_rows = pl.ds(pl.multiple_of(p * 128 + 64 * e, 64), 64)
                for b in range(NT):
                    lo, hi = KEY_RANGE[b]
                    cols = slice(b * TILE, (b + 1) * TILE)
                    qaug = qkv[0, cols, lanes] * (half_mask(e) * 0.125) + qpat[e, cols, :]
                    st = mm_nt(kaug[lo:hi], qaug)
                    weights = jnp.exp(st - lse[pl.ds(2 * p + e, 1), cols])
                    n, span = chunk(4 * e + b)
                    pool[n, lo:hi, span] = weights.astype(BF16)
                    goe = go[cols, lanes] * half_mask(e)
                    dp = mm_nt(qkv[2, lo:hi, lanes], goe)
                    ds = (weights * (dp - delta[pl.ds(2 * p + e, 1), cols])).astype(BF16)
                    n, span = chunk(8 + 4 * e + b)
                    pool[n, lo:hi, span] = ds
                    dqt[64 * e : 64 * e + 64, cols] = mm(kt[head_rows, lo:hi], ds)
            keep = keep_row(128, cfg_ref[0, 1] * HDIM - p * 128)
            for t in range(NT):
                rows = slice(t * TILE, (t + 1) * TILE)
                dk = jnp.zeros((TILE, 128), F32)
                dv = jnp.zeros((TILE, 128), F32)
                for b in range(NT):
                    if not KEY_RANGE[b][0] <= t * TILE < KEY_RANGE[b][1]:
                        continue
                    cols = slice(b * TILE, (b + 1) * TILE)
                    for e in range(2):
                        n, span = chunk(8 + 4 * e + b)
                        dk = dk + mm(pool[n, rows, span], qkv[0, cols, lanes] * half_mask(e))
                        n, span = chunk(4 * e + b)
                        dv = dv + mm(pool[n, rows, span], go[cols, lanes] * half_mask(e))
                dq = dqt[:, rows].T
                for i, value in enumerate((dq * (keep * 0.125), dk * (keep * 0.125), dv * keep)):
                    tg[rows, pl.ds(pl.multiple_of(256 * i + pp * 128, 128), 128)] = value.astype(BF16)

        run(*after_loop[j])
        make(5 + j, False, hlt, tg.at[:, columns(1 - core)])
        make(5 + j, True, hlt, tg.at[:, columns(core)])
        run(*after_make[j])

        def back(t, bias, j=j):
            rows = rows_of(t)
            fg[rows, :] += mm_nt(tg[rows, :], square(wbuf, wa_slot[j]))
            return bias + col_sum(tg[rows, :].astype(F32))

        bias = lax.fori_loop(0, NT, back, zero)
        put(small, "bq", bias[:, 0:256], 256 * j)
        put(small, "bv", bias[:, 512:768], 256 * j)
        run(*after_back[j])

    c_wp.wait()
    c_feat.wait()
    zero_feat = jnp.zeros((1, FEAT), F32)
    nrmt = tr.at[0]

    def first(t, bias_sum):
        rows = rows_of(t)
        nrmt[0:FEAT, rows] = norm0(feat, svec, rows)[2].T
        low = (fg[rows, :] * keep_row(D, width)).astype(BF16)
        dg[rows, :] = low
        return bias_sum + col_sum(low.astype(F32))

    put(small, "bp", lax.fori_loop(0, NT, first, zero))
    run((5, 2))
    make(8, False, nrmt, dg.at[:, columns(1 - core)])
    make(8, True, nrmt, dg.at[:, columns(core)])

    def second(t, sums):
        gain_sum, shift_sum = sums
        rows = rows_of(t)
        hat, inv, _ = norm0(feat, svec, rows)
        g = mm_nt(dg[rows, :], wp[...].reshape(FEAT, D))
        gain_sum = gain_sum + col_sum(g * hat)
        shift_sum = shift_sum + col_sum(g)
        a = g * piece(svec, "g0")
        dx = inv * (a - row_sum(a) * (1.0 / FEAT) - hat * (row_sum(a * hat) * (1.0 / FEAT)))
        fg[rows, 0:FEAT] = 0.1 * dx
        return gain_sum, shift_sum

    gain_sum, shift_sum = lax.fori_loop(0, NT, second, (zero_feat, zero_feat))
    put(small, "g0", gain_sum)
    put(small, "b0", shift_sum)
    c_dx = pltpu.make_async_copy(fg.at[:, 0:FEAT], dx_out, sem_dx)
    c_dx.start()
    if fast:
        late.start()
        run((8, -1), (6, 1), (7, 0), ("l", 0), (8, 0), (6, 2), ("l", 1), (7, 1), (8, 1), ("l", 2))
        sg[...] = sv_held[3]
        early.finish()
        late.finish()
        scatter.finish()
    else:
        for i in range(len(R_PARTS)):
            plain_copy(i, True).wait()
        for i in range(len(R_PARTS) - 2, len(R_PARTS)):
            plain_copy(i, False).wait()
    c_dx.wait()


def adam_rule(weight, moment, square_in, grad, rate):
    moment_new = BETA_ONE * moment + (1.0 - BETA_ONE) * grad
    square_new = BETA_TWO * square_in + (1.0 - BETA_TWO) * grad * grad
    fix_one = 1.0 - BETA_ONE**STEP
    fix_two = 1.0 - BETA_TWO**STEP
    direction = moment_new / fix_one / (jnp.sqrt(square_new / fix_two) + ADAM_EPS)
    return (moment_new, square_new, weight - rate * (direction + DECAY * weight))


def adam_kernel(*refs):
    gu_hbm, gp_hbm, gs_hbm, act_hbm, dx_hbm = refs[0:5]
    ins, act_out, dx_out, outs = refs[5:20], refs[20], refs[21], refs[22:42]
    gu, gp, gs = refs[42:45]
    held = refs[45:60]
    new = refs[60:75]
    sem_in, sem_out = refs[75:]
    moves = [
        pltpu.make_async_copy(src, dst, sem_out.at[20 + i])
        for i, (src, dst) in enumerate([(act_hbm, act_out), (dx_hbm, dx_out)])
    ]
    loads = [
        pltpu.make_async_copy(src, dst, sem_in.at[i])
        for i, (src, dst) in enumerate(zip((gp_hbm, gu_hbm, gs_hbm) + tuple(ins), (gp, gu, gs) + tuple(held)))
    ]
    for copy in loads + moves:
        copy.start()

    def update(k, index, grad, rate):
        w, m, v = (ref[index] for ref in held[3 * k : 3 * k + 3])
        for ref, value in zip(new[3 * k : 3 * k + 3], adam_rule(w, m, v, grad, rate)):
            ref[index] = value
        return grad

    def ready(k):
        for copy in loads[3 + 3 * k : 6 + 3 * k]:
            copy.wait()

    stores = []

    def store(k):
        for i in range(3):
            copy = pltpu.make_async_copy(new[3 * k + i], outs[4 * k + 1 + i], sem_out.at[4 * k + 1 + i])
            copy.start()
            stores.append(copy)
        copy = pltpu.make_async_copy(held[3 * k + 1], outs[4 * k], sem_out.at[4 * k])
        copy.start()
        stores.append(copy)

    def keep(k, index, grad):
        held[3 * k + 1][index] = grad

    everything = (slice(None), slice(None))
    loads[1].wait()
    ready(3)
    for i in range(2):
        for q in range(4):
            span = (i, slice(None), slice(D * q, D * q + D))
            keep(3, span, update(3, span, gu[4 + 4 * i + q], RATE))
    store(3)
    ready(1)
    for i in range(3):
        for j in range(3):
            span = (i, slice(None), slice(256 * j, 256 * j + 256))
            keep(1, span, update(1, span, gu[j, :, 256 * i : 256 * i + 256], RATE))
    store(1)
    ready(2)
    keep(2, everything, update(2, everything, gu[3], RATE))
    store(2)
    loads[0].wait()
    ready(0)
    keep(0, everything, update(0, everything, gp[...], RATE))
    store(0)
    loads[2].wait()
    ready(4)
    keep(4, everything, update(4, everything, gs[...], SMALL_RATE))
    store(4)
    for copy in stores + moves:
        copy.wait()


def adam_call(gu, gp, gs, act, dx, state):
    shape = jax.ShapeDtypeStruct
    f32 = lambda s: pltpu.VMEM(s, F32)
    outs = [shape((LEN, D), BF16), shape((LEN, FEAT), F32)]
    outs += [shape(state[3 * k].shape, F32) for k in range(5) for _ in range(4)]
    scratch = [f32(gu.shape), f32(gp.shape), f32(gs.shape)]
    scratch += [f32(state[i].shape) for i in range(15)] + [f32(state[i].shape) for i in range(15)]
    scratch += [pltpu.SemaphoreType.DMA((18,)), pltpu.SemaphoreType.DMA((22,))]
    return pl.pallas_call(
        adam_kernel,
        out_shape=outs,
        in_specs=[any_spec()] * 20,
        out_specs=[any_spec()] * 22,
        scratch_shapes=scratch,
        compiler_params=pltpu.CompilerParams(vmem_limit_bytes=VMEM_LIMIT),
        name="adam",
    )(gu, gp, gs, act, dx, *state)


def any_spec():
    return pl.BlockSpec(memory_space=pl.ANY)


def vmem_spec():
    return pl.BlockSpec(memory_space=pltpu.VMEM)


def smem_spec():
    return pl.BlockSpec(memory_space=pltpu.SMEM)


def forward_call(fast, seg, cfg, feat, cot, weights):
    shape = jax.ShapeDtypeStruct
    outs = [
        (shape((LEN, D), BF16), any_spec()),
        (shape((D, LEN), BF16), any_spec()),
        (shape((3, LEN, D), BF16), any_spec()),
        (shape((D, LEN), BF16), any_spec()),
        (shape((LEN, D), BF16), any_spec()),
        (shape((D, LEN), BF16), any_spec()),
        (shape((LEN, D), BF16), any_spec()),
        (shape((LEN, 128), F32), vmem_spec()),
        (shape((D, LEN), BF16), any_spec()),
        (shape((4, LEN, D), BF16), any_spec()),
        (shape((4, LEN, D), BF16), any_spec()),
        (shape((LEN, D), F32), any_spec()),
        (shape((LEN, D), BF16), any_spec()),
        (shape((D, LEN), BF16), any_spec()),
        (shape((16, LEN), F32), vmem_spec()),
        (shape((88, 128), F32), vmem_spec()),
    ]
    if fast:
        outs += [
            (shape((12,) + CUBE + (48, D), BF16), any_spec()),
            (shape(CUBE + (32, D), BF16), any_spec()),
            (shape((1, VEC), F32), vmem_spec()),
        ]
    bf = lambda *s: pltpu.VMEM(s, BF16)
    f32 = lambda *s: pltpu.VMEM(s, F32)
    dma = lambda *s: pltpu.SemaphoreType.DMA(s)
    scratch = [
        bf(LEN, FEAT), bf(LEN, D), bf(12, *CUBE, 48, D), bf(*CUBE, 32, D), f32(LEN, D),
        bf(LEN, D), bf(D, LEN), bf(3, LEN, D), bf(D, LEN), bf(D, LEN), bf(LEN, D), bf(D, LEN),
        bf(LEN, D), bf(LEN, D), bf(D, LEN), bf(4, LEN, D), bf(4, LEN, D), bf(LEN, D), bf(D, LEN),
        bf(2, LEN, 128), bf(2, LEN, 128), dma(15), dma(32),
    ]
    if fast:
        scratch += [
            f32(16, D), f32(3, 24, D), f32(24, D), f32(2, 24, FF), f32(12, 48, D), f32(32, D), dma(5),
            dma(len(PARTS), 11), dma(len(PARTS), 11), f32(4, 88, 128), f32(7, 88, 128), dma(7), dma(7),
        ]
        specs = [any_spec()] * len(weights)
        params = dict(collective_id=0, has_side_effects=True)
    else:
        specs = [any_spec()] * 2 + [vmem_spec()]
        params = {}
    return pl.pallas_call(
        functools.partial(forward_kernel, fast),
        out_shape=[o[0] for o in outs],
        in_specs=[smem_spec(), smem_spec()] + [any_spec()] * 2 + specs,
        out_specs=[o[1] for o in outs],
        scratch_shapes=scratch,
        compiler_params=pltpu.CompilerParams(vmem_limit_bytes=VMEM_LIMIT, **params),
        name="forward",
    )(seg, cfg, feat, cot, *weights)


def backward_call(fast, seg, cfg, feat, wg, wp, svec, saved):
    shape = jax.ShapeDtypeStruct
    bf = lambda *s: pltpu.VMEM(s, BF16)
    f32 = lambda *s: pltpu.VMEM(s, F32)
    dma = lambda *s: pltpu.SemaphoreType.DMA(s)
    n = len(R_PARTS)
    scratch = [
        bf(LEN, FEAT), bf(4, *CUBE, 48, D), bf(*CUBE, 32, D), bf(6, LEN, D), bf(2, D, LEN), bf(D, LEN),
        bf(3, LEN, D), bf(LEN, D), f32(LEN, 128), f32(LEN, D), bf(LEN, D), bf(LEN, D), f32(16, LEN),
        f32(128, LEN), bf(2, LEN, 128), bf(2, LEN, 128),
        bf(4, *CUBE, 48, D), bf(4, *CUBE, 48, 384), bf(*CUBE, 32, 384), bf(2, *CUBE, 48, D),
        dma(17), dma(2, 4), pltpu.SemaphoreType.DMA,
    ]
    if fast:
        scratch += [
            bf(4, *CUBE, 48, D), bf(4, *CUBE, 48, 384), bf(*CUBE, 32, 384), bf(2, *CUBE, 48, D),
            f32(4, 48, D), f32(4, 48, 384), f32(32, 384), dma(n, 8), dma(n, 8), dma(n),
            pltpu.SemaphoreType.REGULAR, f32(4, 88, 128), f32(7, 88, 128), dma(2, 7), dma(2, 7),
        ]
        grads = [shape((12, 24, D), F32), shape((16, D), F32)]
        params = dict(collective_id=1, has_side_effects=True)
    else:
        scratch += [dma(n, 2)]
        grads = [shape((12,) + CUBE + (48, D), BF16), shape(CUBE + (32, D), BF16)]
        params = {}
    return pl.pallas_call(
        functools.partial(backward_kernel, fast),
        out_shape=[shape((LEN, FEAT), F32)] + grads + [shape((88, 128), F32)],
        in_specs=[smem_spec(), smem_spec()] + [any_spec()] * 3 + [vmem_spec()]
        + [any_spec()] * 13 + [vmem_spec()] * 2,
        out_specs=[any_spec()] * 3 + [vmem_spec()],
        scratch_shapes=scratch,
        compiler_params=pltpu.CompilerParams(vmem_limit_bytes=VMEM_LIMIT, **params),
        name="backward",
    )(seg, cfg, feat, wg, wp, svec, *saved)


AXES = ("grp", "dp")


def gathered(projection_weight, attention_weight, output_weight, feedforward_weight, small_params):
    gather = lambda w, axis: lax.all_gather(w.astype(BF16), AXES, axis=axis, tiled=True)
    wp = gather(projection_weight, 0)
    wa = gather(attention_weight, 1)
    wo = gather(output_weight, 0)
    wf = gather(feedforward_weight, 1)
    svec = gather(small_params, 0).astype(F32).reshape(1, VEC)
    return units(wp, wa, wo, wf) + (svec,)


def units(wp, wa, wo, wf):
    groups = wa.reshape(3, D, 3, 256).transpose(2, 1, 0, 3).reshape(3, D, D)
    quarters = wf.reshape(2, D, 4, D).transpose(0, 2, 1, 3).reshape(8, D, D)
    wg = jnp.concatenate([groups, wo[None], quarters], 0)
    return wg.reshape((12,) + CUBE + (48, D)), wp.reshape(CUBE + (32, D))


def layer(fast, features, lengths, config, cotangent, weights):
    feat = features.reshape(LEN, FEAT)
    cot = cotangent.reshape(LEN, D)
    saved = forward_call(fast, lengths, config, feat, cot, weights)
    activations = saved[0]
    wg, wp, svec = saved[16:] if fast else weights
    dx, gu, gwp, sg = backward_call(fast, lengths, config, feat, wg, wp, svec, saved[1:16])
    return activations, dx, gu, gwp, sg


def per_device(
    fast,
    features, segment_lengths, subnet_config, cotangent,
    projection_weight, projection_moment, projection_square,
    attention_weight, attention_moment, attention_square,
    output_weight, output_moment, output_square,
    feedforward_weight, feedforward_moment, feedforward_square,
    small_params, small_moment, small_square,
):
    weights = (projection_weight, attention_weight, output_weight, feedforward_weight)
    if fast:
        me = lax.axis_index(AXES)
        low = lax.reduce_precision(small_params, 8, 7)
        placed = lax.dynamic_update_slice(jnp.zeros((88 * 128,), F32), low, (me * low.shape[0],))
        weights = weights + (placed.reshape(88, 128),)
    else:
        weights = gathered(*weights, small_params)
    activations, dx, gu, gwp, sg = layer(
        fast, features, segment_lengths, subnet_config, cotangent, weights
    )
    state = (
        projection_weight, projection_moment, projection_square,
        attention_weight, attention_moment, attention_square,
        output_weight, output_moment, output_square,
        feedforward_weight, feedforward_moment, feedforward_square,
        small_params[None], small_moment[None], small_square[None],
    )
    out = [activations.reshape(1, LEN, D), dx.reshape(1, LEN, FEAT)]
    vec = sg.reshape(88 * 128)
    if fast:
        gs = lax.dynamic_slice(vec, (me * small_params.shape[0],), small_params.shape)
        done = adam_call(gu, gwp, gs[None], activations, dx, state)
        return (
            (done[0].reshape(1, LEN, D), done[1].reshape(1, LEN, FEAT))
            + tuple(done[2:18]) + tuple(x[0] for x in done[18:])
        )
    gu = gu.reshape(12, D, D).astype(F32)
    scatter = lambda g, dim: lax.psum_scatter(g, AXES, scatter_dimension=dim, tiled=True)
    ga = gu[0:3].reshape(3, D, 3, 256).transpose(2, 1, 0, 3).reshape(3, D, D)
    gf = gu[4:12].reshape(2, 4, D, D).transpose(0, 2, 1, 3).reshape(2, D, FF)
    sums = (
        scatter(gwp.reshape(FEAT, D).astype(F32), 0), scatter(ga, 1), scatter(gu[3], 0), scatter(gf, 1),
        scatter(vec[:VEC], 0)[None],
    )
    for k, g in enumerate(sums):
        new = (g,) + adam_rule(*state[3 * k : 3 * k + 3], g, RATE if k < 4 else SMALL_RATE)
        out.extend(x[0] if k == 4 else x for x in new)
    return tuple(out)


def solution(mesh):
    rows3, rows2, stacked, flat = (
        P(AXES, None, None), P(AXES, None), P(None, AXES, None), P(AXES),
    )
    return jax.shard_map(
        functools.partial(per_device, dict(mesh.shape) == dict(grp=4, dp=8)),
        mesh=mesh,
        in_specs=(
            rows3, rows2, P("grp", None), rows3, rows2, rows2, rows2, stacked, stacked, stacked,
            rows2, rows2, rows2, stacked, stacked, stacked, flat, flat, flat,
        ),
        out_specs=(rows3, rows3) + (rows2,) * 4 + (stacked,) * 4 + (rows2,) * 4 + (stacked,) * 4 + (flat,) * 4,
        check_vma=False,
    )
```

```python
import functools
import math

import jax
import jax.numpy as jnp
from jax import lax
from jax.experimental import pallas as pl
from jax.experimental.pallas import tpu as pltpu
from jax.sharding import PartitionSpec as P

D = 768
FF = 3072
FEAT = 512
HDIM = 64
HEADS = 12
PAIRS = HEADS // 2
LEN = 1024
STEP = 10
TILE = 256
NT = LEN // TILE
VEC = 11008

NORM_EPS = 1e-05
RATE = 0.08
SMALL_RATE = 0.3
BETA_ONE = 0.9
BETA_TWO = 0.999
ADAM_EPS = 1e-08
DECAY = 0.01

F32 = jnp.float32
BF16 = jnp.bfloat16
BIG = 2.0**100
VMEM_LIMIT = 63 << 20

WIDTHS = dict(
    g0=FEAT, b0=FEAT, bp=D, bq=D, bv=D, bo=D, g1=D, c1=D, b1=FF, b2=D, g2=D, c2=D
)
OFFSETS = {}
_at = 0
for _name, _width in WIDTHS.items():
    OFFSETS[_name] = _at
    _at += _width

KEY_RANGE = [
    (max(0, (i * TILE - 511) // TILE * TILE), min(LEN, -(-(i * TILE + TILE + 511) // TILE) * TILE))
    for i in range(NT)
]


def mm(a, b):
    return jnp.dot(a, b, preferred_element_type=F32)


def mm_nt(a, b):
    return lax.dot_general(a, b, (((1,), (1,)), ((), ())), preferred_element_type=F32)


def piece(ref, name, start=0, width=None):
    begin = OFFSETS[name] + start
    return ref[0:1, begin : begin + (width or WIDTHS[name])]


def put(ref, name, value, start=0):
    begin = OFFSETS[name] // 128 + start // 128
    for i in range(value.shape[1] // 128):
        ref[pl.ds(begin + i, 1), :] = value[:, 128 * i : 128 * i + 128]


def keep_row(width, limit, start=0):
    lane = lax.broadcasted_iota(jnp.int32, (1, width), 1) + start
    return (lane < limit).astype(F32)


def col_sum(value):
    return jnp.sum(value, 0, keepdims=True)


def row_sum(value):
    return jnp.sum(value, 1, keepdims=True)


def rows_of(t):
    return pl.ds(pl.multiple_of(t * TILE, TILE), TILE)


def lanes_of(p, width=128):
    return pl.ds(pl.multiple_of(p * width, width), width)


def gelu_both(u):
    half = jnp.exp(-0.5 * u * u)
    t = 1.0 / (1.0 + (0.3275911 * 0.7071067811865476) * jnp.abs(u))
    poly = 0.5 * 1.061405429
    for c in (-1.453152027, 1.421413741, -0.284496736, 0.254829592):
        poly = poly * t + 0.5 * c
    tail = poly * t * half
    cdf = jnp.where(u >= 0.0, 1.0 - tail, tail)
    return u * cdf, cdf + u * (half * 0.3989422804014327)


def fill_patterns(seg_ref, kpat, qpat):
    e0 = seg_ref[0, 0]
    e1 = e0 + seg_ref[0, 1]
    e2 = e1 + seg_ref[0, 2]

    @pl.loop(0, NT)
    def _(t):
        pos = lax.broadcasted_iota(jnp.int32, (TILE, 128), 0) + t * TILE
        lane = lax.broadcasted_iota(jnp.int32, (TILE, 128), 1)
        seg = (
            (pos >= e0).astype(jnp.int32)
            + (pos >= e1).astype(jnp.int32)
            + (pos >= e2).astype(jnp.int32)
        )
        for e in range(2):
            slot = lane - (64 if e == 0 else 0)
            valid = (slot >= 0) & (slot < 4)
            same = slot == seg
            kpat[e, rows_of(t), :] = jnp.where(same, 1.0, 0.0).astype(BF16)
            qpat[e, rows_of(t), :] = jnp.where(valid & (slot != seg), -BIG, 0.0).astype(BF16)


def half_mask(e):
    lane = lax.broadcasted_iota(jnp.int32, (1, 128), 1)
    return ((lane < 64) if e == 0 else (lane >= 64)).astype(F32).astype(BF16)


def norm0(feat, svec, rows):
    x = feat[rows, :].astype(F32)
    centred = x - row_sum(x) * (1.0 / FEAT)
    inv = lax.rsqrt(row_sum(centred * centred) * (1.0 / FEAT) + NORM_EPS)
    hat = centred * inv
    normed = (hat * piece(svec, "g0") + piece(svec, "b0")).astype(BF16)
    return hat, inv, normed


DIMS = ("y", "x", "z1", "z0")
CUBE = (2, 2, 2, 2)


def here():
    g = lax.axis_index("grp")
    d = lax.axis_index("dp")
    return dict(
        y=g // 2, x=g % 2, z1=d // 4, z0=(d // 2) % 2, c=d % 2,
    )


def partner(pos, dims):
    near = {k: (1 - v if k in dims else v) for k, v in pos.items()}
    return (near["y"] * 2 + near["x"], near["z1"] * 4 + near["z0"] * 2 + near["c"])


def cube(pos, full, other=()):
    return tuple(
        slice(None) if dim in full else (1 - pos[dim] if dim in other else pos[dim])
        for dim in DIMS
    )


def subsets(dims):
    return [(d,) for d in dims] + ([tuple(dims)] if len(dims) == 2 else [])


NEAR = [("c",), ("x",), ("y",), ("x", "y"), ("z0",), ("z1",), ("z1", "z0")]


def greet(pos):
    barrier = pltpu.get_barrier_semaphore()
    for dims in NEAR:
        pl.semaphore_signal(
            barrier, inc=1, device_id=partner(pos, dims), device_id_type=pl.DeviceIdType.MESH
        )
    pl.semaphore_wait(barrier, len(NEAR))


def remote(src, dst, send_sem, recv_sem, device):
    return pltpu.make_async_remote_copy(
        src_ref=src, dst_ref=dst, send_sem=send_sem, recv_sem=recv_sem,
        device_id=device, device_id_type=pl.DeviceIdType.MESH,
    )


def by_core(pos, action):
    for c in range(2):
        pl.when(pos["c"] == c)(functools.partial(action, c))


def half(c):
    return slice(384 * c, 384 * c + 384)


PARTS = [("p", 0), ("h", 0), ("h", 1), ("h", 2), ("h", 3), ("u", 4), ("u", 6), ("u", 8), ("u", 10)]
Z = ("z1", "z0")
SHORT = ((Z, ("x", "y")),) * 2
PLAIN = ((Z, ("x",), ("y",)), (Z, ("y",), ("x",)))
ROUTES = [SHORT, SHORT] + [PLAIN] * 7


class Gather:
    def __init__(self, pos, wg, wp, stage, stage_p, send, recv):
        self.pos, self.wg, self.wp = pos, wg, wp
        self.stage, self.stage_p = stage, stage_p
        self.send, self.recv = send, recv

    def view(self, i, c, index):
        kind, u = PARTS[i]
        if kind == "p":
            return self.wp.at[index + (slice(None), half(c))]
        if kind == "h":
            return self.wg.at[(u,) + index + (slice(None), half(c))]
        return self.wg.at[(u + c,) + index]

    def staged(self, i, c, rows):
        kind, u = PARTS[i]
        if kind == "p":
            return self.stage_p.at[rows, half(c)]
        if kind == "h":
            return self.stage.at[u, rows, half(c)]
        return self.stage.at[u + c, rows, :]

    def swap(self, i, c):
        own = pl.ds(16 * c, 16) if PARTS[i][0] == "p" else pl.ds(24 * c, 24)
        view = self.staged(i, 1 - c, own)
        return remote(view, view, self.send.at[i, 10], self.recv.at[i, 10], partner(self.pos, ("c",)))

    def hops(self, i, s, c):
        route = ROUTES[i][c]
        first = sum(len(subsets(dims)) for dims in route[:s])
        view = self.view(i, c, cube(self.pos, sum(route[:s], ())))
        return [
            remote(view, view, self.send.at[i, first + n], self.recv.at[i, first + n], partner(self.pos, dims))
            for n, dims in enumerate(subsets(route[s]))
        ]

    def gives(self, i, late, c):
        route = ROUTES[i][c]
        full = sum(route[:-1], ())
        ways = subsets(route[-1]) if late else [()]
        views = [self.view(i, c, cube(self.pos, full, dims)) for dims in ways]
        return [
            remote(
                view, view, self.send.at[i, 6 + late + n], self.recv.at[i, 6 + late + n],
                partner(self.pos, ("c",)),
            )
            for n, view in enumerate(views)
        ]

    def begin(self, i):
        def action(c):
            other = pl.ds(16 * (1 - c), 16) if PARTS[i][0] == "p" else pl.ds(24 * (1 - c), 24)
            view = self.staged(i, c, other)
            remote(
                view, view, self.send.at[i, 10], self.recv.at[i, 10], partner(self.pos, ("c",))
            ).wait_recv()
            rows = slice(0, 32 if PARTS[i][0] == "p" else 48)
            block = self.view(i, c, cube(self.pos, ()))
            block[...] = self.staged(i, c, rows)[...].astype(BF16)
            for copy in self.hops(i, 0, c):
                copy.start()

        by_core(self.pos, action)

    def step(self, i, s):
        def action(c):
            last = len(ROUTES[i][c]) - 1
            for copy in self.hops(i, s, c):
                copy.wait_recv()
            if s < last:
                for copy in self.hops(i, s + 1, c):
                    copy.start()
            if s >= last - 1:
                for copy in self.gives(i, s - last + 1, c):
                    copy.start()

        by_core(self.pos, action)

    def need(self, i):
        def action(c):
            for late in range(2):
                for copy in self.gives(i, late, 1 - c):
                    copy.wait_recv()

        by_core(self.pos, action)

    def finish(self):
        def action(c):
            for i in range(len(PARTS)):
                self.swap(i, c).wait_send()
                for s in range(len(ROUTES[i][c])):
                    for copy in self.hops(i, s, c):
                        copy.wait_send()
                for late in range(2):
                    for copy in self.gives(i, late, c):
                        copy.wait_send()

        by_core(self.pos, action)


class VectorSum:
    PHASES = (("c",), ("x", "y"), Z)

    def __init__(self, pos, rows, held, got, send, recv):
        self.pos, self.rows, self.held, self.got, self.send, self.recv = pos, rows, held, got, send, recv

    def copies(self, s):
        first = sum(len(subsets(dims)) for dims in self.PHASES[:s])
        return [
            remote(
                self.held.at[s, self.rows], self.got.at[first + n, self.rows],
                self.send.at[first + n], self.recv.at[first + n], partner(self.pos, dims),
            )
            for n, dims in enumerate(subsets(self.PHASES[s]))
        ]

    def start(self, s=0):
        for copy in self.copies(s):
            copy.start()

    def step(self, s):
        first = sum(len(subsets(dims)) for dims in self.PHASES[:s])
        total = self.held[s, self.rows]
        for n, copy in enumerate(self.copies(s)):
            copy.wait_recv()
            total = total + self.got[first + n, self.rows]
        self.held[s + 1, self.rows] = total
        if s < 2:
            self.start(s + 1)

    def finish(self):
        for s in range(3):
            for copy in self.copies(s):
                copy.wait_send()


def square(ref, u):
    return ref[u].reshape(D, D)


def forward_kernel(
    fast,
    *refs,
):
    refs = list(refs)
    take = lambda n: [refs.pop(0) for _ in range(n)]
    seg_ref, cfg_ref, feat_hbm, cot_hbm = take(4)
    if fast:
        own_p, own_a, own_o, own_f, own_s = take(5)
        wg_out, wp_out, svec = None, None, None
    else:
        wg_hbm, wp_hbm, svec = take(3)
    (
        act_out, hlt_out, qkv_out, kt_out, mixed_out, mixedt_out, xh1_out, inv1_out, flt_out,
        active_out, gp_out, d2_out, dg_out, dgt_out, lse_out, sg_out,
    ) = take(16)
    if fast:
        wg_out, wp_out, svec = take(3)
    (
        feat, cot, wg, wp, hid, hl, hlt, qkv, kt, vt, mixed, mixedt, xh1, fl, flt, active, gp, dg, dgt,
        kpat, qpat, sem_in, sem_out,
    ) = take(23)
    if fast:
        raw_p, raw_a, raw_o, raw_f, stage, stage_p, sem_raw, g_send, g_recv, sv_held, sv_got, v_send, v_recv = take(13)
    act = hl
    outs = []

    def load(i, src, dst):
        copy = pltpu.make_async_copy(src, dst, sem_in.at[i])
        copy.start()
        return copy

    def save(src, dst, part=None):
        i = len(outs)
        pick = lambda ref: ref if part is None else ref.at[part]
        make = lambda: pltpu.make_async_copy(pick(src), pick(dst), sem_out.at[i])
        make().start()
        outs.append(make)

    def need(i):
        kind, u = PARTS[i]
        if fast:
            gather.need(i)
            if kind == "p":
                save(wp, wp_out)
            elif kind == "h":
                save(wg, wg_out, u)
            else:
                save(wg, wg_out, pl.ds(u, 2))
        elif kind == "p":
            c_wp.wait()
        else:
            for v in range(u, u + (2 if kind == "u" else 1)):
                c_w[v].wait()

    def run(*steps):
        if fast:
            for i, s in steps:
                if i == "v":
                    vector.step(s)
                elif s < 0:
                    gather.begin(i)
                else:
                    gather.step(i, s)

    width = cfg_ref[0, 0]
    count = 1.0 / width.astype(F32)
    c_feat = load(0, feat_hbm, feat)
    if fast:
        pos = here()
        raws = [
            pltpu.make_async_copy(src, dst, sem_raw.at[i])
            for i, (src, dst) in enumerate(
                [(own_p, raw_p), (own_a, raw_a), (own_o, raw_o), (own_f, raw_f), (own_s, sv_held.at[0])]
            )
        ]
        for copy in raws:
            copy.start()
        gather = Gather(pos, wg, wp, stage, stage_p, g_send, g_recv)
        vector = VectorSum(pos, slice(0, 88), sv_held, sv_got, v_send, v_recv)
        for copy in raws:
            copy.wait()

        def arrange(c):
            rows = slice(24 * c, 24 * c + 24)
            stage_p[16 * c : 16 * c + 16, :] = raw_p[...]
            for j in range(3):
                for i in range(3):
                    stage[j, rows, 256 * i : 256 * i + 256] = raw_a[i, :, 256 * j : 256 * j + 256]
            stage[3, rows, :] = raw_o[...]
            for i in range(2):
                for q in range(4):
                    stage[4 + 4 * i + q, rows, :] = raw_f[i, :, D * q : D * q + D]

        by_core(pos, arrange)
        greet(pos)
        by_core(pos, lambda c: gather.swap(0, c).start())
        vector.start(0)
        for i in range(1, len(PARTS)):
            by_core(pos, lambda c, i=i: gather.swap(i, c).start())
        run((0, -1), (1, -1))
    else:
        c_wp = load(1, wp_hbm, wp)
        c_w = [load(2 + u, wg_hbm.at[u], wg.at[u]) for u in range(12)]
    c_cot = load(14, cot_hbm, cot)
    fill_patterns(seg_ref, kpat, qpat)
    run(("v", 0), (0, 0), ("v", 1), (2, -1), (1, 0), (3, -1), ("v", 2), (0, 1))
    if fast:
        for i in range(VEC // 128):
            svec[0:1, 128 * i : 128 * i + 128] = sv_held[3, i : i + 1, :]
    c_feat.wait()
    need(0)

    @pl.loop(0, NT)
    def _(t):
        rows = rows_of(t)
        normed = norm0(feat, svec, rows)[2]
        h = (mm(normed, wp[...].reshape(FEAT, D)) + piece(svec, "bp")) * keep_row(D, width)
        hid[rows, :] = h
        low = h.astype(BF16)
        hl[rows, :] = low
        hlt[:, rows] = low.T

    save(hlt, hlt_out)
    run((2, 0), (1, 1), (3, 0), (4, -1), (5, -1))
    need(1)

    slots = [
        [[], [(2, 1), (3, 1)]],
        [[(4, 0), (6, -1)], [(5, 0), (7, -1), (4, 1), (2, 2)]],
        [[], [(6, 0), (8, -1)]],
        [[(4, 2), (5, 1), (7, 0)], []],
        [[], [(6, 1), (8, 0)]],
        [[(7, 1)], [(5, 2)]],
    ]

    def at_slot(p, e):
        if fast:
            for i in range(PAIRS):
                if slots[i][e]:

                    @pl.when(p == i)
                    def _(i=i):
                        run(*slots[i][e])

    @pl.loop(0, PAIRS)
    def _(p):
        for j in range(3):

            @pl.when(p == 2 * j)
            def _(j=j):
                if j:
                    need(1 + j)

        @pl.when(lax.rem(p, 2) == 0)
        def _():
            j = lax.div(p, 2)
            group = lanes_of(j, 256)

            @pl.loop(0, NT)
            def _(t):
                rows = rows_of(t)
                keep = keep_row(256, cfg_ref[0, 1] * HDIM - j * 256)
                o = mm(hl[rows, :], square(wg, j))
                bias = lambda name: svec[0:1, pl.ds(pl.multiple_of(OFFSETS[name] + j * 256, 128), 256)]
                qkv[0, rows, group] = ((o[:, 0:256] + bias("bq")) * keep).astype(BF16)
                k = (o[:, 256:512] * keep).astype(BF16)
                qkv[1, rows, group] = k
                v = ((o[:, 512:768] + bias("bv")) * keep).astype(BF16)
                qkv[2, rows, group] = v
                down = pl.ds(pl.multiple_of(j * 256, 256), 256)
                kt[down, rows] = k.T
                vt[down, rows] = v.T

        if fast:

            @pl.when(p == 2)
            def _():
                run((3, 2))

        lanes = lanes_of(p)
        for e in range(2):
            kaug = qkv[1, :, lanes] * half_mask(e) + kpat[e]
            head_rows = pl.ds(pl.multiple_of(p * 128 + 64 * e, 64), 64)
            for b in range(NT):
                lo, hi = KEY_RANGE[b]
                cols = slice(b * TILE, (b + 1) * TILE)
                qaug = qkv[0, cols, lanes] * (half_mask(e) * 0.125) + qpat[e, cols, :]
                st = mm_nt(kaug[lo:hi], qaug)
                peak = jnp.max(st, 0, keepdims=True)
                power = jnp.exp(st - peak)
                total = col_sum(power)
                ot = mm(vt[head_rows, lo:hi], power.astype(BF16))
                mixedt[head_rows, cols] = (ot * (1.0 / total)).astype(BF16)
                lse_out[pl.ds(2 * p + e, 1), cols] = peak + jnp.log(total)
            at_slot(p, e)

    save(qkv, qkv_out)
    save(kt, kt_out)
    save(mixedt, mixedt_out)
    need(4)

    @pl.loop(0, NT)
    def _(t):
        rows = rows_of(t)
        keep = keep_row(D, width)
        mix = mixedt[:, rows].T
        mixed[rows, :] = mix
        z = hid[rows, :] + (mm(mix, square(wg, 3)) + piece(svec, "bo")) * keep
        centred = (z - row_sum(z * keep) * count) * keep
        inv = lax.rsqrt(row_sum(centred * centred) * count + NORM_EPS)
        hat = centred * inv
        first = (hat * piece(svec, "g1") + piece(svec, "c1")) * keep
        xh1[rows, :] = hat.astype(BF16)
        inv1_out[rows, :] = jnp.broadcast_to(inv, (TILE, 128))
        hid[rows, :] = first + piece(svec, "b2") * keep
        low = first.astype(BF16)
        fl[rows, :] = low
        flt[:, rows] = low.T

    save(mixed, mixed_out)
    save(xh1, xh1_out)
    save(flt, flt_out)
    need(5)

    def up(q):
        @pl.loop(0, NT)
        def _(t):
            rows = rows_of(t)
            u = (mm(fl[rows, :], square(wg, 4 + q)) + piece(svec, "b1", q * D, D)) * keep_row(
                D, cfg_ref[0, 2], q * D
            )
            g, slope = gelu_both(u)
            active[q, rows, :] = g.astype(BF16)
            gp[q, rows, :] = slope.astype(BF16)

        save(active, active_out, q)
        save(gp, gp_out, q)

    def down(q):
        @pl.loop(0, NT)
        def _(t):
            rows = rows_of(t)
            hid[rows, :] += mm_nt(active[q, rows, :], square(wg, 8 + q)) * keep_row(D, width)

    up(0)
    run((8, 1), (6, 2))
    up(1)
    need(6)
    up(2)
    run((7, 2))
    up(3)
    need(7)
    down(0)
    down(1)
    run((8, 2))
    need(8)
    down(2)
    down(3)
    c_cot.wait()
    zero = jnp.zeros((1, D), F32)

    def last(t, sums):
        gain_sum, shift_sum, bias_sum = sums
        rows = rows_of(t)
        keep = keep_row(D, width)
        z = hid[rows, :]
        centred = (z - row_sum(z * keep) * count) * keep
        inv = lax.rsqrt(row_sum(centred * centred) * count + NORM_EPS)
        hat = centred * inv
        gain = piece(svec, "g2")
        act[rows, :] = ((hat * gain + piece(svec, "c2")) * keep).astype(BF16)
        g = cot[rows, :].astype(F32) * keep
        gain_sum = gain_sum + col_sum(g * hat)
        shift_sum = shift_sum + col_sum(g)
        a = g * gain
        d2 = inv * (a - keep * (row_sum(a) * count) - hat * (row_sum(a * hat) * count))
        hid[rows, :] = d2
        low = d2.astype(BF16)
        dg[rows, :] = low
        dgt[:, rows] = low.T
        return gain_sum, shift_sum, bias_sum + col_sum(low.astype(F32))

    gain_sum, shift_sum, bias_sum = lax.fori_loop(0, NT, last, (zero, zero, zero))
    sg_out[...] = jnp.zeros((88, 128), F32)
    put(sg_out, "g2", gain_sum)
    put(sg_out, "c2", shift_sum)
    put(sg_out, "b2", bias_sum)
    save(act, act_out)
    save(hid, d2_out)
    save(dg, dg_out)
    save(dgt, dgt_out)
    if fast:
        gather.finish()
        vector.finish()
    for make in outs:
        make().wait()


R_PARTS = [("u", 8), ("u", 4), ("u", 10), ("u", 6), ("h", 3), ("h", 0), ("h", 1), ("h", 2), ("p", 0)]
R_PLAIN = ((("x",), ("y",), Z), (("y",), ("x",), Z))
R_SHORT = ((("x", "y"), Z),) * 2
R_ROUTES = [R_PLAIN] * 7 + [R_SHORT] * 2


class Scatter:
    def __init__(self, pos, acc, got, given, first, fin, gout, goutp, send, recv, local, credit):
        self.pos, self.acc, self.got, self.given, self.first = pos, acc, got, given, first
        self.fin, self.gout, self.goutp = fin, gout, goutp
        self.send, self.recv, self.local, self.credit = send, recv, local, credit

    def trim(self, i):
        kind = R_PARTS[i][0]
        if kind == "u":
            return ()
        return (slice(0, 32 if kind == "p" else 48), slice(0, 384))

    def held(self, bufs, i, index):
        kind = R_PARTS[i][0]
        if kind == "p":
            return bufs[2].at[index]
        if kind == "h":
            return bufs[1].at[(i - 4,) + index]
        return bufs[0].at[(i,) + index]

    def slot(self, buf, i):
        full = (slice(None),) * 4
        return buf.at[(i % 2,) + full + self.trim(i)]

    def hand(self, i):
        return remote(
            self.slot(self.given, i), self.slot(self.first, i), self.send.at[i, 6], self.recv.at[i, 6],
            partner(self.pos, ("c",)),
        )

    def hops(self, i, s, c):
        route = R_ROUTES[i][c]
        first = sum(len(subsets(dims)) for dims in route[:s])
        rest = sum(route[s + 1 :], ())
        dst = self.held(self.got, i, cube(self.pos, rest, sum(route[: s + 1], ())))
        return [
            remote(
                self.held(self.acc, i, cube(self.pos, rest, dims)), dst,
                self.send.at[i, first + n], self.recv.at[i, first + n], partner(self.pos, dims),
            )
            for n, dims in enumerate(subsets(route[s]))
        ]

    def came(self, i, s, c):
        route = R_ROUTES[i][c]
        rest = sum(route[s + 1 :], ())
        before = sum(route[:s], ())
        return [
            self.held(self.got, i, cube(self.pos, rest, before + tuple(d for d in route[s] if d not in dims)))
            for dims in subsets(route[s])
        ]

    def offer(self, i):
        if i >= 2:
            pl.semaphore_wait(self.credit, 1)
        self.hand(i).start()

    def reuse(self, i):
        if i >= 2:
            self.hand(i - 2).wait_send()

    def begin(self, i):
        self.hand(i).wait_recv()
        mine = self.held(self.acc, i, (slice(None),) * 4)
        mine[...] = mine[...] + self.slot(self.first, i)[...]
        if i < len(R_PARTS) - 2:
            pl.semaphore_signal(
                self.credit, inc=1, device_id=partner(self.pos, ("c",)),
                device_id_type=pl.DeviceIdType.MESH,
            )

        def action(c):
            for copy in self.hops(i, 0, c):
                copy.start()

        by_core(self.pos, action)

    def ends(self, i, c, own):
        kind, u = R_PARTS[i]
        rows = 16 if kind == "p" else 24
        fin = self.held(self.fin, i, ())
        if kind == "p":
            dst = self.goutp.at[:, half(c)]
        elif kind == "h":
            dst = self.gout.at[u, :, half(c)]
        else:
            dst = self.gout.at[u + c]
        if own:
            return pltpu.make_async_copy(fin.at[pl.ds(rows * c, rows)], dst, self.local.at[i])
        return remote(
            fin.at[pl.ds(rows * (1 - c), rows)], dst, self.send.at[i, 7], self.recv.at[i, 7],
            partner(self.pos, ("c",)),
        )

    def step(self, i, s):
        def action(c):
            route = R_ROUTES[i][c]
            for copy in self.hops(i, s, c):
                copy.wait_recv()
            mine = self.held(self.acc, i, cube(self.pos, sum(route[s + 1 :], ())))
            total = mine[...].astype(F32)
            for came in self.came(i, s, c):
                total = total + came[...].astype(F32)
            if s < len(route) - 1:
                mine[...] = total.astype(BF16)
                for copy in self.hops(i, s + 1, c):
                    copy.start()
            else:
                self.held(self.fin, i, ())[...] = total
                for own in (True, False):
                    self.ends(i, c, own).start()

        by_core(self.pos, action)

    def finish(self):
        n = len(R_PARTS)
        for i in range(n - 2, n):
            self.hand(i).wait_send()

        def action(c):
            for i in range(n):
                for s in range(len(R_ROUTES[i][c])):
                    for copy in self.hops(i, s, c):
                        copy.wait_send()
                self.ends(i, c, True).wait()
                self.ends(i, c, False).wait_send()
                self.ends(i, 1 - c, False).wait_recv()

        by_core(self.pos, action)


def backward_kernel(fast, *refs):
    refs = list(refs)
    take = lambda n: [refs.pop(0) for _ in range(n)]
    seg_ref, cfg_ref, feat_hbm, wg_hbm, wp_hbm, svec = take(6)
    (
        hlt_hbm, qkv_hbm, kt_hbm, mixed_hbm, mixedt_hbm, xh1_hbm, inv1_hbm, flt_hbm,
        active_hbm, gp_hbm, d2_hbm, dg_hbm, dgt_hbm, lse, sg_in,
    ) = take(15)
    dx_out, gu_out, gwp_out, sg = take(4)
    (
        feat, wbuf, wp, pool, tr, kt, qkv, go, inv1, fg, dg, tg, delta, dqt, kpat, qpat,
        acc_u, acc_h, acc_p, given, sem_in, sem_q, sem_dx,
    ) = take(23)
    if fast:
        (
            got_u, got_h, got_p, first_in, fin_u, fin_h, fin_p, r_send, r_recv, r_local, credit,
            sv_held, sv_got, v_send, v_recv,
        ) = take(15)
        pos = here()
        core = pos["c"]
        small = sv_held.at[0]
        scatter = Scatter(
            pos, (acc_u, acc_h, acc_p), (got_u, got_h, got_p), given, first_in, (fin_u, fin_h, fin_p),
            gu_out, gwp_out, r_send, r_recv, r_local, credit,
        )
        late, early = (
            VectorSum(pos, rows, sv_held, sv_got, v_send.at[i], v_recv.at[i])
            for i, rows in enumerate((slice(0, 32), slice(32, 88)))
        )
    else:
        sem_out = take(1)[0]
        core = lax.axis_index("dp") % 2
        small = sg
        holder = Scatter(None, (acc_u, acc_h, acc_p), *[None] * 10)

    def load(i, src, dst):
        copy = pltpu.make_async_copy(src, dst, sem_in.at[i])
        copy.start()
        return copy

    def run(*steps):
        if fast:
            for i, s in steps:
                if i == "e":
                    early.step(s)
                elif i == "l":
                    late.step(s)
                elif s < 0:
                    scatter.begin(i)
                else:
                    scatter.step(i, s)

    def columns(h):
        return pl.ds(pl.multiple_of(384 * h, 128), 384)

    def plain_copy(i, mine):
        kind, u = R_PARTS[i]
        which = core if mine else 1 - core
        full = (slice(None),) * 4
        if mine:
            src = holder.held(holder.acc, i, full)
        else:
            src = given.at[(i % 2,) + full + holder.trim(i)]
        if kind == "p":
            dst = gwp_out.at[full + (slice(None), columns(which))]
        elif kind == "h":
            dst = gu_out.at[(u,) + full + (slice(None), columns(which))]
        else:
            dst = gu_out.at[u + which]
        return pltpu.make_async_copy(src, dst, sem_out.at[i, 1 if mine else 0])

    def make(i, mine, left, right):
        kind = R_PARTS[i][0]
        rows, width = (32, 384) if kind == "p" else (48, 384 if kind == "h" else D)
        if not mine:
            if fast:
                scatter.reuse(i)
            elif i >= 2:
                plain_copy(i - 2, False).wait()

        @pl.loop(0, 2)
        def _(y):
            span = pl.ds(pl.multiple_of(y * 8 * rows, 8 * rows), 8 * rows)
            value = mm(left[span, :], right[...]).astype(BF16).reshape(2, 2, 2, rows, width)
            if not mine:
                trim = (slice(0, rows), slice(0, width))
                given[(i % 2, y) + (slice(None),) * 3 + trim] = value
            elif kind == "p":
                acc_p[y] = value
            elif kind == "h":
                acc_h[i - 4, y] = value
            else:
                acc_u[i, y] = value

        if fast:
            if not mine:
                scatter.offer(i)
        else:
            plain_copy(i, mine).start()

    def quarter(k):
        s = k % 2
        q = 2 * (k // 2) + (core if k % 2 else 1 - core)
        pairs = [
            (active_hbm.at[q], pool.at[s]),
            (wg_hbm.at[8 + q], wbuf.at[s]),
            (gp_hbm.at[q], pool.at[2 + s]),
            (wg_hbm.at[4 + q], wbuf.at[2 + s]),
        ]
        return q, [
            pltpu.make_async_copy(src, dst, sem_q.at[s, i]) for i, (src, dst) in enumerate(pairs)
        ]

    dgt, flt, ig = tr.at[0], tr.at[1], pool.at[4]
    c_dgt = load(0, dgt_hbm, dgt)
    for copy in quarter(0)[1]:
        copy.start()
    c_dg = load(1, dg_hbm, dg)
    c_flt = load(2, flt_hbm, flt)
    c_d2 = load(3, d2_hbm, fg)
    for copy in quarter(1)[1]:
        copy.start()
    c_xh1 = load(4, xh1_hbm, go)
    c_inv1 = load(5, inv1_hbm, inv1)
    c_mixed = load(6, mixed_hbm, pool.at[5])
    c_qkv = load(9, qkv_hbm, qkv)
    c_kt = load(10, kt_hbm, kt)
    c_wp = load(15, wp_hbm, wp)
    c_feat = load(16, feat_hbm, feat)

    width = cfg_ref[0, 0]
    count = 1.0 / width.astype(F32)
    if fast:
        greet(pos)
    small[...] = sg_in[...]
    fill_patterns(seg_ref, kpat, qpat)
    c_dgt.wait()
    events = {
        (1, 0): [(0, -1)],
        (1, 2): [(1, -1)],
        (3, 0): [(2, -1), (0, 0)],
        (3, 2): [(3, -1), (1, 0)],
    }
    for k in range(4):
        s = k % 2
        mine = bool(k % 2)
        q, copies = quarter(k)
        at = lambda n: run(*events.get((k, n), []))
        copies[0].wait()
        make(2 * (k // 2), mine, dgt, pool.at[s])
        at(0)
        if k == 0:
            c_dg.wait()
        copies[1].wait()
        copies[2].wait()

        def inner(t, bias, q=q, s=s):
            rows = rows_of(t)
            low = (
                mm(dg[rows, :], square(wbuf, s))
                * pool[2 + s, rows, :].astype(F32)
                * keep_row(D, cfg_ref[0, 2] - q * D)
            ).astype(BF16)
            ig[rows, :] = low
            return bias + col_sum(low.astype(F32))

        put(small, "b1", lax.fori_loop(0, NT, inner, jnp.zeros((1, D), F32)), q * D)
        at(1)
        if k == 0:
            c_flt.wait()
            c_d2.wait()
        make(2 * (k // 2) + 1, mine, flt, ig)
        at(2)
        copies[3].wait()

        @pl.loop(0, NT)
        def _(t, s=s):
            rows = rows_of(t)
            fg[rows, :] += mm_nt(ig[rows, :], square(wbuf, 2 + s))

        at(3)
        if k < 2:
            for copy in quarter(k + 2)[1]:
                copy.start()
        if k == 2:
            c_wo = load(8, wg_hbm.at[3], wbuf.at[0])
            c_wa = [load(12, wg_hbm.at[0], wbuf.at[2])]

    mixedt, hlt, mixed = tr.at[0], tr.at[1], pool.at[5]
    c_mixedt = load(7, mixedt_hbm, mixedt)
    c_hlt = load(11, hlt_hbm, hlt)
    c_wa.append(load(13, wg_hbm.at[1], wbuf.at[1]))
    c_wa.append(load(14, wg_hbm.at[2], wbuf.at[3]))
    wa_slot = (2, 1, 3)
    for copy in (c_xh1, c_inv1, c_mixed, c_wo):
        copy.wait()
    zero = jnp.zeros((1, D), F32)

    def middle(t, sums):
        gain_sum, shift_sum, bias_sum = sums
        rows = rows_of(t)
        keep = keep_row(D, width)
        hat = go[rows, :].astype(F32)
        g = fg[rows, :] * keep
        gain_sum = gain_sum + col_sum(g * hat)
        shift_sum = shift_sum + col_sum(g)
        a = g * piece(svec, "g1")
        d1 = inv1[rows, 0:1] * (a - keep * (row_sum(a) * count) - hat * (row_sum(a * hat) * count))
        fg[rows, :] = d1
        low = d1.astype(BF16)
        dg[rows, :] = low
        mg = mm_nt(low, square(wbuf, 0)).astype(BF16)
        go[rows, :] = mg
        product = mg.astype(F32) * mixed[rows, :].astype(F32)
        high = product.astype(BF16)
        rest = (product - high.astype(F32)).astype(BF16)
        lane = lax.broadcasted_iota(jnp.int32, (16, D), 1)
        head = lax.broadcasted_iota(jnp.int32, (16, D), 0)
        pick = ((lane >= head * HDIM) & (lane < head * HDIM + HDIM)).astype(F32).astype(BF16)
        delta[:, rows] = mm_nt(pick, high) + mm_nt(pick, rest)
        return gain_sum, shift_sum, bias_sum + col_sum(low.astype(F32))

    gain_sum, shift_sum, bias_sum = lax.fori_loop(0, NT, middle, (zero, zero, zero))
    put(small, "g1", gain_sum)
    put(small, "c1", shift_sum)
    put(small, "bo", bias_sum)
    if fast:
        early.start()
    run((0, 1))
    c_mixedt.wait()
    make(4, False, mixedt, dg.at[:, columns(1 - core)])
    make(4, True, mixedt, dg.at[:, columns(core)])

    c_qkv.wait()
    c_kt.wait()
    c_hlt.wait()
    for copy in c_wa:
        copy.wait()
    slots = [
        [[], [(2, 0), (1, 1), (4, -1)], [("e", 0), (3, 0)], []],
        [[], [(5, -1), (1, 2), ("e", 2), (3, 1)], [], [(4, 1)]],
        [[], [(6, -1), (3, 2), (4, 2)], [], [(5, 1)]],
    ]
    after_loop = [[(0, 2), ("e", 1)], [], []]
    after_make = [[(4, 0)], [(5, 0), (2, 2)], [(6, 0)]]
    after_back = [[(2, 1)], [], [(7, -1)]]

    def chunk(n):
        return n // 3, slice(256 * (n % 3), 256 * (n % 3) + 256)

    for j in range(3):

        def at_slot(pp, e, j=j):
            if fast:
                for i in range(2):
                    steps = slots[j][2 * i + e]
                    if steps:

                        @pl.when(pp == i)
                        def _(steps=steps):
                            run(*steps)

        @pl.loop(0, 2)
        def _(pp, j=j):
            p = j * 2 + pp
            lanes = lanes_of(p)
            for e in range(2):
                at_slot(pp, e)
                kaug = qkv[1, :, lanes] * half_mask(e) + kpat[e]
                head_rows = pl.ds(pl.multiple_of(p * 128 + 64 * e, 64), 64)
                for b in range(NT):
                    lo, hi = KEY_RANGE[b]
                    cols = slice(b * TILE, (b + 1) * TILE)
                    qaug = qkv[0, cols, lanes] * (half_mask(e) * 0.125) + qpat[e, cols, :]
                    st = mm_nt(kaug[lo:hi], qaug)
                    weights = jnp.exp(st - lse[pl.ds(2 * p + e, 1), cols])
                    n, span = chunk(4 * e + b)
                    pool[n, lo:hi, span] = weights.astype(BF16)
                    goe = go[cols, lanes] * half_mask(e)
                    dp = mm_nt(qkv[2, lo:hi, lanes], goe)
                    ds = (weights * (dp - delta[pl.ds(2 * p + e, 1), cols])).astype(BF16)
                    n, span = chunk(8 + 4 * e + b)
                    pool[n, lo:hi, span] = ds
                    dqt[64 * e : 64 * e + 64, cols] = mm(kt[head_rows, lo:hi], ds)
            keep = keep_row(128, cfg_ref[0, 1] * HDIM - p * 128)
            for t in range(NT):
                rows = slice(t * TILE, (t + 1) * TILE)
                dk = jnp.zeros((TILE, 128), F32)
                dv = jnp.zeros((TILE, 128), F32)
                for b in range(NT):
                    if not KEY_RANGE[b][0] <= t * TILE < KEY_RANGE[b][1]:
                        continue
                    cols = slice(b * TILE, (b + 1) * TILE)
                    for e in range(2):
                        n, span = chunk(8 + 4 * e + b)
                        dk = dk + mm(pool[n, rows, span], qkv[0, cols, lanes] * half_mask(e))
                        n, span = chunk(4 * e + b)
                        dv = dv + mm(pool[n, rows, span], go[cols, lanes] * half_mask(e))
                dq = dqt[:, rows].T
                for i, value in enumerate((dq * (keep * 0.125), dk * (keep * 0.125), dv * keep)):
                    tg[rows, pl.ds(pl.multiple_of(256 * i + pp * 128, 128), 128)] = value.astype(BF16)

        run(*after_loop[j])
        make(5 + j, False, hlt, tg.at[:, columns(1 - core)])
        make(5 + j, True, hlt, tg.at[:, columns(core)])
        run(*after_make[j])

        def back(t, bias, j=j):
            rows = rows_of(t)
            fg[rows, :] += mm_nt(tg[rows, :], square(wbuf, wa_slot[j]))
            return bias + col_sum(tg[rows, :].astype(F32))

        bias = lax.fori_loop(0, NT, back, zero)
        put(small, "bq", bias[:, 0:256], 256 * j)
        put(small, "bv", bias[:, 512:768], 256 * j)
        run(*after_back[j])

    c_wp.wait()
    c_feat.wait()
    zero_feat = jnp.zeros((1, FEAT), F32)
    nrmt = tr.at[0]

    def first(t, bias_sum):
        rows = rows_of(t)
        nrmt[0:FEAT, rows] = norm0(feat, svec, rows)[2].T
        low = (fg[rows, :] * keep_row(D, width)).astype(BF16)
        dg[rows, :] = low
        return bias_sum + col_sum(low.astype(F32))

    put(small, "bp", lax.fori_loop(0, NT, first, zero))
    run((5, 2))
    make(8, False, nrmt, dg.at[:, columns(1 - core)])
    make(8, True, nrmt, dg.at[:, columns(core)])

    def second(t, sums):
        gain_sum, shift_sum = sums
        rows = rows_of(t)
        hat, inv, _ = norm0(feat, svec, rows)
        g = mm_nt(dg[rows, :], wp[...].reshape(FEAT, D))
        gain_sum = gain_sum + col_sum(g * hat)
        shift_sum = shift_sum + col_sum(g)
        a = g * piece(svec, "g0")
        dx = inv * (a - row_sum(a) * (1.0 / FEAT) - hat * (row_sum(a * hat) * (1.0 / FEAT)))
        fg[rows, 0:FEAT] = 0.1 * dx
        return gain_sum, shift_sum

    gain_sum, shift_sum = lax.fori_loop(0, NT, second, (zero_feat, zero_feat))
    put(small, "g0", gain_sum)
    put(small, "b0", shift_sum)
    c_dx = pltpu.make_async_copy(fg.at[:, 0:FEAT], dx_out, sem_dx)
    c_dx.start()
    if fast:
        late.start()
        run((8, -1), (6, 1), (7, 0), ("l", 0), (8, 0), (6, 2), ("l", 1), (7, 1), (8, 1), ("l", 2))
        sg[...] = sv_held[3]
        early.finish()
        late.finish()
        scatter.finish()
    else:
        for i in range(len(R_PARTS)):
            plain_copy(i, True).wait()
        for i in range(len(R_PARTS) - 2, len(R_PARTS)):
            plain_copy(i, False).wait()
    c_dx.wait()


def adam_rule(weight, moment, square_in, grad, rate):
    moment_new = BETA_ONE * moment + (1.0 - BETA_ONE) * grad
    square_new = BETA_TWO * square_in + (1.0 - BETA_TWO) * grad * grad
    fix_one = 1.0 - BETA_ONE**STEP
    fix_two = 1.0 - BETA_TWO**STEP
    direction = moment_new / fix_one / (jnp.sqrt(square_new / fix_two) + ADAM_EPS)
    return (moment_new, square_new, weight - rate * (direction + DECAY * weight))


def adam_kernel(*refs):
    gu_hbm, gp_hbm, act_hbm, dx_hbm = refs[0:4]
    ins, act_out, dx_out, outs = refs[4:16], refs[16], refs[17], refs[18:34]
    gu, gp, act, dx = refs[34:38]
    held, new = refs[38:50], refs[50:62]
    sem_in, sem_out = refs[62:]
    sources = (gu_hbm,) + tuple(ins[9:12]) + (act_hbm, dx_hbm, gp_hbm) + tuple(ins[0:9])
    places = (gu,) + tuple(held[9:12]) + (act, dx, gp) + tuple(held[0:9])
    loads = [
        pltpu.make_async_copy(src, dst, sem_in.at[i]) for i, (src, dst) in enumerate(zip(sources, places))
    ]
    for copy in loads:
        copy.start()
    stores = []

    def store(src, dst):
        copy = pltpu.make_async_copy(src, dst, sem_out.at[len(stores)])
        copy.start()
        stores.append(copy)

    def update(k, pieces):
        w, m, v = held[3 * k : 3 * k + 3]
        for index, grad in pieces:
            done = adam_rule(w[index], m[index], v[index], grad(), RATE)
            for ref, value in zip(new[3 * k : 3 * k + 3], done):
                ref[index] = value
            m[index] = grad()
        for src, dst in zip((m,) + tuple(new[3 * k : 3 * k + 3]), outs[4 * k : 4 * k + 4]):
            store(src, dst)

    everything = (slice(None), slice(None))
    for copy in loads[0:4]:
        copy.wait()
    update(
        3,
        [
            ((i, slice(None), slice(D * q, D * q + D)), lambda i=i, q=q: gu[4 + 4 * i + q])
            for i in range(2) for q in range(4)
        ],
    )
    for copy in loads[4:6]:
        copy.wait()
    store(act, act_out)
    store(dx, dx_out)
    for copy in loads[6:16]:
        copy.wait()
    update(
        1,
        [
            ((i, slice(None), slice(256 * j, 256 * j + 256)), lambda i=i, j=j: gu[j, :, 256 * i : 256 * i + 256])
            for i in range(3) for j in range(3)
        ],
    )
    update(2, [(everything, lambda: gu[3])])
    update(0, [(everything, lambda: gp[...])])
    for copy in stores:
        copy.wait()


def adam_call(gu, gp, act, dx, state):
    shape = jax.ShapeDtypeStruct
    f32 = lambda s: pltpu.VMEM(s, F32)
    outs = [shape((LEN, D), BF16), shape((LEN, FEAT), F32)]
    outs += [shape(state[3 * k].shape, F32) for k in range(4) for _ in range(4)]
    scratch = [f32(gu.shape), f32(gp.shape), pltpu.VMEM((LEN, D), BF16), f32((LEN, FEAT))]
    scratch += [f32(x.shape) for x in state] * 2
    scratch += [pltpu.SemaphoreType.DMA((16,)), pltpu.SemaphoreType.DMA((18,))]
    return pl.pallas_call(
        adam_kernel,
        out_shape=outs,
        in_specs=[any_spec()] * 16,
        out_specs=[any_spec()] * 18,
        scratch_shapes=scratch,
        compiler_params=pltpu.CompilerParams(vmem_limit_bytes=VMEM_LIMIT),
        name="adam",
    )(gu, gp, act, dx, *state)


def any_spec():
    return pl.BlockSpec(memory_space=pl.ANY)


def vmem_spec():
    return pl.BlockSpec(memory_space=pltpu.VMEM)


def smem_spec():
    return pl.BlockSpec(memory_space=pltpu.SMEM)


def forward_call(fast, seg, cfg, feat, cot, weights):
    shape = jax.ShapeDtypeStruct
    outs = [
        (shape((LEN, D), BF16), any_spec()),
        (shape((D, LEN), BF16), any_spec()),
        (shape((3, LEN, D), BF16), any_spec()),
        (shape((D, LEN), BF16), any_spec()),
        (shape((LEN, D), BF16), any_spec()),
        (shape((D, LEN), BF16), any_spec()),
        (shape((LEN, D), BF16), any_spec()),
        (shape((LEN, 128), F32), vmem_spec()),
        (shape((D, LEN), BF16), any_spec()),
        (shape((4, LEN, D), BF16), any_spec()),
        (shape((4, LEN, D), BF16), any_spec()),
        (shape((LEN, D), F32), any_spec()),
        (shape((LEN, D), BF16), any_spec()),
        (shape((D, LEN), BF16), any_spec()),
        (shape((16, LEN), F32), vmem_spec()),
        (shape((88, 128), F32), vmem_spec()),
    ]
    if fast:
        outs += [
            (shape((12,) + CUBE + (48, D), BF16), any_spec()),
            (shape(CUBE + (32, D), BF16), any_spec()),
            (shape((1, VEC), F32), vmem_spec()),
        ]
    bf = lambda *s: pltpu.VMEM(s, BF16)
    f32 = lambda *s: pltpu.VMEM(s, F32)
    dma = lambda *s: pltpu.SemaphoreType.DMA(s)
    scratch = [
        bf(LEN, FEAT), bf(LEN, D), bf(12, *CUBE, 48, D), bf(*CUBE, 32, D), f32(LEN, D),
        bf(LEN, D), bf(D, LEN), bf(3, LEN, D), bf(D, LEN), bf(D, LEN), bf(LEN, D), bf(D, LEN),
        bf(LEN, D), bf(LEN, D), bf(D, LEN), bf(4, LEN, D), bf(4, LEN, D), bf(LEN, D), bf(D, LEN),
        bf(2, LEN, 128), bf(2, LEN, 128), dma(15), dma(32),
    ]
    if fast:
        scratch += [
            f32(16, D), f32(3, 24, D), f32(24, D), f32(2, 24, FF), f32(12, 48, D), f32(32, D), dma(5),
            dma(len(PARTS), 11), dma(len(PARTS), 11), f32(4, 88, 128), f32(7, 88, 128), dma(7), dma(7),
        ]
        specs = [any_spec()] * len(weights)
        params = dict(collective_id=0, has_side_effects=True)
    else:
        specs = [any_spec()] * 2 + [vmem_spec()]
        params = {}
    return pl.pallas_call(
        functools.partial(forward_kernel, fast),
        out_shape=[o[0] for o in outs],
        in_specs=[smem_spec(), smem_spec()] + [any_spec()] * 2 + specs,
        out_specs=[o[1] for o in outs],
        scratch_shapes=scratch,
        compiler_params=pltpu.CompilerParams(vmem_limit_bytes=VMEM_LIMIT, **params),
        name="forward",
    )(seg, cfg, feat, cot, *weights)


def backward_call(fast, seg, cfg, feat, wg, wp, svec, saved):
    shape = jax.ShapeDtypeStruct
    bf = lambda *s: pltpu.VMEM(s, BF16)
    f32 = lambda *s: pltpu.VMEM(s, F32)
    dma = lambda *s: pltpu.SemaphoreType.DMA(s)
    n = len(R_PARTS)
    scratch = [
        bf(LEN, FEAT), bf(4, *CUBE, 48, D), bf(*CUBE, 32, D), bf(6, LEN, D), bf(2, D, LEN), bf(D, LEN),
        bf(3, LEN, D), bf(LEN, D), f32(LEN, 128), f32(LEN, D), bf(LEN, D), bf(LEN, D), f32(16, LEN),
        f32(128, LEN), bf(2, LEN, 128), bf(2, LEN, 128),
        bf(4, *CUBE, 48, D), bf(4, *CUBE, 48, 384), bf(*CUBE, 32, 384), bf(2, *CUBE, 48, D),
        dma(17), dma(2, 4), pltpu.SemaphoreType.DMA,
    ]
    if fast:
        scratch += [
            bf(4, *CUBE, 48, D), bf(4, *CUBE, 48, 384), bf(*CUBE, 32, 384), bf(2, *CUBE, 48, D),
            f32(4, 48, D), f32(4, 48, 384), f32(32, 384), dma(n, 8), dma(n, 8), dma(n),
            pltpu.SemaphoreType.REGULAR, f32(4, 88, 128), f32(7, 88, 128), dma(2, 7), dma(2, 7),
        ]
        grads = [shape((12, 24, D), F32), shape((16, D), F32)]
        params = dict(collective_id=1, has_side_effects=True)
    else:
        scratch += [dma(n, 2)]
        grads = [shape((12,) + CUBE + (48, D), BF16), shape(CUBE + (32, D), BF16)]
        params = {}
    return pl.pallas_call(
        functools.partial(backward_kernel, fast),
        out_shape=[shape((LEN, FEAT), F32)] + grads + [shape((88, 128), F32)],
        in_specs=[smem_spec(), smem_spec()] + [any_spec()] * 3 + [vmem_spec()]
        + [any_spec()] * 13 + [vmem_spec()] * 2,
        out_specs=[any_spec()] * 3 + [vmem_spec()],
        scratch_shapes=scratch,
        compiler_params=pltpu.CompilerParams(vmem_limit_bytes=VMEM_LIMIT, **params),
        name="backward",
    )(seg, cfg, feat, wg, wp, svec, *saved)


AXES = ("grp", "dp")


def gathered(projection_weight, attention_weight, output_weight, feedforward_weight, small_params):
    gather = lambda w, axis: lax.all_gather(w.astype(BF16), AXES, axis=axis, tiled=True)
    wp = gather(projection_weight, 0)
    wa = gather(attention_weight, 1)
    wo = gather(output_weight, 0)
    wf = gather(feedforward_weight, 1)
    svec = gather(small_params, 0).astype(F32).reshape(1, VEC)
    return units(wp, wa, wo, wf) + (svec,)


def units(wp, wa, wo, wf):
    groups = wa.reshape(3, D, 3, 256).transpose(2, 1, 0, 3).reshape(3, D, D)
    quarters = wf.reshape(2, D, 4, D).transpose(0, 2, 1, 3).reshape(8, D, D)
    wg = jnp.concatenate([groups, wo[None], quarters], 0)
    return wg.reshape((12,) + CUBE + (48, D)), wp.reshape(CUBE + (32, D))


def layer(fast, features, lengths, config, cotangent, weights):
    feat = features.reshape(LEN, FEAT)
    cot = cotangent.reshape(LEN, D)
    saved = forward_call(fast, lengths, config, feat, cot, weights)
    activations = saved[0]
    wg, wp, svec = saved[16:] if fast else weights
    dx, gu, gwp, sg = backward_call(fast, lengths, config, feat, wg, wp, svec, saved[1:16])
    return activations, dx, gu, gwp, sg


def per_device(
    fast,
    features, segment_lengths, subnet_config, cotangent,
    projection_weight, projection_moment, projection_square,
    attention_weight, attention_moment, attention_square,
    output_weight, output_moment, output_square,
    feedforward_weight, feedforward_moment, feedforward_square,
    small_params, small_moment, small_square,
):
    weights = (projection_weight, attention_weight, output_weight, feedforward_weight)
    if fast:
        me = lax.axis_index(AXES)
        low = lax.reduce_precision(small_params, 8, 7)
        placed = lax.dynamic_update_slice(jnp.zeros((88 * 128,), F32), low, (me * low.shape[0],))
        weights = weights + (placed.reshape(88, 128),)
    else:
        weights = gathered(*weights, small_params)
    activations, dx, gu, gwp, sg = layer(
        fast, features, segment_lengths, subnet_config, cotangent, weights
    )
    state = (
        projection_weight, projection_moment, projection_square,
        attention_weight, attention_moment, attention_square,
        output_weight, output_moment, output_square,
        feedforward_weight, feedforward_moment, feedforward_square,
        small_params[None], small_moment[None], small_square[None],
    )
    out = [activations.reshape(1, LEN, D), dx.reshape(1, LEN, FEAT)]
    vec = sg.reshape(88 * 128)
    if fast:
        gs = lax.dynamic_slice(vec, (me * small_params.shape[0],), small_params.shape)
        done = adam_call(gu, gwp, activations, dx, state[:12])
        return (
            (done[0].reshape(1, LEN, D), done[1].reshape(1, LEN, FEAT))
            + tuple(done[2:18])
            + (gs,) + adam_rule(small_params, small_moment, small_square, gs, SMALL_RATE)
        )
    gu = gu.reshape(12, D, D).astype(F32)
    scatter = lambda g, dim: lax.psum_scatter(g, AXES, scatter_dimension=dim, tiled=True)
    ga = gu[0:3].reshape(3, D, 3, 256).transpose(2, 1, 0, 3).reshape(3, D, D)
    gf = gu[4:12].reshape(2, 4, D, D).transpose(0, 2, 1, 3).reshape(2, D, FF)
    sums = (
        scatter(gwp.reshape(FEAT, D).astype(F32), 0), scatter(ga, 1), scatter(gu[3], 0), scatter(gf, 1),
        scatter(vec[:VEC], 0)[None],
    )
    for k, g in enumerate(sums):
        new = (g,) + adam_rule(*state[3 * k : 3 * k + 3], g, RATE if k < 4 else SMALL_RATE)
        out.extend(x[0] if k == 4 else x for x in new)
    return tuple(out)


def solution(mesh):
    rows3, rows2, stacked, flat = (
        P(AXES, None, None), P(AXES, None), P(None, AXES, None), P(AXES),
    )
    return jax.shard_map(
        functools.partial(per_device, dict(mesh.shape) == dict(grp=4, dp=8)),
        mesh=mesh,
        in_specs=(
            rows3, rows2, P("grp", None), rows3, rows2, rows2, rows2, stacked, stacked, stacked,
            rows2, rows2, rows2, stacked, stacked, stacked, flat, flat, flat,
        ),
        out_specs=(rows3, rows3) + (rows2,) * 4 + (stacked,) * 4 + (rows2,) * 4 + (stacked,) * 4 + (flat,) * 4,
        check_vma=False,
    )
```

```python
import functools
import math

import jax
import jax.numpy as jnp
from jax import lax
from jax.experimental import pallas as pl
from jax.experimental.pallas import tpu as pltpu
from jax.sharding import PartitionSpec as P

D = 768
FF = 3072
FEAT = 512
HDIM = 64
HEADS = 12
PAIRS = HEADS // 2
LEN = 1024
STEP = 10
TILE = 256
NT = LEN // TILE
VEC = 11008

NORM_EPS = 1e-05
RATE = 0.08
SMALL_RATE = 0.3
BETA_ONE = 0.9
BETA_TWO = 0.999
ADAM_EPS = 1e-08
DECAY = 0.01

F32 = jnp.float32
BF16 = jnp.bfloat16
BIG = 2.0**100
VMEM_LIMIT = 63 << 20

WIDTHS = dict(
    g0=FEAT, b0=FEAT, bp=D, bq=D, bv=D, bo=D, g1=D, c1=D, b1=FF, b2=D, g2=D, c2=D
)
OFFSETS = {}
_at = 0
for _name, _width in WIDTHS.items():
    OFFSETS[_name] = _at
    _at += _width

KEY_RANGE = [
    (max(0, (i * TILE - 511) // TILE * TILE), min(LEN, -(-(i * TILE + TILE + 511) // TILE) * TILE))
    for i in range(NT)
]


def mm(a, b):
    return jnp.dot(a, b, preferred_element_type=F32)


def mm_nt(a, b):
    return lax.dot_general(a, b, (((1,), (1,)), ((), ())), preferred_element_type=F32)


def piece(ref, name, start=0, width=None):
    begin = OFFSETS[name] + start
    return ref[0:1, begin : begin + (width or WIDTHS[name])]


def put(ref, name, value, start=0):
    begin = OFFSETS[name] // 128 + start // 128
    for i in range(value.shape[1] // 128):
        ref[pl.ds(begin + i, 1), :] = value[:, 128 * i : 128 * i + 128]


def keep_row(width, limit, start=0):
    lane = lax.broadcasted_iota(jnp.int32, (1, width), 1) + start
    return (lane < limit).astype(F32)


def col_sum(value):
    return jnp.sum(value, 0, keepdims=True)


def row_sum(value):
    return jnp.sum(value, 1, keepdims=True)


def rows_of(t):
    return pl.ds(pl.multiple_of(t * TILE, TILE), TILE)


def span_of(t, size):
    return pl.ds(pl.multiple_of(t * size, size), size)


def lanes_of(p, width=128):
    return pl.ds(pl.multiple_of(p * width, width), width)


def gelu_both(u):
    half = jnp.exp(-0.5 * u * u)
    t = 1.0 / (1.0 + (0.3275911 * 0.7071067811865476) * jnp.abs(u))
    poly = 0.5 * 1.061405429
    for c in (-1.453152027, 1.421413741, -0.284496736, 0.254829592):
        poly = poly * t + 0.5 * c
    tail = poly * t * half
    cdf = jnp.where(u >= 0.0, 1.0 - tail, tail)
    return u * cdf, cdf + u * (half * 0.3989422804014327)


def fill_patterns(seg_ref, kpat, qpat):
    e0 = seg_ref[0, 0]
    e1 = e0 + seg_ref[0, 1]
    e2 = e1 + seg_ref[0, 2]

    @pl.loop(0, NT)
    def _(t):
        pos = lax.broadcasted_iota(jnp.int32, (TILE, 128), 0) + t * TILE
        lane = lax.broadcasted_iota(jnp.int32, (TILE, 128), 1)
        seg = (
            (pos >= e0).astype(jnp.int32)
            + (pos >= e1).astype(jnp.int32)
            + (pos >= e2).astype(jnp.int32)
        )
        for e in range(2):
            slot = lane - (64 if e == 0 else 0)
            valid = (slot >= 0) & (slot < 4)
            same = slot == seg
            kpat[e, rows_of(t), :] = jnp.where(same, 1.0, 0.0).astype(BF16)
            qpat[e, rows_of(t), :] = jnp.where(valid & (slot != seg), -BIG, 0.0).astype(BF16)


def half_mask(e):
    lane = lax.broadcasted_iota(jnp.int32, (1, 128), 1)
    return ((lane < 64) if e == 0 else (lane >= 64)).astype(F32).astype(BF16)


def norm0(feat, svec, rows):
    x = feat[rows, :].astype(F32)
    centred = x - row_sum(x) * (1.0 / FEAT)
    inv = lax.rsqrt(row_sum(centred * centred) * (1.0 / FEAT) + NORM_EPS)
    hat = centred * inv
    normed = (hat * piece(svec, "g0") + piece(svec, "b0")).astype(BF16)
    return hat, inv, normed


DIMS = ("y", "x", "z1", "z0")
CUBE = (2, 2, 2, 2)


def here():
    g = lax.axis_index("grp")
    d = lax.axis_index("dp")
    return dict(
        y=g // 2, x=g % 2, z1=d // 4, z0=(d // 2) % 2, c=d % 2,
    )


def partner(pos, dims):
    near = {k: (1 - v if k in dims else v) for k, v in pos.items()}
    return (near["y"] * 2 + near["x"], near["z1"] * 4 + near["z0"] * 2 + near["c"])


def cube(pos, full, other=()):
    return tuple(
        slice(None) if dim in full else (1 - pos[dim] if dim in other else pos[dim])
        for dim in DIMS
    )


def subsets(dims):
    return [(d,) for d in dims] + ([tuple(dims)] if len(dims) == 2 else [])


NEAR = [("c",), ("x",), ("y",), ("x", "y"), ("z0",), ("z1",), ("z1", "z0")]


def greet(pos):
    barrier = pltpu.get_barrier_semaphore()
    for dims in NEAR:
        pl.semaphore_signal(
            barrier, inc=1, device_id=partner(pos, dims), device_id_type=pl.DeviceIdType.MESH
        )
    pl.semaphore_wait(barrier, len(NEAR))


def remote(src, dst, send_sem, recv_sem, device):
    return pltpu.make_async_remote_copy(
        src_ref=src, dst_ref=dst, send_sem=send_sem, recv_sem=recv_sem,
        device_id=device, device_id_type=pl.DeviceIdType.MESH,
    )


def by_core(pos, action):
    for c in range(2):
        pl.when(pos["c"] == c)(functools.partial(action, c))


def half(c):
    return slice(384 * c, 384 * c + 384)


PARTS = [("p", 0), ("h", 0), ("h", 1), ("h", 2), ("h", 3), ("u", 4), ("u", 6), ("u", 8), ("u", 10)]
Z = ("z1", "z0")
SHORT = ((Z, ("x", "y")),) * 2
PLAIN = ((Z, ("x",), ("y",)), (Z, ("y",), ("x",)))
ROUTES = [SHORT, SHORT] + [PLAIN] * 7


class Gather:
    def __init__(self, pos, wg, wp, stage, stage_p, send, recv):
        self.pos, self.wg, self.wp = pos, wg, wp
        self.stage, self.stage_p = stage, stage_p
        self.send, self.recv = send, recv

    def view(self, i, c, index):
        kind, u = PARTS[i]
        if kind == "p":
            return self.wp.at[index + (slice(None), half(c))]
        if kind == "h":
            return self.wg.at[(u,) + index + (slice(None), half(c))]
        return self.wg.at[(u + c,) + index]

    def staged(self, i, c, rows):
        kind, u = PARTS[i]
        if kind == "p":
            return self.stage_p.at[rows, half(c)]
        if kind == "h":
            return self.stage.at[u, rows, half(c)]
        return self.stage.at[u + c, rows, :]

    def swap(self, i, c):
        own = pl.ds(16 * c, 16) if PARTS[i][0] == "p" else pl.ds(24 * c, 24)
        view = self.staged(i, 1 - c, own)
        return remote(view, view, self.send.at[i, 10], self.recv.at[i, 10], partner(self.pos, ("c",)))

    def hops(self, i, s, c):
        route = ROUTES[i][c]
        first = sum(len(subsets(dims)) for dims in route[:s])
        view = self.view(i, c, cube(self.pos, sum(route[:s], ())))
        return [
            remote(view, view, self.send.at[i, first + n], self.recv.at[i, first + n], partner(self.pos, dims))
            for n, dims in enumerate(subsets(route[s]))
        ]

    def gives(self, i, late, c):
        route = ROUTES[i][c]
        full = sum(route[:-1], ())
        ways = subsets(route[-1]) if late else [()]
        views = [self.view(i, c, cube(self.pos, full, dims)) for dims in ways]
        return [
            remote(
                view, view, self.send.at[i, 6 + late + n], self.recv.at[i, 6 + late + n],
                partner(self.pos, ("c",)),
            )
            for n, view in enumerate(views)
        ]

    def begin(self, i):
        def action(c):
            other = pl.ds(16 * (1 - c), 16) if PARTS[i][0] == "p" else pl.ds(24 * (1 - c), 24)
            view = self.staged(i, c, other)
            remote(
                view, view, self.send.at[i, 10], self.recv.at[i, 10], partner(self.pos, ("c",))
            ).wait_recv()
            rows = slice(0, 32 if PARTS[i][0] == "p" else 48)
            block = self.view(i, c, cube(self.pos, ()))
            block[...] = self.staged(i, c, rows)[...].astype(BF16)
            for copy in self.hops(i, 0, c):
                copy.start()

        by_core(self.pos, action)

    def step(self, i, s):
        def action(c):
            last = len(ROUTES[i][c]) - 1
            for copy in self.hops(i, s, c):
                copy.wait_recv()
            if s < last:
                for copy in self.hops(i, s + 1, c):
                    copy.start()
            if s >= last - 1:
                for copy in self.gives(i, s - last + 1, c):
                    copy.start()

        by_core(self.pos, action)

    def need(self, i):
        def action(c):
            for late in range(2):
                for copy in self.gives(i, late, 1 - c):
                    copy.wait_recv()

        by_core(self.pos, action)

    def finish(self):
        def action(c):
            for i in range(len(PARTS)):
                self.swap(i, c).wait_send()
                for s in range(len(ROUTES[i][c])):
                    for copy in self.hops(i, s, c):
                        copy.wait_send()
                for late in range(2):
                    for copy in self.gives(i, late, c):
                        copy.wait_send()

        by_core(self.pos, action)


class VectorSum:
    PHASES = (("c",), ("x", "y"), Z)

    def __init__(self, pos, rows, held, got, send, recv):
        self.pos, self.rows, self.held, self.got, self.send, self.recv = pos, rows, held, got, send, recv

    def copies(self, s):
        first = sum(len(subsets(dims)) for dims in self.PHASES[:s])
        return [
            remote(
                self.held.at[s, self.rows], self.got.at[first + n, self.rows],
                self.send.at[first + n], self.recv.at[first + n], partner(self.pos, dims),
            )
            for n, dims in enumerate(subsets(self.PHASES[s]))
        ]

    def start(self, s=0):
        for copy in self.copies(s):
            copy.start()

    def step(self, s):
        first = sum(len(subsets(dims)) for dims in self.PHASES[:s])
        total = self.held[s, self.rows]
        for n, copy in enumerate(self.copies(s)):
            copy.wait_recv()
            total = total + self.got[first + n, self.rows]
        self.held[s + 1, self.rows] = total
        if s < 2:
            self.start(s + 1)

    def finish(self):
        for s in range(3):
            for copy in self.copies(s):
                copy.wait_send()


def square(ref, u):
    return ref[u].reshape(D, D)


def forward_kernel(
    fast,
    *refs,
):
    refs = list(refs)
    take = lambda n: [refs.pop(0) for _ in range(n)]
    seg_ref, cfg_ref, feat_hbm, cot_hbm = take(4)
    if fast:
        own_p, own_a, own_o, own_f, own_s = take(5)
        wg_out, wp_out, svec = None, None, None
    else:
        wg_hbm, wp_hbm, svec = take(3)
    (
        act_out, hlt_out, qkv_out, kt_out, mixed_out, mixedt_out, xh1_out, inv1_out, flt_out,
        active_out, gp_out, d2_out, dg_out, dgt_out, lse_out, sg_out,
    ) = take(16)
    if fast:
        wg_out, wp_out, svec = take(3)
    (
        feat, cot, wg, wp, hid, hl, hlt, qkv, kt, vt, mixed, mixedt, xh1, fl, flt, active, gp, dg, dgt,
        kpat, qpat, sem_in, sem_out,
    ) = take(23)
    if fast:
        raw_p, raw_a, raw_o, raw_f, stage, stage_p, sem_raw, g_send, g_recv, sv_held, sv_got, v_send, v_recv = take(13)
    act = hl
    outs = []

    def load(i, src, dst):
        copy = pltpu.make_async_copy(src, dst, sem_in.at[i])
        copy.start()
        return copy

    def save(src, dst, part=None):
        i = len(outs)
        pick = lambda ref: ref if part is None else ref.at[part]
        make = lambda: pltpu.make_async_copy(pick(src), pick(dst), sem_out.at[i])
        make().start()
        outs.append(make)

    def need(i):
        kind, u = PARTS[i]
        if fast:
            gather.need(i)
            if kind == "p":
                save(wp, wp_out)
            elif kind == "h":
                save(wg, wg_out, u)
            else:
                save(wg, wg_out, pl.ds(u, 2))
        elif kind == "p":
            c_wp.wait()
        else:
            for v in range(u, u + (2 if kind == "u" else 1)):
                c_w[v].wait()

    def run(*steps):
        if fast:
            for i, s in steps:
                if i == "v":
                    vector.step(s)
                elif s < 0:
                    gather.begin(i)
                else:
                    gather.step(i, s)

    width = cfg_ref[0, 0]
    count = 1.0 / width.astype(F32)
    c_feat = load(0, feat_hbm, feat)
    if fast:
        pos = here()
        raws = [
            pltpu.make_async_copy(src, dst, sem_raw.at[i])
            for i, (src, dst) in enumerate(
                [(own_p, raw_p), (own_a, raw_a), (own_o, raw_o), (own_f, raw_f), (own_s, sv_held.at[0])]
            )
        ]
        for copy in raws:
            copy.start()
        gather = Gather(pos, wg, wp, stage, stage_p, g_send, g_recv)
        vector = VectorSum(pos, slice(0, 88), sv_held, sv_got, v_send, v_recv)
        for copy in raws:
            copy.wait()

        def arrange(c):
            rows = slice(24 * c, 24 * c + 24)
            stage_p[16 * c : 16 * c + 16, :] = raw_p[...]
            for j in range(3):
                for i in range(3):
                    stage[j, rows, 256 * i : 256 * i + 256] = raw_a[i, :, 256 * j : 256 * j + 256]
            stage[3, rows, :] = raw_o[...]
            for i in range(2):
                for q in range(4):
                    stage[4 + 4 * i + q, rows, :] = raw_f[i, :, D * q : D * q + D]

        by_core(pos, arrange)
        greet(pos)
        by_core(pos, lambda c: gather.swap(0, c).start())
        vector.start(0)
        for i in range(1, len(PARTS)):
            by_core(pos, lambda c, i=i: gather.swap(i, c).start())
        run((0, -1), (1, -1))
    else:
        c_wp = load(1, wp_hbm, wp)
        c_w = [load(2 + u, wg_hbm.at[u], wg.at[u]) for u in range(12)]
    c_cot = load(14, cot_hbm, cot)
    fill_patterns(seg_ref, kpat, qpat)
    run(("v", 0), (0, 0), ("v", 1), (2, -1), (1, 0), (3, -1), ("v", 2), (0, 1))
    if fast:
        for i in range(VEC // 128):
            svec[0:1, 128 * i : 128 * i + 128] = sv_held[3, i : i + 1, :]
    c_feat.wait()
    need(0)

    @pl.loop(0, NT)
    def _(t):
        rows = rows_of(t)
        normed = norm0(feat, svec, rows)[2]
        h = (mm(normed, wp[...].reshape(FEAT, D)) + piece(svec, "bp")) * keep_row(D, width)
        hid[rows, :] = h
        low = h.astype(BF16)
        hl[rows, :] = low
        hlt[:, rows] = low.T

    save(hlt, hlt_out)
    run((2, 0), (1, 1), (3, 0), (4, -1), (5, -1))
    need(1)

    slots = [
        [[], [(2, 1), (3, 1)]],
        [[(4, 0), (6, -1)], [(5, 0), (7, -1), (4, 1), (2, 2)]],
        [[], [(6, 0), (8, -1)]],
        [[(4, 2), (5, 1), (7, 0)], []],
        [[], [(6, 1), (8, 0)]],
        [[(7, 1)], [(5, 2)]],
    ]

    def at_slot(p, e):
        if fast:
            for i in range(PAIRS):
                if slots[i][e]:

                    @pl.when(p == i)
                    def _(i=i):
                        run(*slots[i][e])

    @pl.loop(0, PAIRS)
    def _(p):
        for j in range(3):

            @pl.when(p == 2 * j)
            def _(j=j):
                if j:
                    need(1 + j)

        @pl.when(lax.rem(p, 2) == 0)
        def _():
            j = lax.div(p, 2)
            group = lanes_of(j, 256)

            @pl.loop(0, NT)
            def _(t):
                rows = rows_of(t)
                keep = keep_row(256, cfg_ref[0, 1] * HDIM - j * 256)
                o = mm(hl[rows, :], square(wg, j))
                bias = lambda name: svec[0:1, pl.ds(pl.multiple_of(OFFSETS[name] + j * 256, 128), 256)]
                qkv[0, rows, group] = ((o[:, 0:256] + bias("bq")) * keep).astype(BF16)
                k = (o[:, 256:512] * keep).astype(BF16)
                qkv[1, rows, group] = k
                v = ((o[:, 512:768] + bias("bv")) * keep).astype(BF16)
                qkv[2, rows, group] = v
                down = pl.ds(pl.multiple_of(j * 256, 256), 256)
                kt[down, rows] = k.T
                vt[down, rows] = v.T

        if fast:

            @pl.when(p == 2)
            def _():
                run((3, 2))

        lanes = lanes_of(p)
        for e in range(2):
            kaug = qkv[1, :, lanes] * half_mask(e) + kpat[e]
            head_rows = pl.ds(pl.multiple_of(p * 128 + 64 * e, 64), 64)
            for b in range(NT):
                lo, hi = KEY_RANGE[b]
                cols = slice(b * TILE, (b + 1) * TILE)
                qaug = qkv[0, cols, lanes] * (half_mask(e) * 0.125) + qpat[e, cols, :]
                st = mm_nt(kaug[lo:hi], qaug)
                peak = jnp.max(st, 0, keepdims=True)
                power = jnp.exp(st - peak)
                total = col_sum(power)
                ot = mm(vt[head_rows, lo:hi], power.astype(BF16))
                mixedt[head_rows, cols] = (ot * (1.0 / total)).astype(BF16)
                lse_out[pl.ds(2 * p + e, 1), cols] = peak + jnp.log(total)
            at_slot(p, e)

    save(qkv, qkv_out)
    save(kt, kt_out)
    save(mixedt, mixedt_out)
    need(4)

    @pl.loop(0, NT)
    def _(t):
        rows = rows_of(t)
        keep = keep_row(D, width)
        mix = mixedt[:, rows].T
        mixed[rows, :] = mix
        z = hid[rows, :] + (mm(mix, square(wg, 3)) + piece(svec, "bo")) * keep
        centred = (z - row_sum(z * keep) * count) * keep
        inv = lax.rsqrt(row_sum(centred * centred) * count + NORM_EPS)
        hat = centred * inv
        first = (hat * piece(svec, "g1") + piece(svec, "c1")) * keep
        xh1[rows, :] = hat.astype(BF16)
        inv1_out[rows, :] = jnp.broadcast_to(inv, (TILE, 128))
        hid[rows, :] = first + piece(svec, "b2") * keep
        low = first.astype(BF16)
        fl[rows, :] = low
        flt[:, rows] = low.T

    save(mixed, mixed_out)
    save(xh1, xh1_out)
    save(flt, flt_out)
    need(5)

    def up(q):
        @pl.loop(0, LEN // 512)
        def _(t):
            rows = span_of(t, 512)
            u = (mm(fl[rows, :], square(wg, 4 + q)) + piece(svec, "b1", q * D, D)) * keep_row(
                D, cfg_ref[0, 2], q * D
            )
            g, slope = gelu_both(u)
            active[q, rows, :] = g.astype(BF16)
            gp[q, rows, :] = slope.astype(BF16)

        save(active, active_out, q)
        save(gp, gp_out, q)

    def down(q):
        hid[...] += mm_nt(active[q], square(wg, 8 + q)) * keep_row(D, width)

    up(0)
    run((8, 1), (6, 2))
    up(1)
    need(6)
    up(2)
    run((7, 2))
    up(3)
    need(7)
    down(0)
    down(1)
    run((8, 2))
    need(8)
    down(2)
    down(3)
    c_cot.wait()
    zero = jnp.zeros((1, D), F32)

    def last(t, sums):
        gain_sum, shift_sum, bias_sum = sums
        rows = rows_of(t)
        keep = keep_row(D, width)
        z = hid[rows, :]
        centred = (z - row_sum(z * keep) * count) * keep
        inv = lax.rsqrt(row_sum(centred * centred) * count + NORM_EPS)
        hat = centred * inv
        gain = piece(svec, "g2")
        act[rows, :] = ((hat * gain + piece(svec, "c2")) * keep).astype(BF16)
        g = cot[rows, :].astype(F32) * keep
        gain_sum = gain_sum + col_sum(g * hat)
        shift_sum = shift_sum + col_sum(g)
        a = g * gain
        d2 = inv * (a - keep * (row_sum(a) * count) - hat * (row_sum(a * hat) * count))
        hid[rows, :] = d2
        low = d2.astype(BF16)
        dg[rows, :] = low
        dgt[:, rows] = low.T
        return gain_sum, shift_sum, bias_sum + col_sum(low.astype(F32))

    gain_sum, shift_sum, bias_sum = lax.fori_loop(0, NT, last, (zero, zero, zero))
    sg_out[...] = jnp.zeros((88, 128), F32)
    put(sg_out, "g2", gain_sum)
    put(sg_out, "c2", shift_sum)
    put(sg_out, "b2", bias_sum)
    save(act, act_out)
    save(hid, d2_out)
    save(dg, dg_out)
    save(dgt, dgt_out)
    if fast:
        gather.finish()
        vector.finish()
    for make in outs:
        make().wait()


R_PARTS = [("u", 8), ("u", 4), ("u", 10), ("u", 6), ("h", 3), ("h", 0), ("h", 1), ("h", 2), ("p", 0)]
R_PLAIN = ((("x",), ("y",), Z), (("y",), ("x",), Z))
R_SHORT = ((("x", "y"), Z),) * 2
R_ROUTES = [R_PLAIN] * 7 + [R_SHORT] * 2


class Scatter:
    def __init__(self, pos, acc, got, given, first, fin, gout, goutp, send, recv, local, credit):
        self.pos, self.acc, self.got, self.given, self.first = pos, acc, got, given, first
        self.fin, self.gout, self.goutp = fin, gout, goutp
        self.send, self.recv, self.local, self.credit = send, recv, local, credit

    def trim(self, i):
        kind = R_PARTS[i][0]
        if kind == "u":
            return ()
        return (slice(0, 32 if kind == "p" else 48), slice(0, 384))

    def held(self, bufs, i, index):
        kind = R_PARTS[i][0]
        if kind == "p":
            return bufs[2].at[index]
        if kind == "h":
            return bufs[1].at[(i - 4,) + index]
        return bufs[0].at[(i,) + index]

    def slot(self, buf, i):
        full = (slice(None),) * 4
        return buf.at[(i % 2,) + full + self.trim(i)]

    def hand(self, i):
        return remote(
            self.slot(self.given, i), self.slot(self.first, i), self.send.at[i, 6], self.recv.at[i, 6],
            partner(self.pos, ("c",)),
        )

    def hops(self, i, s, c):
        route = R_ROUTES[i][c]
        first = sum(len(subsets(dims)) for dims in route[:s])
        rest = sum(route[s + 1 :], ())
        dst = self.held(self.got, i, cube(self.pos, rest, sum(route[: s + 1], ())))
        return [
            remote(
                self.held(self.acc, i, cube(self.pos, rest, dims)), dst,
                self.send.at[i, first + n], self.recv.at[i, first + n], partner(self.pos, dims),
            )
            for n, dims in enumerate(subsets(route[s]))
        ]

    def came(self, i, s, c):
        route = R_ROUTES[i][c]
        rest = sum(route[s + 1 :], ())
        before = sum(route[:s], ())
        return [
            self.held(self.got, i, cube(self.pos, rest, before + tuple(d for d in route[s] if d not in dims)))
            for dims in subsets(route[s])
        ]

    def offer(self, i):
        if i >= 2:
            pl.semaphore_wait(self.credit, 1)
        self.hand(i).start()

    def reuse(self, i):
        if i >= 2:
            self.hand(i - 2).wait_send()

    def begin(self, i):
        self.hand(i).wait_recv()
        mine = self.held(self.acc, i, (slice(None),) * 4)
        mine[...] = mine[...] + self.slot(self.first, i)[...]
        if i < len(R_PARTS) - 2:
            pl.semaphore_signal(
                self.credit, inc=1, device_id=partner(self.pos, ("c",)),
                device_id_type=pl.DeviceIdType.MESH,
            )

        def action(c):
            for copy in self.hops(i, 0, c):
                copy.start()

        by_core(self.pos, action)

    def ends(self, i, c, own):
        kind, u = R_PARTS[i]
        rows = 16 if kind == "p" else 24
        fin = self.held(self.fin, i, ())
        if kind == "p":
            dst = self.goutp.at[:, half(c)]
        elif kind == "h":
            dst = self.gout.at[u, :, half(c)]
        else:
            dst = self.gout.at[u + c]
        if own:
            return pltpu.make_async_copy(fin.at[pl.ds(rows * c, rows)], dst, self.local.at[i])
        return remote(
            fin.at[pl.ds(rows * (1 - c), rows)], dst, self.send.at[i, 7], self.recv.at[i, 7],
            partner(self.pos, ("c",)),
        )

    def step(self, i, s):
        def action(c):
            route = R_ROUTES[i][c]
            for copy in self.hops(i, s, c):
                copy.wait_recv()
            mine = self.held(self.acc, i, cube(self.pos, sum(route[s + 1 :], ())))
            total = mine[...].astype(F32)
            for came in self.came(i, s, c):
                total = total + came[...].astype(F32)
            if s < len(route) - 1:
                mine[...] = total.astype(BF16)
                for copy in self.hops(i, s + 1, c):
                    copy.start()
            else:
                self.held(self.fin, i, ())[...] = total
                for own in (True, False):
                    self.ends(i, c, own).start()

        by_core(self.pos, action)

    def finish(self):
        n = len(R_PARTS)
        for i in range(n - 2, n):
            self.hand(i).wait_send()

        def action(c):
            for i in range(n):
                for s in range(len(R_ROUTES[i][c])):
                    for copy in self.hops(i, s, c):
                        copy.wait_send()
                self.ends(i, c, True).wait()
                self.ends(i, c, False).wait_send()
                self.ends(i, 1 - c, False).wait_recv()

        by_core(self.pos, action)


def backward_kernel(fast, *refs):
    refs = list(refs)
    take = lambda n: [refs.pop(0) for _ in range(n)]
    seg_ref, cfg_ref, feat_hbm, wg_hbm, wp_hbm, svec = take(6)
    (
        hlt_hbm, qkv_hbm, kt_hbm, mixed_hbm, mixedt_hbm, xh1_hbm, inv1_hbm, flt_hbm,
        active_hbm, gp_hbm, d2_hbm, dg_hbm, dgt_hbm, lse, sg_in,
    ) = take(15)
    dx_out, gu_out, gwp_out, sg = take(4)
    (
        feat, wbuf, wp, pool, tr, kt, qkv, go, inv1, fg, dg, tg, delta, dqt, kpat, qpat,
        acc_u, acc_h, acc_p, given, sem_in, sem_q, sem_dx,
    ) = take(23)
    if fast:
        (
            got_u, got_h, got_p, first_in, fin_u, fin_h, fin_p, r_send, r_recv, r_local, credit,
            sv_held, sv_got, v_send, v_recv,
        ) = take(15)
        pos = here()
        core = pos["c"]
        small = sv_held.at[0]
        scatter = Scatter(
            pos, (acc_u, acc_h, acc_p), (got_u, got_h, got_p), given, first_in, (fin_u, fin_h, fin_p),
            gu_out, gwp_out, r_send, r_recv, r_local, credit,
        )
        late, early = (
            VectorSum(pos, rows, sv_held, sv_got, v_send.at[i], v_recv.at[i])
            for i, rows in enumerate((slice(0, 32), slice(32, 88)))
        )
    else:
        sem_out = take(1)[0]
        core = lax.axis_index("dp") % 2
        small = sg
        holder = Scatter(None, (acc_u, acc_h, acc_p), *[None] * 10)

    def load(i, src, dst):
        copy = pltpu.make_async_copy(src, dst, sem_in.at[i])
        copy.start()
        return copy

    def run(*steps):
        if fast:
            for i, s in steps:
                if i == "e":
                    early.step(s)
                elif i == "l":
                    late.step(s)
                elif s < 0:
                    scatter.begin(i)
                else:
                    scatter.step(i, s)

    def columns(h):
        return pl.ds(pl.multiple_of(384 * h, 128), 384)

    def plain_copy(i, mine):
        kind, u = R_PARTS[i]
        which = core if mine else 1 - core
        full = (slice(None),) * 4
        if mine:
            src = holder.held(holder.acc, i, full)
        else:
            src = given.at[(i % 2,) + full + holder.trim(i)]
        if kind == "p":
            dst = gwp_out.at[full + (slice(None), columns(which))]
        elif kind == "h":
            dst = gu_out.at[(u,) + full + (slice(None), columns(which))]
        else:
            dst = gu_out.at[u + which]
        return pltpu.make_async_copy(src, dst, sem_out.at[i, 1 if mine else 0])

    def make(i, mine, left, right):
        if not mine:
            if fast:
                scatter.reuse(i)
            elif i >= 2:
                plain_copy(i - 2, False).wait()
        value = mm(left[...], right[...]).astype(BF16).reshape(CUBE + (48, D))
        if mine:
            acc_u[i] = value
        else:
            given[i % 2] = value
        if fast:
            if not mine:
                scatter.offer(i)
        else:
            plain_copy(i, mine).start()

    def make_both(i, left, right):
        kind = R_PARTS[i][0]
        rows = 32 if kind == "p" else 48
        if fast:
            scatter.reuse(i)
        elif i >= 2:
            plain_copy(i - 2, False).wait()

        def action(c):
            @pl.loop(0, 2)
            def _(y):
                value = mm(left[span_of(y, 8 * rows), :], right[...]).astype(BF16)
                mine = value[:, half(c)].reshape(2, 2, 2, rows, 384)
                given[(i % 2, y) + (slice(None),) * 3 + (slice(0, rows), slice(0, 384))] = value[
                    :, half(1 - c)
                ].reshape(2, 2, 2, rows, 384)
                if kind == "p":
                    acc_p[y] = mine
                else:
                    acc_h[i - 4, y] = mine

        by_core(dict(c=core), action)
        if fast:
            scatter.offer(i)
        else:
            plain_copy(i, False).start()
            plain_copy(i, True).start()

    def quarter(k):
        s = k % 2
        q = 2 * (k // 2) + (core if k % 2 else 1 - core)
        pairs = [
            (active_hbm.at[q], pool.at[s]),
            (wg_hbm.at[8 + q], wbuf.at[s]),
            (gp_hbm.at[q], pool.at[2 + s]),
            (wg_hbm.at[4 + q], wbuf.at[2 + s]),
        ]
        return q, [
            pltpu.make_async_copy(src, dst, sem_q.at[s, i]) for i, (src, dst) in enumerate(pairs)
        ]

    dgt, flt, ig = tr.at[0], tr.at[1], pool.at[4]
    c_dgt = load(0, dgt_hbm, dgt)
    for copy in quarter(0)[1]:
        copy.start()
    c_dg = load(1, dg_hbm, dg)
    c_flt = load(2, flt_hbm, flt)
    c_d2 = load(3, d2_hbm, fg)
    for copy in quarter(1)[1]:
        copy.start()
    c_xh1 = load(4, xh1_hbm, go)
    c_inv1 = load(5, inv1_hbm, inv1)
    c_mixed = load(6, mixed_hbm, pool.at[5])
    c_qkv = load(9, qkv_hbm, qkv)
    c_kt = load(10, kt_hbm, kt)
    c_wp = load(15, wp_hbm, wp)
    c_feat = load(16, feat_hbm, feat)

    width = cfg_ref[0, 0]
    count = 1.0 / width.astype(F32)
    if fast:
        greet(pos)
    small[...] = sg_in[...]
    fill_patterns(seg_ref, kpat, qpat)
    c_dgt.wait()
    events = {
        (1, 0): [(0, -1)],
        (1, 2): [(1, -1)],
        (3, 0): [(2, -1), (0, 0)],
        (3, 2): [(3, -1), (1, 0)],
    }
    for k in range(4):
        s = k % 2
        mine = bool(k % 2)
        q, copies = quarter(k)
        at = lambda n: run(*events.get((k, n), []))
        copies[0].wait()
        make(2 * (k // 2), mine, dgt, pool.at[s])
        at(0)
        if k == 0:
            c_dg.wait()
        copies[1].wait()
        copies[2].wait()

        def inner(t, bias, q=q, s=s):
            rows = span_of(t, 512)
            low = (
                mm(dg[rows, :], square(wbuf, s))
                * pool[2 + s, rows, :].astype(F32)
                * keep_row(D, cfg_ref[0, 2] - q * D)
            ).astype(BF16)
            ig[rows, :] = low
            return bias + col_sum(low.astype(F32))

        put(small, "b1", lax.fori_loop(0, LEN // 512, inner, jnp.zeros((1, D), F32)), q * D)
        at(1)
        if k == 0:
            c_flt.wait()
            c_d2.wait()
        make(2 * (k // 2) + 1, mine, flt, ig)
        at(2)
        copies[3].wait()

        fg[...] += mm_nt(ig[...], square(wbuf, 2 + s))
        at(3)
        if k < 2:
            for copy in quarter(k + 2)[1]:
                copy.start()
        if k == 2:
            c_wo = load(8, wg_hbm.at[3], wbuf.at[0])
            c_wa = [load(12, wg_hbm.at[0], wbuf.at[2])]

    mixedt, hlt, mixed = tr.at[0], tr.at[1], pool.at[5]
    c_mixedt = load(7, mixedt_hbm, mixedt)
    c_hlt = load(11, hlt_hbm, hlt)
    c_wa.append(load(13, wg_hbm.at[1], wbuf.at[1]))
    c_wa.append(load(14, wg_hbm.at[2], wbuf.at[3]))
    wa_slot = (2, 1, 3)
    for copy in (c_xh1, c_inv1, c_mixed, c_wo):
        copy.wait()
    zero = jnp.zeros((1, D), F32)

    def middle(t, sums):
        gain_sum, shift_sum, bias_sum = sums
        rows = rows_of(t)
        keep = keep_row(D, width)
        hat = go[rows, :].astype(F32)
        g = fg[rows, :] * keep
        gain_sum = gain_sum + col_sum(g * hat)
        shift_sum = shift_sum + col_sum(g)
        a = g * piece(svec, "g1")
        d1 = inv1[rows, 0:1] * (a - keep * (row_sum(a) * count) - hat * (row_sum(a * hat) * count))
        fg[rows, :] = d1
        low = d1.astype(BF16)
        dg[rows, :] = low
        mg = mm_nt(low, square(wbuf, 0)).astype(BF16)
        go[rows, :] = mg
        product = mg.astype(F32) * mixed[rows, :].astype(F32)
        high = product.astype(BF16)
        rest = (product - high.astype(F32)).astype(BF16)
        lane = lax.broadcasted_iota(jnp.int32, (16, D), 1)
        head = lax.broadcasted_iota(jnp.int32, (16, D), 0)
        pick = ((lane >= head * HDIM) & (lane < head * HDIM + HDIM)).astype(F32).astype(BF16)
        delta[:, rows] = mm_nt(pick, high) + mm_nt(pick, rest)
        return gain_sum, shift_sum, bias_sum + col_sum(low.astype(F32))

    gain_sum, shift_sum, bias_sum = lax.fori_loop(0, NT, middle, (zero, zero, zero))
    put(small, "g1", gain_sum)
    put(small, "c1", shift_sum)
    put(small, "bo", bias_sum)
    if fast:
        early.start()
    run((0, 1))
    c_mixedt.wait()
    make_both(4, mixedt, dg)

    c_qkv.wait()
    c_kt.wait()
    c_hlt.wait()
    for copy in c_wa:
        copy.wait()
    slots = [
        [[], [(2, 0), (1, 1), (4, -1)], [("e", 0), (3, 0)], []],
        [[], [(5, -1), (1, 2), ("e", 2), (3, 1)], [], [(4, 1)]],
        [[], [(6, -1), (3, 2), (4, 2)], [], [(5, 1)]],
    ]
    after_loop = [[(0, 2), ("e", 1)], [], []]
    after_make = [[(4, 0)], [(5, 0), (2, 2)], [(6, 0)]]
    after_back = [[(2, 1)], [], [(7, -1)]]

    def chunk(n):
        return n // 3, slice(256 * (n % 3), 256 * (n % 3) + 256)

    for j in range(3):

        def at_slot(pp, e, j=j):
            if fast:
                for i in range(2):
                    steps = slots[j][2 * i + e]
                    if steps:

                        @pl.when(pp == i)
                        def _(steps=steps):
                            run(*steps)

        @pl.loop(0, 2)
        def _(pp, j=j):
            p = j * 2 + pp
            lanes = lanes_of(p)
            for e in range(2):
                at_slot(pp, e)
                kaug = qkv[1, :, lanes] * half_mask(e) + kpat[e]
                head_rows = pl.ds(pl.multiple_of(p * 128 + 64 * e, 64), 64)
                for b in range(NT):
                    lo, hi = KEY_RANGE[b]
                    cols = slice(b * TILE, (b + 1) * TILE)
                    qaug = qkv[0, cols, lanes] * (half_mask(e) * 0.125) + qpat[e, cols, :]
                    st = mm_nt(kaug[lo:hi], qaug)
                    weights = jnp.exp(st - lse[pl.ds(2 * p + e, 1), cols])
                    n, span = chunk(4 * e + b)
                    pool[n, lo:hi, span] = weights.astype(BF16)
                    goe = go[cols, lanes] * half_mask(e)
                    dp = mm_nt(qkv[2, lo:hi, lanes], goe)
                    ds = (weights * (dp - delta[pl.ds(2 * p + e, 1), cols])).astype(BF16)
                    n, span = chunk(8 + 4 * e + b)
                    pool[n, lo:hi, span] = ds
                    dqt[64 * e : 64 * e + 64, cols] = mm(kt[head_rows, lo:hi], ds)
            keep = keep_row(128, cfg_ref[0, 1] * HDIM - p * 128)
            for t in range(NT):
                rows = slice(t * TILE, (t + 1) * TILE)
                dk = jnp.zeros((TILE, 128), F32)
                dv = jnp.zeros((TILE, 128), F32)
                for b in range(NT):
                    if not KEY_RANGE[b][0] <= t * TILE < KEY_RANGE[b][1]:
                        continue
                    cols = slice(b * TILE, (b + 1) * TILE)
                    for e in range(2):
                        n, span = chunk(8 + 4 * e + b)
                        dk = dk + mm(pool[n, rows, span], qkv[0, cols, lanes] * half_mask(e))
                        n, span = chunk(4 * e + b)
                        dv = dv + mm(pool[n, rows, span], go[cols, lanes] * half_mask(e))
                dq = dqt[:, rows].T
                for i, value in enumerate((dq * (keep * 0.125), dk * (keep * 0.125), dv * keep)):
                    tg[rows, pl.ds(pl.multiple_of(256 * i + pp * 128, 128), 128)] = value.astype(BF16)

        run(*after_loop[j])
        make_both(5 + j, hlt, tg)
        run(*after_make[j])

        fg[...] += mm_nt(tg[...], square(wbuf, wa_slot[j]))
        bias = lax.fori_loop(
            0, NT, lambda t, total: total + col_sum(tg[rows_of(t), :].astype(F32)), zero
        )
        put(small, "bq", bias[:, 0:256], 256 * j)
        put(small, "bv", bias[:, 512:768], 256 * j)
        run(*after_back[j])

    c_wp.wait()
    c_feat.wait()
    zero_feat = jnp.zeros((1, FEAT), F32)
    nrmt = tr.at[0]

    def first(t, bias_sum):
        rows = rows_of(t)
        nrmt[0:FEAT, rows] = norm0(feat, svec, rows)[2].T
        low = (fg[rows, :] * keep_row(D, width)).astype(BF16)
        dg[rows, :] = low
        return bias_sum + col_sum(low.astype(F32))

    put(small, "bp", lax.fori_loop(0, NT, first, zero))
    run((5, 2))
    make_both(8, nrmt, dg)

    def second(t, sums):
        gain_sum, shift_sum = sums
        rows = rows_of(t)
        hat, inv, _ = norm0(feat, svec, rows)
        g = mm_nt(dg[rows, :], wp[...].reshape(FEAT, D))
        gain_sum = gain_sum + col_sum(g * hat)
        shift_sum = shift_sum + col_sum(g)
        a = g * piece(svec, "g0")
        dx = inv * (a - row_sum(a) * (1.0 / FEAT) - hat * (row_sum(a * hat) * (1.0 / FEAT)))
        fg[rows, 0:FEAT] = 0.1 * dx
        return gain_sum, shift_sum

    gain_sum, shift_sum = lax.fori_loop(0, NT, second, (zero_feat, zero_feat))
    put(small, "g0", gain_sum)
    put(small, "b0", shift_sum)
    c_dx = pltpu.make_async_copy(fg.at[:, 0:FEAT], dx_out, sem_dx)
    c_dx.start()
    if fast:
        late.start()
        run((8, -1), (6, 1), (7, 0), ("l", 0), (8, 0), (6, 2), ("l", 1), (7, 1), (8, 1), ("l", 2))
        sg[...] = sv_held[3]
        early.finish()
        late.finish()
        scatter.finish()
    else:
        for i in range(len(R_PARTS)):
            plain_copy(i, True).wait()
        for i in range(len(R_PARTS) - 2, len(R_PARTS)):
            plain_copy(i, False).wait()
    c_dx.wait()


def adam_rule(weight, moment, square_in, grad, rate):
    moment_new = BETA_ONE * moment + (1.0 - BETA_ONE) * grad
    square_new = BETA_TWO * square_in + (1.0 - BETA_TWO) * grad * grad
    fix_one = 1.0 - BETA_ONE**STEP
    fix_two = 1.0 - BETA_TWO**STEP
    direction = moment_new / fix_one / (jnp.sqrt(square_new / fix_two) + ADAM_EPS)
    return (moment_new, square_new, weight - rate * (direction + DECAY * weight))


def adam_kernel(*refs):
    gu_hbm, gp_hbm, act_hbm, dx_hbm = refs[0:4]
    ins, act_out, dx_out, outs = refs[4:16], refs[16], refs[17], refs[18:34]
    gu, gp, act, dx = refs[34:38]
    held, new = refs[38:50], refs[50:62]
    sem_in, sem_out = refs[62:]
    sources = (gu_hbm,) + tuple(ins[9:12]) + (act_hbm, dx_hbm, gp_hbm) + tuple(ins[0:9])
    places = (gu,) + tuple(held[9:12]) + (act, dx, gp) + tuple(held[0:9])
    loads = [
        pltpu.make_async_copy(src, dst, sem_in.at[i]) for i, (src, dst) in enumerate(zip(sources, places))
    ]
    for copy in loads:
        copy.start()
    stores = []

    def store(src, dst):
        copy = pltpu.make_async_copy(src, dst, sem_out.at[len(stores)])
        copy.start()
        stores.append(copy)

    def update(k, pieces):
        w, m, v = held[3 * k : 3 * k + 3]
        for index, grad in pieces:
            done = adam_rule(w[index], m[index], v[index], grad(), RATE)
            for ref, value in zip(new[3 * k : 3 * k + 3], done):
                ref[index] = value
            m[index] = grad()
        for src, dst in zip((m,) + tuple(new[3 * k : 3 * k + 3]), outs[4 * k : 4 * k + 4]):
            store(src, dst)

    everything = (slice(None), slice(None))
    for copy in loads[0:4]:
        copy.wait()
    update(
        3,
        [
            ((i, slice(None), slice(D * q, D * q + D)), lambda i=i, q=q: gu[4 + 4 * i + q])
            for i in range(2) for q in range(4)
        ],
    )
    for copy in loads[4:6]:
        copy.wait()
    store(act, act_out)
    store(dx, dx_out)
    for copy in loads[6:16]:
        copy.wait()
    update(
        1,
        [
            ((i, slice(None), slice(256 * j, 256 * j + 256)), lambda i=i, j=j: gu[j, :, 256 * i : 256 * i + 256])
            for i in range(3) for j in range(3)
        ],
    )
    update(2, [(everything, lambda: gu[3])])
    update(0, [(everything, lambda: gp[...])])
    for copy in stores:
        copy.wait()


def adam_call(gu, gp, act, dx, state):
    shape = jax.ShapeDtypeStruct
    f32 = lambda s: pltpu.VMEM(s, F32)
    outs = [shape((LEN, D), BF16), shape((LEN, FEAT), F32)]
    outs += [shape(state[3 * k].shape, F32) for k in range(4) for _ in range(4)]
    scratch = [f32(gu.shape), f32(gp.shape), pltpu.VMEM((LEN, D), BF16), f32((LEN, FEAT))]
    scratch += [f32(x.shape) for x in state] * 2
    scratch += [pltpu.SemaphoreType.DMA((16,)), pltpu.SemaphoreType.DMA((18,))]
    return pl.pallas_call(
        adam_kernel,
        out_shape=outs,
        in_specs=[any_spec()] * 16,
        out_specs=[any_spec()] * 18,
        scratch_shapes=scratch,
        compiler_params=pltpu.CompilerParams(vmem_limit_bytes=VMEM_LIMIT),
        name="adam",
    )(gu, gp, act, dx, *state)


def any_spec():
    return pl.BlockSpec(memory_space=pl.ANY)


def vmem_spec():
    return pl.BlockSpec(memory_space=pltpu.VMEM)


def smem_spec():
    return pl.BlockSpec(memory_space=pltpu.SMEM)


def forward_call(fast, seg, cfg, feat, cot, weights):
    shape = jax.ShapeDtypeStruct
    outs = [
        (shape((LEN, D), BF16), any_spec()),
        (shape((D, LEN), BF16), any_spec()),
        (shape((3, LEN, D), BF16), any_spec()),
        (shape((D, LEN), BF16), any_spec()),
        (shape((LEN, D), BF16), any_spec()),
        (shape((D, LEN), BF16), any_spec()),
        (shape((LEN, D), BF16), any_spec()),
        (shape((LEN, 128), F32), vmem_spec()),
        (shape((D, LEN), BF16), any_spec()),
        (shape((4, LEN, D), BF16), any_spec()),
        (shape((4, LEN, D), BF16), any_spec()),
        (shape((LEN, D), F32), any_spec()),
        (shape((LEN, D), BF16), any_spec()),
        (shape((D, LEN), BF16), any_spec()),
        (shape((16, LEN), F32), vmem_spec()),
        (shape((88, 128), F32), vmem_spec()),
    ]
    if fast:
        outs += [
            (shape((12,) + CUBE + (48, D), BF16), any_spec()),
            (shape(CUBE + (32, D), BF16), any_spec()),
            (shape((1, VEC), F32), vmem_spec()),
        ]
    bf = lambda *s: pltpu.VMEM(s, BF16)
    f32 = lambda *s: pltpu.VMEM(s, F32)
    dma = lambda *s: pltpu.SemaphoreType.DMA(s)
    scratch = [
        bf(LEN, FEAT), bf(LEN, D), bf(12, *CUBE, 48, D), bf(*CUBE, 32, D), f32(LEN, D),
        bf(LEN, D), bf(D, LEN), bf(3, LEN, D), bf(D, LEN), bf(D, LEN), bf(LEN, D), bf(D, LEN),
        bf(LEN, D), bf(LEN, D), bf(D, LEN), bf(4, LEN, D), bf(4, LEN, D), bf(LEN, D), bf(D, LEN),
        bf(2, LEN, 128), bf(2, LEN, 128), dma(15), dma(32),
    ]
    if fast:
        scratch += [
            f32(16, D), f32(3, 24, D), f32(24, D), f32(2, 24, FF), f32(12, 48, D), f32(32, D), dma(5),
            dma(len(PARTS), 11), dma(len(PARTS), 11), f32(4, 88, 128), f32(7, 88, 128), dma(7), dma(7),
        ]
        specs = [any_spec()] * len(weights)
        params = dict(collective_id=0, has_side_effects=True)
    else:
        specs = [any_spec()] * 2 + [vmem_spec()]
        params = {}
    return pl.pallas_call(
        functools.partial(forward_kernel, fast),
        out_shape=[o[0] for o in outs],
        in_specs=[smem_spec(), smem_spec()] + [any_spec()] * 2 + specs,
        out_specs=[o[1] for o in outs],
        scratch_shapes=scratch,
        compiler_params=pltpu.CompilerParams(vmem_limit_bytes=VMEM_LIMIT, **params),
        name="forward",
    )(seg, cfg, feat, cot, *weights)


def backward_call(fast, seg, cfg, feat, wg, wp, svec, saved):
    shape = jax.ShapeDtypeStruct
    bf = lambda *s: pltpu.VMEM(s, BF16)
    f32 = lambda *s: pltpu.VMEM(s, F32)
    dma = lambda *s: pltpu.SemaphoreType.DMA(s)
    n = len(R_PARTS)
    scratch = [
        bf(LEN, FEAT), bf(4, *CUBE, 48, D), bf(*CUBE, 32, D), bf(6, LEN, D), bf(2, D, LEN), bf(D, LEN),
        bf(3, LEN, D), bf(LEN, D), f32(LEN, 128), f32(LEN, D), bf(LEN, D), bf(LEN, D), f32(16, LEN),
        f32(128, LEN), bf(2, LEN, 128), bf(2, LEN, 128),
        bf(4, *CUBE, 48, D), bf(4, *CUBE, 48, 384), bf(*CUBE, 32, 384), bf(2, *CUBE, 48, D),
        dma(17), dma(2, 4), pltpu.SemaphoreType.DMA,
    ]
    if fast:
        scratch += [
            bf(4, *CUBE, 48, D), bf(4, *CUBE, 48, 384), bf(*CUBE, 32, 384), bf(2, *CUBE, 48, D),
            f32(4, 48, D), f32(4, 48, 384), f32(32, 384), dma(n, 8), dma(n, 8), dma(n),
            pltpu.SemaphoreType.REGULAR, f32(4, 88, 128), f32(7, 88, 128), dma(2, 7), dma(2, 7),
        ]
        grads = [shape((12, 24, D), F32), shape((16, D), F32)]
        params = dict(collective_id=1, has_side_effects=True)
    else:
        scratch += [dma(n, 2)]
        grads = [shape((12,) + CUBE + (48, D), BF16), shape(CUBE + (32, D), BF16)]
        params = {}
    return pl.pallas_call(
        functools.partial(backward_kernel, fast),
        out_shape=[shape((LEN, FEAT), F32)] + grads + [shape((88, 128), F32)],
        in_specs=[smem_spec(), smem_spec()] + [any_spec()] * 3 + [vmem_spec()]
        + [any_spec()] * 13 + [vmem_spec()] * 2,
        out_specs=[any_spec()] * 3 + [vmem_spec()],
        scratch_shapes=scratch,
        compiler_params=pltpu.CompilerParams(vmem_limit_bytes=VMEM_LIMIT, **params),
        name="backward",
    )(seg, cfg, feat, wg, wp, svec, *saved)


AXES = ("grp", "dp")


def gathered(projection_weight, attention_weight, output_weight, feedforward_weight, small_params):
    gather = lambda w, axis: lax.all_gather(w.astype(BF16), AXES, axis=axis, tiled=True)
    wp = gather(projection_weight, 0)
    wa = gather(attention_weight, 1)
    wo = gather(output_weight, 0)
    wf = gather(feedforward_weight, 1)
    svec = gather(small_params, 0).astype(F32).reshape(1, VEC)
    return units(wp, wa, wo, wf) + (svec,)


def units(wp, wa, wo, wf):
    groups = wa.reshape(3, D, 3, 256).transpose(2, 1, 0, 3).reshape(3, D, D)
    quarters = wf.reshape(2, D, 4, D).transpose(0, 2, 1, 3).reshape(8, D, D)
    wg = jnp.concatenate([groups, wo[None], quarters], 0)
    return wg.reshape((12,) + CUBE + (48, D)), wp.reshape(CUBE + (32, D))


def layer(fast, features, lengths, config, cotangent, weights):
    feat = features.reshape(LEN, FEAT)
    cot = cotangent.reshape(LEN, D)
    saved = forward_call(fast, lengths, config, feat, cot, weights)
    activations = saved[0]
    wg, wp, svec = saved[16:] if fast else weights
    dx, gu, gwp, sg = backward_call(fast, lengths, config, feat, wg, wp, svec, saved[1:16])
    return activations, dx, gu, gwp, sg


def per_device(
    fast,
    features, segment_lengths, subnet_config, cotangent,
    projection_weight, projection_moment, projection_square,
    attention_weight, attention_moment, attention_square,
    output_weight, output_moment, output_square,
    feedforward_weight, feedforward_moment, feedforward_square,
    small_params, small_moment, small_square,
):
    weights = (projection_weight, attention_weight, output_weight, feedforward_weight)
    if fast:
        me = lax.axis_index(AXES)
        low = lax.reduce_precision(small_params, 8, 7)
        placed = lax.dynamic_update_slice(jnp.zeros((88 * 128,), F32), low, (me * low.shape[0],))
        weights = weights + (placed.reshape(88, 128),)
    else:
        weights = gathered(*weights, small_params)
    activations, dx, gu, gwp, sg = layer(
        fast, features, segment_lengths, subnet_config, cotangent, weights
    )
    state = (
        projection_weight, projection_moment, projection_square,
        attention_weight, attention_moment, attention_square,
        output_weight, output_moment, output_square,
        feedforward_weight, feedforward_moment, feedforward_square,
        small_params[None], small_moment[None], small_square[None],
    )
    out = [activations.reshape(1, LEN, D), dx.reshape(1, LEN, FEAT)]
    vec = sg.reshape(88 * 128)
    if fast:
        gs = lax.dynamic_slice(vec, (me * small_params.shape[0],), small_params.shape)
        done = adam_call(gu, gwp, activations, dx, state[:12])
        return (
            (done[0].reshape(1, LEN, D), done[1].reshape(1, LEN, FEAT))
            + tuple(done[2:18])
            + (gs,) + adam_rule(small_params, small_moment, small_square, gs, SMALL_RATE)
        )
    gu = gu.reshape(12, D, D).astype(F32)
    scatter = lambda g, dim: lax.psum_scatter(g, AXES, scatter_dimension=dim, tiled=True)
    ga = gu[0:3].reshape(3, D, 3, 256).transpose(2, 1, 0, 3).reshape(3, D, D)
    gf = gu[4:12].reshape(2, 4, D, D).transpose(0, 2, 1, 3).reshape(2, D, FF)
    sums = (
        scatter(gwp.reshape(FEAT, D).astype(F32), 0), scatter(ga, 1), scatter(gu[3], 0), scatter(gf, 1),
        scatter(vec[:VEC], 0)[None],
    )
    for k, g in enumerate(sums):
        new = (g,) + adam_rule(*state[3 * k : 3 * k + 3], g, RATE if k < 4 else SMALL_RATE)
        out.extend(x[0] if k == 4 else x for x in new)
    return tuple(out)


def solution(mesh):
    rows3, rows2, stacked, flat = (
        P(AXES, None, None), P(AXES, None), P(None, AXES, None), P(AXES),
    )
    return jax.shard_map(
        functools.partial(per_device, dict(mesh.shape) == dict(grp=4, dp=8)),
        mesh=mesh,
        in_specs=(
            rows3, rows2, P("grp", None), rows3, rows2, rows2, rows2, stacked, stacked, stacked,
            rows2, rows2, rows2, stacked, stacked, stacked, flat, flat, flat,
        ),
        out_specs=(rows3, rows3) + (rows2,) * 4 + (stacked,) * 4 + (rows2,) * 4 + (stacked,) * 4 + (flat,) * 4,
        check_vma=False,
    )
```

```python
import functools
import math

import jax
import jax.numpy as jnp
from jax import lax
from jax.experimental import pallas as pl
from jax.experimental.pallas import tpu as pltpu
from jax.sharding import PartitionSpec as P

D = 768
FF = 3072
FEAT = 512
HDIM = 64
HEADS = 12
PAIRS = HEADS // 2
LEN = 1024
STEP = 10
TILE = 256
NT = LEN // TILE
VEC = 11008

NORM_EPS = 1e-05
RATE = 0.08
SMALL_RATE = 0.3
BETA_ONE = 0.9
BETA_TWO = 0.999
ADAM_EPS = 1e-08
DECAY = 0.01

F32 = jnp.float32
BF16 = jnp.bfloat16
BIG = 2.0**100
VMEM_LIMIT = 63 << 20

WIDTHS = dict(
    g0=FEAT, b0=FEAT, bp=D, bq=D, bv=D, bo=D, g1=D, c1=D, b1=FF, b2=D, g2=D, c2=D
)
OFFSETS = {}
_at = 0
for _name, _width in WIDTHS.items():
    OFFSETS[_name] = _at
    _at += _width

KEY_RANGE = [
    (max(0, (i * TILE - 511) // TILE * TILE), min(LEN, -(-(i * TILE + TILE + 511) // TILE) * TILE))
    for i in range(NT)
]


def mm(a, b):
    return jnp.dot(a, b, preferred_element_type=F32)


def mm_nt(a, b):
    return lax.dot_general(a, b, (((1,), (1,)), ((), ())), preferred_element_type=F32)


def piece(ref, name, start=0, width=None):
    begin = OFFSETS[name] + start
    return ref[0:1, begin : begin + (width or WIDTHS[name])]


def put(ref, name, value, start=0):
    begin = OFFSETS[name] // 128 + start // 128
    for i in range(value.shape[1] // 128):
        ref[pl.ds(begin + i, 1), :] = value[:, 128 * i : 128 * i + 128]


def keep_row(width, limit, start=0):
    lane = lax.broadcasted_iota(jnp.int32, (1, width), 1) + start
    return (lane < limit).astype(F32)


def col_sum(value):
    return jnp.sum(value, 0, keepdims=True)


def row_sum(value):
    return jnp.sum(value, 1, keepdims=True)


def rows_of(t):
    return pl.ds(pl.multiple_of(t * TILE, TILE), TILE)


def span_of(t, size):
    return pl.ds(pl.multiple_of(t * size, size), size)


def lanes_of(p, width=128):
    return pl.ds(pl.multiple_of(p * width, width), width)


def gelu_both(u):
    half = jnp.exp(-0.5 * u * u)
    t = 1.0 / (1.0 + (0.3275911 * 0.7071067811865476) * jnp.abs(u))
    poly = 0.5 * 1.061405429
    for c in (-1.453152027, 1.421413741, -0.284496736, 0.254829592):
        poly = poly * t + 0.5 * c
    tail = poly * t * half
    cdf = jnp.where(u >= 0.0, 1.0 - tail, tail)
    return u * cdf, cdf + u * (half * 0.3989422804014327)


def fill_patterns(seg_ref, kpat, qpat):
    e0 = seg_ref[0, 0]
    e1 = e0 + seg_ref[0, 1]
    e2 = e1 + seg_ref[0, 2]

    @pl.loop(0, NT)
    def _(t):
        pos = lax.broadcasted_iota(jnp.int32, (TILE, 128), 0) + t * TILE
        lane = lax.broadcasted_iota(jnp.int32, (TILE, 128), 1)
        seg = (
            (pos >= e0).astype(jnp.int32)
            + (pos >= e1).astype(jnp.int32)
            + (pos >= e2).astype(jnp.int32)
        )
        for e in range(2):
            slot = lane - (64 if e == 0 else 0)
            valid = (slot >= 0) & (slot < 4)
            same = slot == seg
            kpat[e, rows_of(t), :] = jnp.where(same, 1.0, 0.0).astype(BF16)
            qpat[e, rows_of(t), :] = jnp.where(valid & (slot != seg), -BIG, 0.0).astype(BF16)


def half_mask(e):
    lane = lax.broadcasted_iota(jnp.int32, (1, 128), 1)
    return ((lane < 64) if e == 0 else (lane >= 64)).astype(F32).astype(BF16)


def norm0(feat, svec, rows):
    x = feat[rows, :].astype(F32)
    centred = x - row_sum(x) * (1.0 / FEAT)
    inv = lax.rsqrt(row_sum(centred * centred) * (1.0 / FEAT) + NORM_EPS)
    hat = centred * inv
    normed = (hat * piece(svec, "g0") + piece(svec, "b0")).astype(BF16)
    return hat, inv, normed


DIMS = ("y", "x", "z1", "z0")
CUBE = (2, 2, 2, 2)


def here():
    g = lax.axis_index("grp")
    d = lax.axis_index("dp")
    return dict(
        y=g // 2, x=g % 2, z1=d // 4, z0=(d // 2) % 2, c=d % 2,
    )


def partner(pos, dims):
    near = {k: (1 - v if k in dims else v) for k, v in pos.items()}
    return (near["y"] * 2 + near["x"], near["z1"] * 4 + near["z0"] * 2 + near["c"])


def cube(pos, full, other=()):
    return tuple(
        slice(None) if dim in full else (1 - pos[dim] if dim in other else pos[dim])
        for dim in DIMS
    )


def subsets(dims):
    return [(d,) for d in dims] + ([tuple(dims)] if len(dims) == 2 else [])


NEAR = [("c",), ("x",), ("y",), ("x", "y"), ("z0",), ("z1",), ("z1", "z0")]


def greet(pos):
    for dims in NEAR:
        pl.semaphore_signal(
            pltpu.get_barrier_semaphore(), inc=1, device_id=partner(pos, dims),
            device_id_type=pl.DeviceIdType.MESH,
        )


def meet():
    pl.semaphore_wait(pltpu.get_barrier_semaphore(), len(NEAR))


def remote(src, dst, send_sem, recv_sem, device):
    return pltpu.make_async_remote_copy(
        src_ref=src, dst_ref=dst, send_sem=send_sem, recv_sem=recv_sem,
        device_id=device, device_id_type=pl.DeviceIdType.MESH,
    )


def by_core(pos, action):
    for c in range(2):
        pl.when(pos["c"] == c)(functools.partial(action, c))


def half(c):
    return slice(384 * c, 384 * c + 384)


PARTS = [("p", 0), ("h", 0), ("h", 1), ("h", 2), ("h", 3), ("u", 4), ("u", 6), ("u", 8), ("u", 10)]
Z = ("z1", "z0")
SHORT = ((Z, ("x", "y")),) * 2
PLAIN = ((Z, ("x",), ("y",)), (Z, ("y",), ("x",)))
ROUTES = [SHORT, SHORT] + [PLAIN] * 7


class Gather:
    def __init__(self, pos, wg, wp, stage, stage_p, send, recv):
        self.pos, self.wg, self.wp = pos, wg, wp
        self.stage, self.stage_p = stage, stage_p
        self.send, self.recv = send, recv

    def view(self, i, c, index):
        kind, u = PARTS[i]
        if kind == "p":
            return self.wp.at[index + (slice(None), half(c))]
        if kind == "h":
            return self.wg.at[(u,) + index + (slice(None), half(c))]
        return self.wg.at[(u + c,) + index]

    def staged(self, i, c, rows):
        kind, u = PARTS[i]
        if kind == "p":
            return self.stage_p.at[rows, half(c)]
        if kind == "h":
            return self.stage.at[u, rows, half(c)]
        return self.stage.at[u + c, rows, :]

    def swap(self, i, c):
        own = pl.ds(16 * c, 16) if PARTS[i][0] == "p" else pl.ds(24 * c, 24)
        view = self.staged(i, 1 - c, own)
        return remote(view, view, self.send.at[i, 10], self.recv.at[i, 10], partner(self.pos, ("c",)))

    def hops(self, i, s, c):
        route = ROUTES[i][c]
        first = sum(len(subsets(dims)) for dims in route[:s])
        view = self.view(i, c, cube(self.pos, sum(route[:s], ())))
        return [
            remote(view, view, self.send.at[i, first + n], self.recv.at[i, first + n], partner(self.pos, dims))
            for n, dims in enumerate(subsets(route[s]))
        ]

    def gives(self, i, late, c):
        route = ROUTES[i][c]
        full = sum(route[:-1], ())
        ways = subsets(route[-1]) if late else [()]
        views = [self.view(i, c, cube(self.pos, full, dims)) for dims in ways]
        return [
            remote(
                view, view, self.send.at[i, 6 + late + n], self.recv.at[i, 6 + late + n],
                partner(self.pos, ("c",)),
            )
            for n, view in enumerate(views)
        ]

    def begin(self, i):
        def action(c):
            other = pl.ds(16 * (1 - c), 16) if PARTS[i][0] == "p" else pl.ds(24 * (1 - c), 24)
            view = self.staged(i, c, other)
            remote(
                view, view, self.send.at[i, 10], self.recv.at[i, 10], partner(self.pos, ("c",))
            ).wait_recv()
            rows = slice(0, 32 if PARTS[i][0] == "p" else 48)
            block = self.view(i, c, cube(self.pos, ()))
            block[...] = self.staged(i, c, rows)[...].astype(BF16)
            for copy in self.hops(i, 0, c):
                copy.start()

        by_core(self.pos, action)

    def step(self, i, s):
        def action(c):
            last = len(ROUTES[i][c]) - 1
            for copy in self.hops(i, s, c):
                copy.wait_recv()
            if s < last:
                for copy in self.hops(i, s + 1, c):
                    copy.start()
            if s >= last - 1:
                for copy in self.gives(i, s - last + 1, c):
                    copy.start()

        by_core(self.pos, action)

    def need(self, i):
        def action(c):
            for late in range(2):
                for copy in self.gives(i, late, 1 - c):
                    copy.wait_recv()

        by_core(self.pos, action)

    def finish(self):
        def action(c):
            for i in range(len(PARTS)):
                self.swap(i, c).wait_send()
                for s in range(len(ROUTES[i][c])):
                    for copy in self.hops(i, s, c):
                        copy.wait_send()
                for late in range(2):
                    for copy in self.gives(i, late, c):
                        copy.wait_send()

        by_core(self.pos, action)


class VectorSum:
    PHASES = (("c",), ("x", "y"), Z)

    def __init__(self, pos, rows, held, got, send, recv):
        self.pos, self.rows, self.held, self.got, self.send, self.recv = pos, rows, held, got, send, recv

    def copies(self, s):
        first = sum(len(subsets(dims)) for dims in self.PHASES[:s])
        return [
            remote(
                self.held.at[s, self.rows], self.got.at[first + n, self.rows],
                self.send.at[first + n], self.recv.at[first + n], partner(self.pos, dims),
            )
            for n, dims in enumerate(subsets(self.PHASES[s]))
        ]

    def start(self, s=0):
        for copy in self.copies(s):
            copy.start()

    def step(self, s):
        first = sum(len(subsets(dims)) for dims in self.PHASES[:s])
        total = self.held[s, self.rows]
        for n, copy in enumerate(self.copies(s)):
            copy.wait_recv()
            total = total + self.got[first + n, self.rows]
        self.held[s + 1, self.rows] = total
        if s < 2:
            self.start(s + 1)

    def finish(self):
        for s in range(3):
            for copy in self.copies(s):
                copy.wait_send()


def square(ref, u):
    return ref[u].reshape(D, D)


def forward_kernel(
    fast,
    *refs,
):
    refs = list(refs)
    take = lambda n: [refs.pop(0) for _ in range(n)]
    seg_ref, cfg_ref, feat_hbm, cot_hbm = take(4)
    if fast:
        own_p, own_a, own_o, own_f, own_s = take(5)
        wg_out, wp_out, svec = None, None, None
    else:
        wg_hbm, wp_hbm, svec = take(3)
    (
        act_out, hlt_out, qkv_out, kt_out, mixed_out, mixedt_out, xh1_out, inv1_out, flt_out,
        active_out, gp_out, d2_out, dg_out, dgt_out, lse_out, sg_out,
    ) = take(16)
    if fast:
        wg_out, wp_out, svec = take(3)
    (
        feat, cot, wg, wp, hid, hl, hlt, qkv, kt, vt, mixed, mixedt, xh1, fl, flt, active, gp, dg, dgt,
        kpat, qpat, sem_in, sem_out,
    ) = take(23)
    if fast:
        raw_p, raw_a, raw_o, raw_f, stage, stage_p, sem_raw, g_send, g_recv, sv_held, sv_got, v_send, v_recv = take(13)
    act = hl
    outs = []

    def load(i, src, dst):
        copy = pltpu.make_async_copy(src, dst, sem_in.at[i])
        copy.start()
        return copy

    def save(src, dst, part=None):
        i = len(outs)
        pick = lambda ref: ref if part is None else ref.at[part]
        make = lambda: pltpu.make_async_copy(pick(src), pick(dst), sem_out.at[i])
        make().start()
        outs.append(make)

    def need(i):
        kind, u = PARTS[i]
        if fast:
            gather.need(i)
            if kind == "p":
                save(wp, wp_out)
            elif kind == "h":
                save(wg, wg_out, u)
            else:
                save(wg, wg_out, pl.ds(u, 2))
        elif kind == "p":
            c_wp.wait()
        else:
            for v in range(u, u + (2 if kind == "u" else 1)):
                c_w[v].wait()

    def run(*steps):
        if fast:
            for i, s in steps:
                if i == "v":
                    vector.step(s)
                elif s < 0:
                    gather.begin(i)
                else:
                    gather.step(i, s)

    width = cfg_ref[0, 0]
    count = 1.0 / width.astype(F32)
    c_feat = load(0, feat_hbm, feat)
    if fast:
        pos = here()
        greet(pos)
        raws = [
            pltpu.make_async_copy(src, dst, sem_raw.at[i])
            for i, (src, dst) in enumerate(
                [(own_p, raw_p), (own_a, raw_a), (own_o, raw_o), (own_f, raw_f), (own_s, sv_held.at[0])]
            )
        ]
        for copy in raws:
            copy.start()
        gather = Gather(pos, wg, wp, stage, stage_p, g_send, g_recv)
        vector = VectorSum(pos, slice(0, 88), sv_held, sv_got, v_send, v_recv)
        for copy in raws:
            copy.wait()

        def arrange(c):
            rows = slice(24 * c, 24 * c + 24)
            stage_p[16 * c : 16 * c + 16, :] = raw_p[...]
            for j in range(3):
                for i in range(3):
                    stage[j, rows, 256 * i : 256 * i + 256] = raw_a[i, :, 256 * j : 256 * j + 256]
            stage[3, rows, :] = raw_o[...]
            for i in range(2):
                for q in range(4):
                    stage[4 + 4 * i + q, rows, :] = raw_f[i, :, D * q : D * q + D]

        by_core(pos, arrange)
        meet()
        by_core(pos, lambda c: gather.swap(0, c).start())
        vector.start(0)
        for i in range(1, len(PARTS)):
            by_core(pos, lambda c, i=i: gather.swap(i, c).start())
        run((0, -1), (1, -1))
    else:
        c_wp = load(1, wp_hbm, wp)
        c_w = [load(2 + u, wg_hbm.at[u], wg.at[u]) for u in range(12)]
    c_cot = load(14, cot_hbm, cot)
    fill_patterns(seg_ref, kpat, qpat)
    run(("v", 0), (0, 0), ("v", 1), (2, -1), (1, 0), (3, -1), ("v", 2), (0, 1))
    if fast:
        for i in range(VEC // 128):
            svec[0:1, 128 * i : 128 * i + 128] = sv_held[3, i : i + 1, :]
    c_feat.wait()
    need(0)

    @pl.loop(0, NT)
    def _(t):
        rows = rows_of(t)
        normed = norm0(feat, svec, rows)[2]
        h = (mm(normed, wp[...].reshape(FEAT, D)) + piece(svec, "bp")) * keep_row(D, width)
        hid[rows, :] = h
        low = h.astype(BF16)
        hl[rows, :] = low
        hlt[:, rows] = low.T

    save(hlt, hlt_out)
    run((2, 0), (1, 1), (3, 0), (4, -1), (5, -1))
    need(1)

    slots = [
        [[], [(2, 1), (3, 1)]],
        [[(4, 0), (6, -1)], [(5, 0), (7, -1), (4, 1), (2, 2)]],
        [[], [(6, 0), (8, -1)]],
        [[(4, 2), (5, 1), (7, 0)], []],
        [[], [(6, 1), (8, 0)]],
        [[(7, 1)], [(5, 2)]],
    ]

    def at_slot(p, e):
        if fast:
            for i in range(PAIRS):
                if slots[i][e]:

                    @pl.when(p == i)
                    def _(i=i):
                        run(*slots[i][e])

    @pl.loop(0, PAIRS)
    def _(p):
        for j in range(3):

            @pl.when(p == 2 * j)
            def _(j=j):
                if j:
                    need(1 + j)

        @pl.when(lax.rem(p, 2) == 0)
        def _():
            j = lax.div(p, 2)
            group = lanes_of(j, 256)

            @pl.loop(0, NT)
            def _(t):
                rows = rows_of(t)
                keep = keep_row(256, cfg_ref[0, 1] * HDIM - j * 256)
                o = mm(hl[rows, :], square(wg, j))
                bias = lambda name: svec[0:1, pl.ds(pl.multiple_of(OFFSETS[name] + j * 256, 128), 256)]
                qkv[0, rows, group] = ((o[:, 0:256] + bias("bq")) * keep).astype(BF16)
                k = (o[:, 256:512] * keep).astype(BF16)
                qkv[1, rows, group] = k
                v = ((o[:, 512:768] + bias("bv")) * keep).astype(BF16)
                qkv[2, rows, group] = v
                down = pl.ds(pl.multiple_of(j * 256, 256), 256)
                kt[down, rows] = k.T
                vt[down, rows] = v.T

        if fast:

            @pl.when(p == 2)
            def _():
                run((3, 2))

        lanes = lanes_of(p)
        for e in range(2):
            kaug = qkv[1, :, lanes] * half_mask(e) + kpat[e]
            head_rows = pl.ds(pl.multiple_of(p * 128 + 64 * e, 64), 64)
            for b in range(NT):
                lo, hi = KEY_RANGE[b]
                cols = slice(b * TILE, (b + 1) * TILE)
                qaug = qkv[0, cols, lanes] * (half_mask(e) * 0.125) + qpat[e, cols, :]
                st = mm_nt(kaug[lo:hi], qaug)
                peak = jnp.max(st, 0, keepdims=True)
                power = jnp.exp(st - peak)
                total = col_sum(power)
                ot = mm(vt[head_rows, lo:hi], power.astype(BF16))
                mixedt[head_rows, cols] = (ot * (1.0 / total)).astype(BF16)
                lse_out[pl.ds(2 * p + e, 1), cols] = peak + jnp.log(total)
            at_slot(p, e)

    save(qkv, qkv_out)
    save(kt, kt_out)
    save(mixedt, mixedt_out)
    need(4)

    @pl.loop(0, NT)
    def _(t):
        rows = rows_of(t)
        keep = keep_row(D, width)
        mix = mixedt[:, rows].T
        mixed[rows, :] = mix
        z = hid[rows, :] + (mm(mix, square(wg, 3)) + piece(svec, "bo")) * keep
        centred = (z - row_sum(z * keep) * count) * keep
        inv = lax.rsqrt(row_sum(centred * centred) * count + NORM_EPS)
        hat = centred * inv
        first = (hat * piece(svec, "g1") + piece(svec, "c1")) * keep
        xh1[rows, :] = hat.astype(BF16)
        inv1_out[rows, :] = jnp.broadcast_to(inv, (TILE, 128))
        hid[rows, :] = first + piece(svec, "b2") * keep
        low = first.astype(BF16)
        fl[rows, :] = low
        flt[:, rows] = low.T

    save(mixed, mixed_out)
    save(xh1, xh1_out)
    save(flt, flt_out)
    need(5)

    def up(q):
        @pl.loop(0, LEN // 512)
        def _(t):
            rows = span_of(t, 512)
            u = (mm(fl[rows, :], square(wg, 4 + q)) + piece(svec, "b1", q * D, D)) * keep_row(
                D, cfg_ref[0, 2], q * D
            )
            g, slope = gelu_both(u)
            active[q, rows, :] = g.astype(BF16)
            gp[q, rows, :] = slope.astype(BF16)

        save(active, active_out, q)
        save(gp, gp_out, q)

    def down(q):
        hid[...] += mm_nt(active[q], square(wg, 8 + q)) * keep_row(D, width)

    up(0)
    run((8, 1), (6, 2))
    up(1)
    need(6)
    up(2)
    run((7, 2))
    up(3)
    need(7)
    down(0)
    down(1)
    run((8, 2))
    need(8)
    down(2)
    down(3)
    c_cot.wait()
    zero = jnp.zeros((1, D), F32)

    def last(t, sums):
        gain_sum, shift_sum, bias_sum = sums
        rows = rows_of(t)
        keep = keep_row(D, width)
        z = hid[rows, :]
        centred = (z - row_sum(z * keep) * count) * keep
        inv = lax.rsqrt(row_sum(centred * centred) * count + NORM_EPS)
        hat = centred * inv
        gain = piece(svec, "g2")
        act[rows, :] = ((hat * gain + piece(svec, "c2")) * keep).astype(BF16)
        g = cot[rows, :].astype(F32) * keep
        gain_sum = gain_sum + col_sum(g * hat)
        shift_sum = shift_sum + col_sum(g)
        a = g * gain
        d2 = inv * (a - keep * (row_sum(a) * count) - hat * (row_sum(a * hat) * count))
        hid[rows, :] = d2
        low = d2.astype(BF16)
        dg[rows, :] = low
        dgt[:, rows] = low.T
        return gain_sum, shift_sum, bias_sum + col_sum(low.astype(F32))

    sums = (zero, zero, zero)
    for h in range(2):
        sums = lax.fori_loop(NT // 2 * h, NT // 2 * (h + 1), last, sums)
        rows = pl.ds(LEN // 2 * h, LEN // 2)
        save(act, act_out, rows)
        save(hid, d2_out, rows)
        save(dg, dg_out, rows)
        save(dgt, dgt_out, (slice(None), rows))
    sg_out[...] = jnp.zeros((88, 128), F32)
    for name, value in zip(("g2", "c2", "b2"), sums):
        put(sg_out, name, value)
    if fast:
        gather.finish()
        vector.finish()
    for make in outs:
        make().wait()


R_PARTS = [("u", 8), ("u", 4), ("u", 10), ("u", 6), ("h", 3), ("h", 0), ("h", 1), ("h", 2), ("p", 0)]
R_PLAIN = ((("x",), ("y",), Z), (("y",), ("x",), Z))
R_SHORT = ((("x", "y"), Z),) * 2
R_ROUTES = [R_PLAIN] * 7 + [R_SHORT] * 2


class Scatter:
    def __init__(self, pos, acc, got, given, first, fin, gout, goutp, send, recv, local, credit):
        self.pos, self.acc, self.got, self.given, self.first = pos, acc, got, given, first
        self.fin, self.gout, self.goutp = fin, gout, goutp
        self.send, self.recv, self.local, self.credit = send, recv, local, credit

    def trim(self, i):
        kind = R_PARTS[i][0]
        if kind == "u":
            return ()
        return (slice(0, 32 if kind == "p" else 48), slice(0, 384))

    def held(self, bufs, i, index):
        kind = R_PARTS[i][0]
        if kind == "p":
            return bufs[2].at[index]
        if kind == "h":
            return bufs[1].at[(i - 4,) + index]
        return bufs[0].at[(i,) + index]

    def slot(self, buf, i):
        full = (slice(None),) * 4
        return buf.at[(i % 2,) + full + self.trim(i)]

    def hand(self, i):
        return remote(
            self.slot(self.given, i), self.slot(self.first, i), self.send.at[i, 6], self.recv.at[i, 6],
            partner(self.pos, ("c",)),
        )

    def hops(self, i, s, c):
        route = R_ROUTES[i][c]
        first = sum(len(subsets(dims)) for dims in route[:s])
        rest = sum(route[s + 1 :], ())
        dst = self.held(self.got, i, cube(self.pos, rest, sum(route[: s + 1], ())))
        return [
            remote(
                self.held(self.acc, i, cube(self.pos, rest, dims)), dst,
                self.send.at[i, first + n], self.recv.at[i, first + n], partner(self.pos, dims),
            )
            for n, dims in enumerate(subsets(route[s]))
        ]

    def came(self, i, s, c):
        route = R_ROUTES[i][c]
        rest = sum(route[s + 1 :], ())
        before = sum(route[:s], ())
        return [
            self.held(self.got, i, cube(self.pos, rest, before + tuple(d for d in route[s] if d not in dims)))
            for dims in subsets(route[s])
        ]

    def offer(self, i):
        if i >= 2:
            pl.semaphore_wait(self.credit, 1)
        self.hand(i).start()

    def reuse(self, i):
        if i >= 2:
            self.hand(i - 2).wait_send()

    def begin(self, i):
        self.hand(i).wait_recv()
        mine = self.held(self.acc, i, (slice(None),) * 4)
        mine[...] = mine[...] + self.slot(self.first, i)[...]
        if i < len(R_PARTS) - 2:
            pl.semaphore_signal(
                self.credit, inc=1, device_id=partner(self.pos, ("c",)),
                device_id_type=pl.DeviceIdType.MESH,
            )

        def action(c):
            for copy in self.hops(i, 0, c):
                copy.start()

        by_core(self.pos, action)

    def ends(self, i, c, own):
        kind, u = R_PARTS[i]
        rows = 16 if kind == "p" else 24
        fin = self.held(self.fin, i, ())
        if kind == "p":
            dst = self.goutp.at[:, half(c)]
        elif kind == "h":
            dst = self.gout.at[u, :, half(c)]
        else:
            dst = self.gout.at[u + c]
        if own:
            return pltpu.make_async_copy(fin.at[pl.ds(rows * c, rows)], dst, self.local.at[i])
        return remote(
            fin.at[pl.ds(rows * (1 - c), rows)], dst, self.send.at[i, 7], self.recv.at[i, 7],
            partner(self.pos, ("c",)),
        )

    def step(self, i, s):
        def action(c):
            route = R_ROUTES[i][c]
            for copy in self.hops(i, s, c):
                copy.wait_recv()
            mine = self.held(self.acc, i, cube(self.pos, sum(route[s + 1 :], ())))
            total = mine[...].astype(F32)
            for came in self.came(i, s, c):
                total = total + came[...].astype(F32)
            if s < len(route) - 1:
                mine[...] = total.astype(BF16)
                for copy in self.hops(i, s + 1, c):
                    copy.start()
            else:
                self.held(self.fin, i, ())[...] = total
                for own in (True, False):
                    self.ends(i, c, own).start()

        by_core(self.pos, action)

    def finish(self):
        n = len(R_PARTS)
        for i in range(n - 2, n):
            self.hand(i).wait_send()

        def action(c):
            for i in range(n):
                for s in range(len(R_ROUTES[i][c])):
                    for copy in self.hops(i, s, c):
                        copy.wait_send()
                self.ends(i, c, True).wait()
                self.ends(i, c, False).wait_send()
                self.ends(i, 1 - c, False).wait_recv()

        by_core(self.pos, action)


def backward_kernel(fast, *refs):
    refs = list(refs)
    take = lambda n: [refs.pop(0) for _ in range(n)]
    seg_ref, cfg_ref, feat_hbm, wg_hbm, wp_hbm, svec = take(6)
    (
        hlt_hbm, qkv_hbm, kt_hbm, mixed_hbm, mixedt_hbm, xh1_hbm, inv1_hbm, flt_hbm,
        active_hbm, gp_hbm, d2_hbm, dg_hbm, dgt_hbm, lse, sg_in,
    ) = take(15)
    dx_out, gu_out, gwp_out, sg = take(4)
    (
        feat, wbuf, wp, pool, tr, kt, qkv, go, inv1, fg, dg, tg, delta, dqt, kpat, qpat,
        acc_u, acc_h, acc_p, given, sem_in, sem_q, sem_dx,
    ) = take(23)
    if fast:
        (
            got_u, got_h, got_p, first_in, fin_u, fin_h, fin_p, r_send, r_recv, r_local, credit,
            sv_held, sv_got, v_send, v_recv,
        ) = take(15)
        pos = here()
        core = pos["c"]
        small = sv_held.at[0]
        scatter = Scatter(
            pos, (acc_u, acc_h, acc_p), (got_u, got_h, got_p), given, first_in, (fin_u, fin_h, fin_p),
            gu_out, gwp_out, r_send, r_recv, r_local, credit,
        )
        late, early = (
            VectorSum(pos, rows, sv_held, sv_got, v_send.at[i], v_recv.at[i])
            for i, rows in enumerate((slice(0, 32), slice(32, 88)))
        )
    else:
        sem_out = take(1)[0]
        core = lax.axis_index("dp") % 2
        small = sg
        holder = Scatter(None, (acc_u, acc_h, acc_p), *[None] * 10)

    def load(i, src, dst):
        copy = pltpu.make_async_copy(src, dst, sem_in.at[i])
        copy.start()
        return copy

    def run(*steps):
        if fast:
            for i, s in steps:
                if i == "e":
                    early.step(s)
                elif i == "l":
                    late.step(s)
                elif s < 0:
                    scatter.begin(i)
                else:
                    scatter.step(i, s)

    def columns(h):
        return pl.ds(pl.multiple_of(384 * h, 128), 384)

    def plain_copy(i, mine):
        kind, u = R_PARTS[i]
        which = core if mine else 1 - core
        full = (slice(None),) * 4
        if mine:
            src = holder.held(holder.acc, i, full)
        else:
            src = given.at[(i % 2,) + full + holder.trim(i)]
        if kind == "p":
            dst = gwp_out.at[full + (slice(None), columns(which))]
        elif kind == "h":
            dst = gu_out.at[(u,) + full + (slice(None), columns(which))]
        else:
            dst = gu_out.at[u + which]
        return pltpu.make_async_copy(src, dst, sem_out.at[i, 1 if mine else 0])

    def make(i, mine, left, right):
        if not mine:
            if fast:
                scatter.reuse(i)
            elif i >= 2:
                plain_copy(i - 2, False).wait()
        value = mm(left[...], right[...]).astype(BF16).reshape(CUBE + (48, D))
        if mine:
            acc_u[i] = value
        else:
            given[i % 2] = value
        if fast:
            if not mine:
                scatter.offer(i)
        else:
            plain_copy(i, mine).start()

    def make_both(i, left, right):
        kind = R_PARTS[i][0]
        rows = 32 if kind == "p" else 48
        if fast:
            scatter.reuse(i)
        elif i >= 2:
            plain_copy(i - 2, False).wait()

        def action(c):
            @pl.loop(0, 2)
            def _(y):
                value = mm(left[span_of(y, 8 * rows), :], right[...]).astype(BF16)
                mine = value[:, half(c)].reshape(2, 2, 2, rows, 384)
                given[(i % 2, y) + (slice(None),) * 3 + (slice(0, rows), slice(0, 384))] = value[
                    :, half(1 - c)
                ].reshape(2, 2, 2, rows, 384)
                if kind == "p":
                    acc_p[y] = mine
                else:
                    acc_h[i - 4, y] = mine

        by_core(dict(c=core), action)
        if fast:
            scatter.offer(i)
        else:
            plain_copy(i, False).start()
            plain_copy(i, True).start()

    def quarter(k):
        s = k % 2
        q = 2 * (k // 2) + (core if k % 2 else 1 - core)
        pairs = [
            (active_hbm.at[q], pool.at[s]),
            (wg_hbm.at[8 + q], wbuf.at[s]),
            (gp_hbm.at[q], pool.at[2 + s]),
            (wg_hbm.at[4 + q], wbuf.at[2 + s]),
        ]
        return q, [
            pltpu.make_async_copy(src, dst, sem_q.at[s, i]) for i, (src, dst) in enumerate(pairs)
        ]

    dgt, flt, ig = tr.at[0], tr.at[1], pool.at[4]
    if fast:
        greet(pos)
    c_dgt = load(0, dgt_hbm, dgt)
    for copy in quarter(0)[1]:
        copy.start()
    c_dg = load(1, dg_hbm, dg)

    width = cfg_ref[0, 0]
    count = 1.0 / width.astype(F32)
    small[...] = sg_in[...]
    fill_patterns(seg_ref, kpat, qpat)
    c_dgt.wait()
    if fast:
        meet()
    events = {(1, 0): [(0, -1)], (1, 2): [(1, -1)], (3, 0): [(2, -1)], (3, 2): [(3, -1)]}
    for k in range(4):
        s = k % 2
        mine = bool(k % 2)
        q, copies = quarter(k)
        at = lambda n: run(*events.get((k, n), []))
        copies[0].wait()
        if k == 0:
            c_flt = load(2, flt_hbm, flt)
            c_d2 = load(3, d2_hbm, fg)
        make(2 * (k // 2), mine, dgt, pool.at[s])
        at(0)
        if k == 0:
            c_dg.wait()
            for copy in quarter(1)[1]:
                copy.start()
        if k == 1:
            c_xh1 = load(4, xh1_hbm, go)
            c_inv1 = load(5, inv1_hbm, inv1)
            c_mixed = load(6, mixed_hbm, pool.at[5])
        if k == 2:
            c_qkv = load(9, qkv_hbm, qkv)
            c_kt = load(10, kt_hbm, kt)
        if k == 3:
            c_wp = load(15, wp_hbm, wp)
            c_feat = load(16, feat_hbm, feat)
        copies[1].wait()
        copies[2].wait()

        def inner(t, bias, q=q, s=s):
            rows = span_of(t, 512)
            low = (
                mm(dg[rows, :], square(wbuf, s))
                * pool[2 + s, rows, :].astype(F32)
                * keep_row(D, cfg_ref[0, 2] - q * D)
            ).astype(BF16)
            ig[rows, :] = low
            return bias + col_sum(low.astype(F32))

        put(small, "b1", lax.fori_loop(0, LEN // 512, inner, jnp.zeros((1, D), F32)), q * D)
        at(1)
        if k == 0:
            c_flt.wait()
            c_d2.wait()
        make(2 * (k // 2) + 1, mine, flt, ig)
        at(2)
        copies[3].wait()

        fg[...] += mm_nt(ig[...], square(wbuf, 2 + s))
        at(3)
        if k < 2:
            for copy in quarter(k + 2)[1]:
                copy.start()
        if k == 2:
            c_wo = load(8, wg_hbm.at[3], wbuf.at[0])
            c_wa = [load(12, wg_hbm.at[0], wbuf.at[2])]

    mixedt, hlt, mixed = tr.at[0], tr.at[1], pool.at[5]
    c_mixedt = load(7, mixedt_hbm, mixedt)
    c_hlt = load(11, hlt_hbm, hlt)
    c_wa.append(load(13, wg_hbm.at[1], wbuf.at[1]))
    c_wa.append(load(14, wg_hbm.at[2], wbuf.at[3]))
    wa_slot = (2, 1, 3)
    for copy in (c_xh1, c_inv1, c_mixed, c_wo):
        copy.wait()
    zero = jnp.zeros((1, D), F32)

    def middle(t, sums):
        gain_sum, shift_sum, bias_sum = sums
        rows = rows_of(t)
        keep = keep_row(D, width)
        hat = go[rows, :].astype(F32)
        g = fg[rows, :] * keep
        gain_sum = gain_sum + col_sum(g * hat)
        shift_sum = shift_sum + col_sum(g)
        a = g * piece(svec, "g1")
        d1 = inv1[rows, 0:1] * (a - keep * (row_sum(a) * count) - hat * (row_sum(a * hat) * count))
        fg[rows, :] = d1
        low = d1.astype(BF16)
        dg[rows, :] = low
        mg = mm_nt(low, square(wbuf, 0)).astype(BF16)
        go[rows, :] = mg
        product = mg.astype(F32) * mixed[rows, :].astype(F32)
        high = product.astype(BF16)
        rest = (product - high.astype(F32)).astype(BF16)
        lane = lax.broadcasted_iota(jnp.int32, (16, D), 1)
        head = lax.broadcasted_iota(jnp.int32, (16, D), 0)
        pick = ((lane >= head * HDIM) & (lane < head * HDIM + HDIM)).astype(F32).astype(BF16)
        delta[:, rows] = mm_nt(pick, high) + mm_nt(pick, rest)
        return gain_sum, shift_sum, bias_sum + col_sum(low.astype(F32))

    gain_sum, shift_sum, bias_sum = lax.fori_loop(0, NT, middle, (zero, zero, zero))
    put(small, "g1", gain_sum)
    put(small, "c1", shift_sum)
    put(small, "bo", bias_sum)
    if fast:
        early.start()
    run((0, 0))
    c_mixedt.wait()
    make_both(4, mixedt, dg)

    c_qkv.wait()
    c_kt.wait()
    c_hlt.wait()
    for copy in c_wa:
        copy.wait()
    slots = [
        [[], [(1, 0)], [(4, -1), ("e", 0)], []],
        [[], [(4, 0), (3, 0), (1, 1), (5, -1)], [("e", 2)], []],
        [[], [(3, 1), (6, -1)], [(1, 2), (4, 2)], []],
    ]
    after_loop = [[], [], [(5, 1)]]
    after_make = [[("e", 1), (0, 1), (2, 0)], [(4, 1), (2, 1)], []]
    after_back = [[], [(5, 0), (0, 2)], [(6, 0), (2, 2)]]

    def chunk(n):
        return n // 3, slice(256 * (n % 3), 256 * (n % 3) + 256)

    for j in range(3):

        def at_slot(pp, e, j=j):
            if fast:
                for i in range(2):
                    steps = slots[j][2 * i + e]
                    if steps:

                        @pl.when(pp == i)
                        def _(steps=steps):
                            run(*steps)

        @pl.loop(0, 2)
        def _(pp, j=j):
            p = j * 2 + pp
            lanes = lanes_of(p)
            for e in range(2):
                at_slot(pp, e)
                kaug = qkv[1, :, lanes] * half_mask(e) + kpat[e]
                head_rows = pl.ds(pl.multiple_of(p * 128 + 64 * e, 64), 64)
                for b in range(NT):
                    lo, hi = KEY_RANGE[b]
                    cols = slice(b * TILE, (b + 1) * TILE)
                    qaug = qkv[0, cols, lanes] * (half_mask(e) * 0.125) + qpat[e, cols, :]
                    st = mm_nt(kaug[lo:hi], qaug)
                    weights = jnp.exp(st - lse[pl.ds(2 * p + e, 1), cols])
                    n, span = chunk(4 * e + b)
                    pool[n, lo:hi, span] = weights.astype(BF16)
                    goe = go[cols, lanes] * half_mask(e)
                    dp = mm_nt(qkv[2, lo:hi, lanes], goe)
                    ds = (weights * (dp - delta[pl.ds(2 * p + e, 1), cols])).astype(BF16)
                    n, span = chunk(8 + 4 * e + b)
                    pool[n, lo:hi, span] = ds
                    dqt[64 * e : 64 * e + 64, cols] = mm(kt[head_rows, lo:hi], ds)
            keep = keep_row(128, cfg_ref[0, 1] * HDIM - p * 128)
            for t in range(NT):
                rows = slice(t * TILE, (t + 1) * TILE)
                dk = jnp.zeros((TILE, 128), F32)
                dv = jnp.zeros((TILE, 128), F32)
                for b in range(NT):
                    if not KEY_RANGE[b][0] <= t * TILE < KEY_RANGE[b][1]:
                        continue
                    cols = slice(b * TILE, (b + 1) * TILE)
                    for e in range(2):
                        n, span = chunk(8 + 4 * e + b)
                        dk = dk + mm(pool[n, rows, span], qkv[0, cols, lanes] * half_mask(e))
                        n, span = chunk(4 * e + b)
                        dv = dv + mm(pool[n, rows, span], go[cols, lanes] * half_mask(e))
                dq = dqt[:, rows].T
                for i, value in enumerate((dq * (keep * 0.125), dk * (keep * 0.125), dv * keep)):
                    tg[rows, pl.ds(pl.multiple_of(256 * i + pp * 128, 128), 128)] = value.astype(BF16)

        run(*after_loop[j])
        make_both(5 + j, hlt, tg)
        run(*after_make[j])

        fg[...] += mm_nt(tg[...], square(wbuf, wa_slot[j]))
        bias = lax.fori_loop(
            0, NT, lambda t, total: total + col_sum(tg[rows_of(t), :].astype(F32)), zero
        )
        put(small, "bq", bias[:, 0:256], 256 * j)
        put(small, "bv", bias[:, 512:768], 256 * j)
        run(*after_back[j])

    c_wp.wait()
    c_feat.wait()
    zero_feat = jnp.zeros((1, FEAT), F32)
    nrmt = tr.at[0]

    def first(t, bias_sum):
        rows = rows_of(t)
        nrmt[0:FEAT, rows] = norm0(feat, svec, rows)[2].T
        low = (fg[rows, :] * keep_row(D, width)).astype(BF16)
        dg[rows, :] = low
        return bias_sum + col_sum(low.astype(F32))

    put(small, "bp", lax.fori_loop(0, NT, first, zero))
    run((7, -1))
    make_both(8, nrmt, dg)

    def second(t, sums):
        gain_sum, shift_sum = sums
        rows = rows_of(t)
        hat, inv, _ = norm0(feat, svec, rows)
        g = mm_nt(dg[rows, :], wp[...].reshape(FEAT, D))
        gain_sum = gain_sum + col_sum(g * hat)
        shift_sum = shift_sum + col_sum(g)
        a = g * piece(svec, "g0")
        dx = inv * (a - row_sum(a) * (1.0 / FEAT) - hat * (row_sum(a * hat) * (1.0 / FEAT)))
        fg[rows, 0:FEAT] = 0.1 * dx
        return gain_sum, shift_sum

    gain_sum, shift_sum = lax.fori_loop(0, NT, second, (zero_feat, zero_feat))
    put(small, "g0", gain_sum)
    put(small, "b0", shift_sum)
    c_dx = pltpu.make_async_copy(fg.at[:, 0:FEAT], dx_out, sem_dx)
    c_dx.start()
    if fast:
        late.start()
        run((3, 2), (5, 2), (8, -1), (6, 1), ("l", 0), (7, 0), (8, 0), (6, 2), ("l", 1), (8, 1), (7, 1), ("l", 2))
        sg[...] = sv_held[3]
        early.finish()
        late.finish()
        scatter.finish()
    else:
        for i in range(len(R_PARTS)):
            plain_copy(i, True).wait()
        for i in range(len(R_PARTS) - 2, len(R_PARTS)):
            plain_copy(i, False).wait()
    c_dx.wait()


def adam_rule(weight, moment, square_in, grad, rate):
    moment_new = BETA_ONE * moment + (1.0 - BETA_ONE) * grad
    square_new = BETA_TWO * square_in + (1.0 - BETA_TWO) * grad * grad
    fix_one = 1.0 - BETA_ONE**STEP
    fix_two = 1.0 - BETA_TWO**STEP
    direction = moment_new / fix_one / (jnp.sqrt(square_new / fix_two) + ADAM_EPS)
    return (moment_new, square_new, weight - rate * (direction + DECAY * weight))


def adam_kernel(*refs):
    gu_hbm, gp_hbm, act_hbm, dx_hbm = refs[0:4]
    ins, act_out, dx_out, outs = refs[4:16], refs[16], refs[17], refs[18:34]
    gu, gp, act, dx = refs[34:38]
    held, new = refs[38:50], refs[50:62]
    sem_in, sem_out = refs[62:]
    sources = (gu_hbm,) + tuple(ins[9:12]) + (act_hbm, dx_hbm, gp_hbm) + tuple(ins[0:9])
    places = (gu,) + tuple(held[9:12]) + (act, dx, gp) + tuple(held[0:9])
    loads = [
        pltpu.make_async_copy(src, dst, sem_in.at[i]) for i, (src, dst) in enumerate(zip(sources, places))
    ]
    for copy in loads:
        copy.start()
    stores = []

    def store(src, dst):
        copy = pltpu.make_async_copy(src, dst, sem_out.at[len(stores)])
        copy.start()
        stores.append(copy)

    def update(k, pieces):
        w, m, v = held[3 * k : 3 * k + 3]
        for index, grad in pieces:
            done = adam_rule(w[index], m[index], v[index], grad(), RATE)
            for ref, value in zip(new[3 * k : 3 * k + 3], done):
                ref[index] = value
            m[index] = grad()
        for src, dst in zip((m,) + tuple(new[3 * k : 3 * k + 3]), outs[4 * k : 4 * k + 4]):
            store(src, dst)

    everything = (slice(None), slice(None))
    for copy in loads[0:4]:
        copy.wait()
    update(
        3,
        [
            ((i, slice(None), slice(D * q, D * q + D)), lambda i=i, q=q: gu[4 + 4 * i + q])
            for i in range(2) for q in range(4)
        ],
    )
    for copy in loads[4:6]:
        copy.wait()
    store(act, act_out)
    store(dx, dx_out)
    for copy in loads[6:16]:
        copy.wait()
    update(
        1,
        [
            ((i, slice(None), slice(256 * j, 256 * j + 256)), lambda i=i, j=j: gu[j, :, 256 * i : 256 * i + 256])
            for i in range(3) for j in range(3)
        ],
    )
    update(2, [(everything, lambda: gu[3])])
    update(0, [(everything, lambda: gp[...])])
    for copy in stores:
        copy.wait()


def adam_call(gu, gp, act, dx, state):
    shape = jax.ShapeDtypeStruct
    f32 = lambda s: pltpu.VMEM(s, F32)
    outs = [shape((LEN, D), BF16), shape((LEN, FEAT), F32)]
    outs += [shape(state[3 * k].shape, F32) for k in range(4) for _ in range(4)]
    scratch = [f32(gu.shape), f32(gp.shape), pltpu.VMEM((LEN, D), BF16), f32((LEN, FEAT))]
    scratch += [f32(x.shape) for x in state] * 2
    scratch += [pltpu.SemaphoreType.DMA((16,)), pltpu.SemaphoreType.DMA((18,))]
    return pl.pallas_call(
        adam_kernel,
        out_shape=outs,
        in_specs=[any_spec()] * 16,
        out_specs=[any_spec()] * 18,
        scratch_shapes=scratch,
        compiler_params=pltpu.CompilerParams(vmem_limit_bytes=VMEM_LIMIT),
        name="adam",
    )(gu, gp, act, dx, *state)


def any_spec():
    return pl.BlockSpec(memory_space=pl.ANY)


def vmem_spec():
    return pl.BlockSpec(memory_space=pltpu.VMEM)


def smem_spec():
    return pl.BlockSpec(memory_space=pltpu.SMEM)


def forward_call(fast, seg, cfg, feat, cot, weights):
    shape = jax.ShapeDtypeStruct
    outs = [
        (shape((LEN, D), BF16), any_spec()),
        (shape((D, LEN), BF16), any_spec()),
        (shape((3, LEN, D), BF16), any_spec()),
        (shape((D, LEN), BF16), any_spec()),
        (shape((LEN, D), BF16), any_spec()),
        (shape((D, LEN), BF16), any_spec()),
        (shape((LEN, D), BF16), any_spec()),
        (shape((LEN, 128), F32), vmem_spec()),
        (shape((D, LEN), BF16), any_spec()),
        (shape((4, LEN, D), BF16), any_spec()),
        (shape((4, LEN, D), BF16), any_spec()),
        (shape((LEN, D), F32), any_spec()),
        (shape((LEN, D), BF16), any_spec()),
        (shape((D, LEN), BF16), any_spec()),
        (shape((16, LEN), F32), vmem_spec()),
        (shape((88, 128), F32), vmem_spec()),
    ]
    if fast:
        outs += [
            (shape((12,) + CUBE + (48, D), BF16), any_spec()),
            (shape(CUBE + (32, D), BF16), any_spec()),
            (shape((1, VEC), F32), vmem_spec()),
        ]
    bf = lambda *s: pltpu.VMEM(s, BF16)
    f32 = lambda *s: pltpu.VMEM(s, F32)
    dma = lambda *s: pltpu.SemaphoreType.DMA(s)
    scratch = [
        bf(LEN, FEAT), bf(LEN, D), bf(12, *CUBE, 48, D), bf(*CUBE, 32, D), f32(LEN, D),
        bf(LEN, D), bf(D, LEN), bf(3, LEN, D), bf(D, LEN), bf(D, LEN), bf(LEN, D), bf(D, LEN),
        bf(LEN, D), bf(LEN, D), bf(D, LEN), bf(4, LEN, D), bf(4, LEN, D), bf(LEN, D), bf(D, LEN),
        bf(2, LEN, 128), bf(2, LEN, 128), dma(15), dma(32),
    ]
    if fast:
        scratch += [
            f32(16, D), f32(3, 24, D), f32(24, D), f32(2, 24, FF), f32(12, 48, D), f32(32, D), dma(5),
            dma(len(PARTS), 11), dma(len(PARTS), 11), f32(4, 88, 128), f32(7, 88, 128), dma(7), dma(7),
        ]
        specs = [any_spec()] * len(weights)
        params = dict(collective_id=0, has_side_effects=True)
    else:
        specs = [any_spec()] * 2 + [vmem_spec()]
        params = {}
    return pl.pallas_call(
        functools.partial(forward_kernel, fast),
        out_shape=[o[0] for o in outs],
        in_specs=[smem_spec(), smem_spec()] + [any_spec()] * 2 + specs,
        out_specs=[o[1] for o in outs],
        scratch_shapes=scratch,
        compiler_params=pltpu.CompilerParams(vmem_limit_bytes=VMEM_LIMIT, **params),
        name="forward",
    )(seg, cfg, feat, cot, *weights)


def backward_call(fast, seg, cfg, feat, wg, wp, svec, saved):
    shape = jax.ShapeDtypeStruct
    bf = lambda *s: pltpu.VMEM(s, BF16)
    f32 = lambda *s: pltpu.VMEM(s, F32)
    dma = lambda *s: pltpu.SemaphoreType.DMA(s)
    n = len(R_PARTS)
    scratch = [
        bf(LEN, FEAT), bf(4, *CUBE, 48, D), bf(*CUBE, 32, D), bf(6, LEN, D), bf(2, D, LEN), bf(D, LEN),
        bf(3, LEN, D), bf(LEN, D), f32(LEN, 128), f32(LEN, D), bf(LEN, D), bf(LEN, D), f32(16, LEN),
        f32(128, LEN), bf(2, LEN, 128), bf(2, LEN, 128),
        bf(4, *CUBE, 48, D), bf(4, *CUBE, 48, 384), bf(*CUBE, 32, 384), bf(2, *CUBE, 48, D),
        dma(17), dma(2, 4), pltpu.SemaphoreType.DMA,
    ]
    if fast:
        scratch += [
            bf(4, *CUBE, 48, D), bf(4, *CUBE, 48, 384), bf(*CUBE, 32, 384), bf(2, *CUBE, 48, D),
            f32(4, 48, D), f32(4, 48, 384), f32(32, 384), dma(n, 8), dma(n, 8), dma(n),
            pltpu.SemaphoreType.REGULAR, f32(4, 88, 128), f32(7, 88, 128), dma(2, 7), dma(2, 7),
        ]
        grads = [shape((12, 24, D), F32), shape((16, D), F32)]
        params = dict(collective_id=1, has_side_effects=True)
    else:
        scratch += [dma(n, 2)]
        grads = [shape((12,) + CUBE + (48, D), BF16), shape(CUBE + (32, D), BF16)]
        params = {}
    return pl.pallas_call(
        functools.partial(backward_kernel, fast),
        out_shape=[shape((LEN, FEAT), F32)] + grads + [shape((88, 128), F32)],
        in_specs=[smem_spec(), smem_spec()] + [any_spec()] * 3 + [vmem_spec()]
        + [any_spec()] * 13 + [vmem_spec()] * 2,
        out_specs=[any_spec()] * 3 + [vmem_spec()],
        scratch_shapes=scratch,
        compiler_params=pltpu.CompilerParams(vmem_limit_bytes=VMEM_LIMIT, **params),
        name="backward",
    )(seg, cfg, feat, wg, wp, svec, *saved)


AXES = ("grp", "dp")


def gathered(projection_weight, attention_weight, output_weight, feedforward_weight, small_params):
    gather = lambda w, axis: lax.all_gather(w.astype(BF16), AXES, axis=axis, tiled=True)
    wp = gather(projection_weight, 0)
    wa = gather(attention_weight, 1)
    wo = gather(output_weight, 0)
    wf = gather(feedforward_weight, 1)
    svec = gather(small_params, 0).astype(F32).reshape(1, VEC)
    return units(wp, wa, wo, wf) + (svec,)


def units(wp, wa, wo, wf):
    groups = wa.reshape(3, D, 3, 256).transpose(2, 1, 0, 3).reshape(3, D, D)
    quarters = wf.reshape(2, D, 4, D).transpose(0, 2, 1, 3).reshape(8, D, D)
    wg = jnp.concatenate([groups, wo[None], quarters], 0)
    return wg.reshape((12,) + CUBE + (48, D)), wp.reshape(CUBE + (32, D))


def layer(fast, features, lengths, config, cotangent, weights):
    feat = features.reshape(LEN, FEAT)
    cot = cotangent.reshape(LEN, D)
    saved = forward_call(fast, lengths, config, feat, cot, weights)
    activations = saved[0]
    wg, wp, svec = saved[16:] if fast else weights
    dx, gu, gwp, sg = backward_call(fast, lengths, config, feat, wg, wp, svec, saved[1:16])
    return activations, dx, gu, gwp, sg


def per_device(
    fast,
    features, segment_lengths, subnet_config, cotangent,
    projection_weight, projection_moment, projection_square,
    attention_weight, attention_moment, attention_square,
    output_weight, output_moment, output_square,
    feedforward_weight, feedforward_moment, feedforward_square,
    small_params, small_moment, small_square,
):
    weights = (projection_weight, attention_weight, output_weight, feedforward_weight)
    if fast:
        me = lax.axis_index(AXES)
        low = lax.reduce_precision(small_params, 8, 7)
        placed = lax.dynamic_update_slice(jnp.zeros((88 * 128,), F32), low, (me * low.shape[0],))
        weights = weights + (placed.reshape(88, 128),)
    else:
        weights = gathered(*weights, small_params)
    activations, dx, gu, gwp, sg = layer(
        fast, features, segment_lengths, subnet_config, cotangent, weights
    )
    state = (
        projection_weight, projection_moment, projection_square,
        attention_weight, attention_moment, attention_square,
        output_weight, output_moment, output_square,
        feedforward_weight, feedforward_moment, feedforward_square,
        small_params[None], small_moment[None], small_square[None],
    )
    out = [activations.reshape(1, LEN, D), dx.reshape(1, LEN, FEAT)]
    vec = sg.reshape(88 * 128)
    if fast:
        gs = lax.dynamic_slice(vec, (me * small_params.shape[0],), small_params.shape)
        done = adam_call(gu, gwp, activations, dx, state[:12])
        return (
            (done[0].reshape(1, LEN, D), done[1].reshape(1, LEN, FEAT))
            + tuple(done[2:18])
            + (gs,) + adam_rule(small_params, small_moment, small_square, gs, SMALL_RATE)
        )
    gu = gu.reshape(12, D, D).astype(F32)
    scatter = lambda g, dim: lax.psum_scatter(g, AXES, scatter_dimension=dim, tiled=True)
    ga = gu[0:3].reshape(3, D, 3, 256).transpose(2, 1, 0, 3).reshape(3, D, D)
    gf = gu[4:12].reshape(2, 4, D, D).transpose(0, 2, 1, 3).reshape(2, D, FF)
    sums = (
        scatter(gwp.reshape(FEAT, D).astype(F32), 0), scatter(ga, 1), scatter(gu[3], 0), scatter(gf, 1),
        scatter(vec[:VEC], 0)[None],
    )
    for k, g in enumerate(sums):
        new = (g,) + adam_rule(*state[3 * k : 3 * k + 3], g, RATE if k < 4 else SMALL_RATE)
        out.extend(x[0] if k == 4 else x for x in new)
    return tuple(out)


def solution(mesh):
    rows3, rows2, stacked, flat = (
        P(AXES, None, None), P(AXES, None), P(None, AXES, None), P(AXES),
    )
    return jax.shard_map(
        functools.partial(per_device, dict(mesh.shape) == dict(grp=4, dp=8)),
        mesh=mesh,
        in_specs=(
            rows3, rows2, P("grp", None), rows3, rows2, rows2, rows2, stacked, stacked, stacked,
            rows2, rows2, rows2, stacked, stacked, stacked, flat, flat, flat,
        ),
        out_specs=(rows3, rows3) + (rows2,) * 4 + (stacked,) * 4 + (rows2,) * 4 + (stacked,) * 4 + (flat,) * 4,
        check_vma=False,
    )
```

```python
import functools
import math

import jax
import jax.numpy as jnp
from jax import lax
from jax.experimental import pallas as pl
from jax.experimental.pallas import tpu as pltpu
from jax.sharding import PartitionSpec as P

D = 768
FF = 3072
FEAT = 512
HDIM = 64
HEADS = 12
PAIRS = HEADS // 2
LEN = 1024
STEP = 10
TILE = 256
NT = LEN // TILE
VEC = 11008

NORM_EPS = 1e-05
RATE = 0.08
SMALL_RATE = 0.3
BETA_ONE = 0.9
BETA_TWO = 0.999
ADAM_EPS = 1e-08
DECAY = 0.01

F32 = jnp.float32
BF16 = jnp.bfloat16
BIG = 2.0**100
VMEM_LIMIT = 63 << 20

WIDTHS = dict(
    g0=FEAT, b0=FEAT, bp=D, bq=D, bv=D, bo=D, g1=D, c1=D, b1=FF, b2=D, g2=D, c2=D
)
OFFSETS = {}
_at = 0
for _name, _width in WIDTHS.items():
    OFFSETS[_name] = _at
    _at += _width

KEY_RANGE = [
    (max(0, (i * TILE - 511) // TILE * TILE), min(LEN, -(-(i * TILE + TILE + 511) // TILE) * TILE))
    for i in range(NT)
]


def mm(a, b):
    return jnp.dot(a, b, preferred_element_type=F32)


def mm_nt(a, b):
    return lax.dot_general(a, b, (((1,), (1,)), ((), ())), preferred_element_type=F32)


def piece(ref, name, start=0, width=None):
    begin = OFFSETS[name] + start
    return ref[0:1, begin : begin + (width or WIDTHS[name])]


def put(ref, name, value, start=0):
    begin = OFFSETS[name] // 128 + start // 128
    for i in range(value.shape[1] // 128):
        ref[pl.ds(begin + i, 1), :] = value[:, 128 * i : 128 * i + 128]


def keep_row(width, limit, start=0):
    lane = lax.broadcasted_iota(jnp.int32, (1, width), 1) + start
    return (lane < limit).astype(F32)


def col_sum(value):
    return jnp.sum(value, 0, keepdims=True)


def row_sum(value):
    return jnp.sum(value, 1, keepdims=True)


def rows_of(t):
    return pl.ds(pl.multiple_of(t * TILE, TILE), TILE)


def span_of(t, size):
    return pl.ds(pl.multiple_of(t * size, size), size)


def lanes_of(p, width=128):
    return pl.ds(pl.multiple_of(p * width, width), width)


def gelu_both(u):
    half = jnp.exp(-0.5 * u * u)
    t = 1.0 / (1.0 + (0.3275911 * 0.7071067811865476) * jnp.abs(u))
    poly = 0.5 * 1.061405429
    for c in (-1.453152027, 1.421413741, -0.284496736, 0.254829592):
        poly = poly * t + 0.5 * c
    tail = poly * t * half
    cdf = jnp.where(u >= 0.0, 1.0 - tail, tail)
    return u * cdf, cdf + u * (half * 0.3989422804014327)


def fill_patterns(seg_ref, kpat, qpat):
    e0 = seg_ref[0, 0]
    e1 = e0 + seg_ref[0, 1]
    e2 = e1 + seg_ref[0, 2]

    @pl.loop(0, NT)
    def _(t):
        pos = lax.broadcasted_iota(jnp.int32, (TILE, 128), 0) + t * TILE
        lane = lax.broadcasted_iota(jnp.int32, (TILE, 128), 1)
        seg = (
            (pos >= e0).astype(jnp.int32)
            + (pos >= e1).astype(jnp.int32)
            + (pos >= e2).astype(jnp.int32)
        )
        for e in range(2):
            slot = lane - (64 if e == 0 else 0)
            valid = (slot >= 0) & (slot < 4)
            same = slot == seg
            kpat[e, rows_of(t), :] = jnp.where(same, 1.0, 0.0).astype(BF16)
            qpat[e, rows_of(t), :] = jnp.where(valid & (slot != seg), -BIG, 0.0).astype(BF16)


def half_mask(e):
    lane = lax.broadcasted_iota(jnp.int32, (1, 128), 1)
    return ((lane < 64) if e == 0 else (lane >= 64)).astype(F32).astype(BF16)


def norm0(feat, svec, rows):
    x = feat[rows, :].astype(F32)
    centred = x - row_sum(x) * (1.0 / FEAT)
    inv = lax.rsqrt(row_sum(centred * centred) * (1.0 / FEAT) + NORM_EPS)
    hat = centred * inv
    normed = (hat * piece(svec, "g0") + piece(svec, "b0")).astype(BF16)
    return hat, inv, normed


DIMS = ("y", "x", "z1", "z0")
CUBE = (2, 2, 2, 2)


def here():
    g = lax.axis_index("grp")
    d = lax.axis_index("dp")
    return dict(
        y=g // 2, x=g % 2, z1=d // 4, z0=(d // 2) % 2, c=d % 2,
    )


def partner(pos, dims):
    near = {k: (1 - v if k in dims else v) for k, v in pos.items()}
    return (near["y"] * 2 + near["x"], near["z1"] * 4 + near["z0"] * 2 + near["c"])


def cube(pos, full, other=()):
    return tuple(
        slice(None) if dim in full else (1 - pos[dim] if dim in other else pos[dim])
        for dim in DIMS
    )


def subsets(dims):
    return [(d,) for d in dims] + ([tuple(dims)] if len(dims) == 2 else [])


NEAR = [("c",), ("x",), ("y",), ("x", "y"), ("z0",), ("z1",), ("z1", "z0")]


def greet(pos):
    for dims in NEAR:
        pl.semaphore_signal(
            pltpu.get_barrier_semaphore(), inc=1, device_id=partner(pos, dims),
            device_id_type=pl.DeviceIdType.MESH,
        )


def meet():
    pl.semaphore_wait(pltpu.get_barrier_semaphore(), len(NEAR))


def remote(src, dst, send_sem, recv_sem, device):
    return pltpu.make_async_remote_copy(
        src_ref=src, dst_ref=dst, send_sem=send_sem, recv_sem=recv_sem,
        device_id=device, device_id_type=pl.DeviceIdType.MESH,
    )


def by_core(pos, action):
    for c in range(2):
        pl.when(pos["c"] == c)(functools.partial(action, c))


def half(c):
    return slice(384 * c, 384 * c + 384)


PARTS = [("p", 0), ("h", 0), ("h", 1), ("h", 2), ("h", 3), ("u", 4), ("u", 6), ("u", 8), ("u", 10)]
Z = ("z1", "z0")
SHORT = ((Z, ("x", "y")),) * 2
PLAIN = ((Z, ("x",), ("y",)), (Z, ("y",), ("x",)))
ROUTES = [SHORT, SHORT] + [PLAIN] * 7


class Gather:
    def __init__(self, pos, wg, wp, stage, stage_p, send, recv):
        self.pos, self.wg, self.wp = pos, wg, wp
        self.stage, self.stage_p = stage, stage_p
        self.send, self.recv = send, recv

    def view(self, i, c, index):
        kind, u = PARTS[i]
        if kind == "p":
            return self.wp.at[index + (slice(None), half(c))]
        if kind == "h":
            return self.wg.at[(u,) + index + (slice(None), half(c))]
        return self.wg.at[(u + c,) + index]

    def staged(self, i, c, rows):
        kind, u = PARTS[i]
        if kind == "p":
            return self.stage_p.at[rows, half(c)]
        if kind == "h":
            return self.stage.at[u, rows, half(c)]
        return self.stage.at[u + c, rows, :]

    def swap(self, i, c):
        own = pl.ds(16 * c, 16) if PARTS[i][0] == "p" else pl.ds(24 * c, 24)
        view = self.staged(i, 1 - c, own)
        return remote(view, view, self.send.at[i, 10], self.recv.at[i, 10], partner(self.pos, ("c",)))

    def hops(self, i, s, c):
        route = ROUTES[i][c]
        first = sum(len(subsets(dims)) for dims in route[:s])
        view = self.view(i, c, cube(self.pos, sum(route[:s], ())))
        return [
            remote(view, view, self.send.at[i, first + n], self.recv.at[i, first + n], partner(self.pos, dims))
            for n, dims in enumerate(subsets(route[s]))
        ]

    def gives(self, i, late, c):
        route = ROUTES[i][c]
        full = sum(route[:-1], ())
        ways = subsets(route[-1]) if late else [()]
        views = [self.view(i, c, cube(self.pos, full, dims)) for dims in ways]
        return [
            remote(
                view, view, self.send.at[i, 6 + late + n], self.recv.at[i, 6 + late + n],
                partner(self.pos, ("c",)),
            )
            for n, view in enumerate(views)
        ]

    def begin(self, i):
        def action(c):
            other = pl.ds(16 * (1 - c), 16) if PARTS[i][0] == "p" else pl.ds(24 * (1 - c), 24)
            view = self.staged(i, c, other)
            remote(
                view, view, self.send.at[i, 10], self.recv.at[i, 10], partner(self.pos, ("c",))
            ).wait_recv()
            rows = slice(0, 32 if PARTS[i][0] == "p" else 48)
            block = self.view(i, c, cube(self.pos, ()))
            block[...] = self.staged(i, c, rows)[...].astype(BF16)
            for copy in self.hops(i, 0, c):
                copy.start()

        by_core(self.pos, action)

    def step(self, i, s):
        def action(c):
            last = len(ROUTES[i][c]) - 1
            for copy in self.hops(i, s, c):
                copy.wait_recv()
            if s < last:
                for copy in self.hops(i, s + 1, c):
                    copy.start()
            if s >= last - 1:
                for copy in self.gives(i, s - last + 1, c):
                    copy.start()

        by_core(self.pos, action)

    def need(self, i):
        def action(c):
            for late in range(2):
                for copy in self.gives(i, late, 1 - c):
                    copy.wait_recv()

        by_core(self.pos, action)

    def finish(self):
        def action(c):
            for i in range(len(PARTS)):
                self.swap(i, c).wait_send()
                for s in range(len(ROUTES[i][c])):
                    for copy in self.hops(i, s, c):
                        copy.wait_send()
                for late in range(2):
                    for copy in self.gives(i, late, c):
                        copy.wait_send()

        by_core(self.pos, action)


class VectorSum:
    PHASES = (("c",), ("x", "y"), Z)

    def __init__(self, pos, rows, held, got, send, recv):
        self.pos, self.rows, self.held, self.got, self.send, self.recv = pos, rows, held, got, send, recv

    def copies(self, s):
        first = sum(len(subsets(dims)) for dims in self.PHASES[:s])
        return [
            remote(
                self.held.at[s, self.rows], self.got.at[first + n, self.rows],
                self.send.at[first + n], self.recv.at[first + n], partner(self.pos, dims),
            )
            for n, dims in enumerate(subsets(self.PHASES[s]))
        ]

    def start(self, s=0):
        for copy in self.copies(s):
            copy.start()

    def step(self, s):
        first = sum(len(subsets(dims)) for dims in self.PHASES[:s])
        total = self.held[s, self.rows]
        for n, copy in enumerate(self.copies(s)):
            copy.wait_recv()
            total = total + self.got[first + n, self.rows]
        self.held[s + 1, self.rows] = total
        if s < 2:
            self.start(s + 1)

    def finish(self):
        for s in range(3):
            for copy in self.copies(s):
                copy.wait_send()


def square(ref, u):
    return ref[u].reshape(D, D)


def forward_kernel(
    fast,
    *refs,
):
    refs = list(refs)
    take = lambda n: [refs.pop(0) for _ in range(n)]
    seg_ref, cfg_ref, feat_hbm, cot_hbm = take(4)
    if fast:
        own_p, own_a, own_o, own_f, own_s = take(5)
        wg_out, wp_out, svec = None, None, None
    else:
        wg_hbm, wp_hbm, svec = take(3)
    (
        act_out, hlt_out, qkv_out, kt_out, mixed_out, mixedt_out, xh1_out, inv1_out, flt_out,
        active_out, gp_out, d2_out, dg_out, dgt_out, lse_out, sg_out,
    ) = take(16)
    if fast:
        wg_out, wp_out, svec = take(3)
    (
        feat, cot, wg, wp, hid, hl, hlt, qkv, kt, vt, mixed, mixedt, xh1, fl, flt, active, gp, dg, dgt,
        kpat, qpat, sem_in, sem_out,
    ) = take(23)
    if fast:
        raw_p, raw_a, raw_o, raw_f, stage, stage_p, sem_raw, g_send, g_recv, sv_held, sv_got, v_send, v_recv = take(13)
    act = hl
    outs = []

    def load(i, src, dst):
        copy = pltpu.make_async_copy(src, dst, sem_in.at[i])
        copy.start()
        return copy

    def save(src, dst, part=None):
        i = len(outs)
        pick = lambda ref: ref if part is None else ref.at[part]
        make = lambda: pltpu.make_async_copy(pick(src), pick(dst), sem_out.at[i])
        make().start()
        outs.append(make)

    def need(i):
        kind, u = PARTS[i]
        if fast:
            gather.need(i)
            if kind == "p":
                save(wp, wp_out)
            elif kind == "h":
                save(wg, wg_out, u)
            else:
                save(wg, wg_out, pl.ds(u, 2))
        elif kind == "p":
            c_wp.wait()
        else:
            for v in range(u, u + (2 if kind == "u" else 1)):
                c_w[v].wait()

    def run(*steps):
        if fast:
            for i, s in steps:
                if i == "v":
                    vector.step(s)
                elif s < 0:
                    gather.begin(i)
                else:
                    gather.step(i, s)

    width = cfg_ref[0, 0]
    count = 1.0 / width.astype(F32)
    c_feat = load(0, feat_hbm, feat)
    if fast:
        pos = here()
        greet(pos)
        raws = [
            pltpu.make_async_copy(src, dst, sem_raw.at[i])
            for i, (src, dst) in enumerate(
                [(own_p, raw_p), (own_a, raw_a), (own_o, raw_o), (own_f, raw_f), (own_s, sv_held.at[0])]
            )
        ]
        for copy in raws:
            copy.start()
        gather = Gather(pos, wg, wp, stage, stage_p, g_send, g_recv)
        vector = VectorSum(pos, slice(0, 88), sv_held, sv_got, v_send, v_recv)
        for copy in raws:
            copy.wait()

        def arrange(c):
            rows = slice(24 * c, 24 * c + 24)
            stage_p[16 * c : 16 * c + 16, :] = raw_p[...]
            for j in range(3):
                for i in range(3):
                    stage[j, rows, 256 * i : 256 * i + 256] = raw_a[i, :, 256 * j : 256 * j + 256]
            stage[3, rows, :] = raw_o[...]
            for i in range(2):
                for q in range(4):
                    stage[4 + 4 * i + q, rows, :] = raw_f[i, :, D * q : D * q + D]

        by_core(pos, arrange)
        meet()
        by_core(pos, lambda c: gather.swap(0, c).start())
        vector.start(0)
        for i in range(1, len(PARTS)):
            by_core(pos, lambda c, i=i: gather.swap(i, c).start())
        run((0, -1), (1, -1))
    else:
        c_wp = load(1, wp_hbm, wp)
        c_w = [load(2 + u, wg_hbm.at[u], wg.at[u]) for u in range(12)]
    c_cot = load(14, cot_hbm, cot)
    fill_patterns(seg_ref, kpat, qpat)
    run(("v", 0), (0, 0), ("v", 1), (2, -1), (1, 0), (3, -1), ("v", 2), (0, 1))
    if fast:
        for i in range(VEC // 128):
            svec[0:1, 128 * i : 128 * i + 128] = sv_held[3, i : i + 1, :]
    c_feat.wait()
    need(0)

    @pl.loop(0, NT)
    def _(t):
        rows = rows_of(t)
        normed = norm0(feat, svec, rows)[2]
        h = (mm(normed, wp[...].reshape(FEAT, D)) + piece(svec, "bp")) * keep_row(D, width)
        hid[rows, :] = h
        low = h.astype(BF16)
        hl[rows, :] = low
        hlt[:, rows] = low.T

    save(hlt, hlt_out)
    run((2, 0), (1, 1), (3, 0), (4, -1), (5, -1))
    need(1)

    slots = [
        [[], [(2, 1), (3, 1)]],
        [[(4, 0), (6, -1)], [(5, 0), (7, -1), (4, 1), (2, 2)]],
        [[], [(6, 0), (8, -1)]],
        [[(4, 2), (5, 1), (7, 0)], []],
        [[], [(6, 1), (8, 0)]],
        [[(7, 1)], [(5, 2)]],
    ]

    def at_slot(p, e):
        if fast:
            for i in range(PAIRS):
                if slots[i][e]:

                    @pl.when(p == i)
                    def _(i=i):
                        run(*slots[i][e])

    @pl.loop(0, PAIRS)
    def _(p):
        for j in range(3):

            @pl.when(p == 2 * j)
            def _(j=j):
                if j:
                    need(1 + j)

        @pl.when(lax.rem(p, 2) == 0)
        def _():
            j = lax.div(p, 2)
            group = lanes_of(j, 256)

            @pl.loop(0, NT)
            def _(t):
                rows = rows_of(t)
                keep = keep_row(256, cfg_ref[0, 1] * HDIM - j * 256)
                o = mm(hl[rows, :], square(wg, j))
                bias = lambda name: svec[0:1, pl.ds(pl.multiple_of(OFFSETS[name] + j * 256, 128), 256)]
                qkv[0, rows, group] = ((o[:, 0:256] + bias("bq")) * keep).astype(BF16)
                k = (o[:, 256:512] * keep).astype(BF16)
                qkv[1, rows, group] = k
                v = ((o[:, 512:768] + bias("bv")) * keep).astype(BF16)
                qkv[2, rows, group] = v
                down = pl.ds(pl.multiple_of(j * 256, 256), 256)
                kt[down, rows] = k.T
                vt[down, rows] = v.T

        if fast:

            @pl.when(p == 2)
            def _():
                run((3, 2))

        lanes = lanes_of(p)
        for e in range(2):
            kaug = qkv[1, :, lanes] * half_mask(e) + kpat[e]
            head_rows = pl.ds(pl.multiple_of(p * 128 + 64 * e, 64), 64)
            for b in range(NT):
                lo, hi = KEY_RANGE[b]
                cols = slice(b * TILE, (b + 1) * TILE)
                qaug = qkv[0, cols, lanes] * (half_mask(e) * 0.125) + qpat[e, cols, :]
                st = mm_nt(kaug[lo:hi], qaug)
                peak = jnp.max(st, 0, keepdims=True)
                power = jnp.exp(st - peak)
                total = col_sum(power)
                ot = mm(vt[head_rows, lo:hi], power.astype(BF16))
                mixedt[head_rows, cols] = (ot * (1.0 / total)).astype(BF16)
                lse_out[pl.ds(2 * p + e, 1), cols] = peak + jnp.log(total)
            at_slot(p, e)

    save(qkv, qkv_out)
    save(kt, kt_out)
    save(mixedt, mixedt_out)
    need(4)

    @pl.loop(0, NT)
    def _(t):
        rows = rows_of(t)
        keep = keep_row(D, width)
        mix = mixedt[:, rows].T
        mixed[rows, :] = mix
        z = hid[rows, :] + (mm(mix, square(wg, 3)) + piece(svec, "bo")) * keep
        centred = (z - row_sum(z * keep) * count) * keep
        inv = lax.rsqrt(row_sum(centred * centred) * count + NORM_EPS)
        hat = centred * inv
        first = (hat * piece(svec, "g1") + piece(svec, "c1")) * keep
        xh1[rows, :] = hat.astype(BF16)
        inv1_out[rows, :] = jnp.broadcast_to(inv, (TILE, 128))
        hid[rows, :] = first + piece(svec, "b2") * keep
        low = first.astype(BF16)
        fl[rows, :] = low
        flt[:, rows] = low.T

    save(mixed, mixed_out)
    save(xh1, xh1_out)
    save(flt, flt_out)
    need(5)

    def up(q):
        @pl.loop(0, LEN // 512)
        def _(t):
            rows = span_of(t, 512)
            u = (mm(fl[rows, :], square(wg, 4 + q)) + piece(svec, "b1", q * D, D)) * keep_row(
                D, cfg_ref[0, 2], q * D
            )
            g, slope = gelu_both(u)
            active[q, rows, :] = g.astype(BF16)
            gp[q, rows, :] = slope.astype(BF16)

        save(active, active_out, q)
        save(gp, gp_out, q)

    def down(q):
        hid[...] += mm_nt(active[q], square(wg, 8 + q)) * keep_row(D, width)

    up(0)
    run((8, 1), (6, 2))
    up(1)
    need(6)
    up(2)
    run((7, 2))
    up(3)
    need(7)
    down(0)
    down(1)
    run((8, 2))
    need(8)
    down(2)
    down(3)
    c_cot.wait()
    zero = jnp.zeros((1, D), F32)

    def last(t, sums):
        gain_sum, shift_sum, bias_sum = sums
        rows = rows_of(t)
        keep = keep_row(D, width)
        z = hid[rows, :]
        centred = (z - row_sum(z * keep) * count) * keep
        inv = lax.rsqrt(row_sum(centred * centred) * count + NORM_EPS)
        hat = centred * inv
        gain = piece(svec, "g2")
        act[rows, :] = ((hat * gain + piece(svec, "c2")) * keep).astype(BF16)
        g = cot[rows, :].astype(F32) * keep
        gain_sum = gain_sum + col_sum(g * hat)
        shift_sum = shift_sum + col_sum(g)
        a = g * gain
        d2 = inv * (a - keep * (row_sum(a) * count) - hat * (row_sum(a * hat) * count))
        hid[rows, :] = d2
        low = d2.astype(BF16)
        dg[rows, :] = low
        dgt[:, rows] = low.T
        return gain_sum, shift_sum, bias_sum + col_sum(low.astype(F32))

    sums = (zero, zero, zero)
    for h in range(2):
        sums = lax.fori_loop(NT // 2 * h, NT // 2 * (h + 1), last, sums)
        rows = pl.ds(LEN // 2 * h, LEN // 2)
        save(act, act_out, rows)
        save(hid, d2_out, rows)
        save(dg, dg_out, rows)
        save(dgt, dgt_out, (slice(None), rows))
    sg_out[...] = jnp.zeros((88, 128), F32)
    for name, value in zip(("g2", "c2", "b2"), sums):
        put(sg_out, name, value)
    if fast:
        gather.finish()
        vector.finish()
    for make in outs:
        make().wait()


R_PARTS = [("u", 8), ("u", 4), ("u", 10), ("u", 6), ("h", 3), ("h", 0), ("h", 1), ("h", 2), ("p", 0)]
R_PLAIN = ((("x",), ("y",), Z), (("y",), ("x",), Z))
R_SHORT = ((("x", "y"), Z),) * 2
R_ROUTES = [R_PLAIN] * 7 + [R_SHORT] * 2


class Scatter:
    def __init__(self, pos, acc, got, given, first, fin, gout, goutp, send, recv, local, credit):
        self.pos, self.acc, self.got, self.given, self.first = pos, acc, got, given, first
        self.fin, self.gout, self.goutp = fin, gout, goutp
        self.send, self.recv, self.local, self.credit = send, recv, local, credit

    def trim(self, i):
        kind = R_PARTS[i][0]
        if kind == "u":
            return ()
        return (slice(0, 32 if kind == "p" else 48), slice(0, 384))

    def held(self, bufs, i, index):
        kind = R_PARTS[i][0]
        if kind == "p":
            return bufs[2].at[index]
        if kind == "h":
            return bufs[1].at[(i - 4,) + index]
        return bufs[0].at[(i,) + index]

    def slot(self, buf, i):
        full = (slice(None),) * 4
        return buf.at[(i % 2,) + full + self.trim(i)]

    def hand(self, i):
        return remote(
            self.slot(self.given, i), self.slot(self.first, i), self.send.at[i, 6], self.recv.at[i, 6],
            partner(self.pos, ("c",)),
        )

    def hops(self, i, s, c):
        route = R_ROUTES[i][c]
        first = sum(len(subsets(dims)) for dims in route[:s])
        rest = sum(route[s + 1 :], ())
        dst = self.held(self.got, i, cube(self.pos, rest, sum(route[: s + 1], ())))
        return [
            remote(
                self.held(self.acc, i, cube(self.pos, rest, dims)), dst,
                self.send.at[i, first + n], self.recv.at[i, first + n], partner(self.pos, dims),
            )
            for n, dims in enumerate(subsets(route[s]))
        ]

    def came(self, i, s, c):
        route = R_ROUTES[i][c]
        rest = sum(route[s + 1 :], ())
        before = sum(route[:s], ())
        return [
            self.held(self.got, i, cube(self.pos, rest, before + tuple(d for d in route[s] if d not in dims)))
            for dims in subsets(route[s])
        ]

    def offer(self, i):
        if i >= 2:
            pl.semaphore_wait(self.credit, 1)
        self.hand(i).start()

    def reuse(self, i):
        if i >= 2:
            self.hand(i - 2).wait_send()

    def begin(self, i):
        self.hand(i).wait_recv()
        mine = self.held(self.acc, i, (slice(None),) * 4)
        mine[...] = mine[...] + self.slot(self.first, i)[...]
        if i < len(R_PARTS) - 2:
            pl.semaphore_signal(
                self.credit, inc=1, device_id=partner(self.pos, ("c",)),
                device_id_type=pl.DeviceIdType.MESH,
            )

        def action(c):
            for copy in self.hops(i, 0, c):
                copy.start()

        by_core(self.pos, action)

    def ends(self, i, c, own):
        kind, u = R_PARTS[i]
        rows = 16 if kind == "p" else 24
        fin = self.held(self.fin, i, ())
        if kind == "p":
            dst = self.goutp.at[:, half(c)]
        elif kind == "h":
            dst = self.gout.at[u, :, half(c)]
        else:
            dst = self.gout.at[u + c]
        if own:
            return pltpu.make_async_copy(fin.at[pl.ds(rows * c, rows)], dst, self.local.at[i])
        return remote(
            fin.at[pl.ds(rows * (1 - c), rows)], dst, self.send.at[i, 7], self.recv.at[i, 7],
            partner(self.pos, ("c",)),
        )

    def step(self, i, s):
        def action(c):
            route = R_ROUTES[i][c]
            for copy in self.hops(i, s, c):
                copy.wait_recv()
            mine = self.held(self.acc, i, cube(self.pos, sum(route[s + 1 :], ())))
            total = mine[...].astype(F32)
            for came in self.came(i, s, c):
                total = total + came[...].astype(F32)
            if s < len(route) - 1:
                mine[...] = total.astype(BF16)
                for copy in self.hops(i, s + 1, c):
                    copy.start()
            else:
                self.held(self.fin, i, ())[...] = total
                for own in (True, False):
                    self.ends(i, c, own).start()

        by_core(self.pos, action)

    def finish(self):
        n = len(R_PARTS)
        for i in range(n - 2, n):
            self.hand(i).wait_send()

        def action(c):
            for i in range(n):
                for s in range(len(R_ROUTES[i][c])):
                    for copy in self.hops(i, s, c):
                        copy.wait_send()
                self.ends(i, c, True).wait()
                self.ends(i, c, False).wait_send()
                self.ends(i, 1 - c, False).wait_recv()

        by_core(self.pos, action)


def backward_kernel(fast, *refs):
    refs = list(refs)
    take = lambda n: [refs.pop(0) for _ in range(n)]
    seg_ref, cfg_ref, feat_hbm, wg_hbm, wp_hbm, svec = take(6)
    (
        hlt_hbm, qkv_hbm, kt_hbm, mixed_hbm, mixedt_hbm, xh1_hbm, inv1_hbm, flt_hbm,
        active_hbm, gp_hbm, d2_hbm, dg_hbm, dgt_hbm, lse, sg_in,
    ) = take(15)
    dx_out, gu_out, gwp_out, sg = take(4)
    (
        feat, wbuf, wp, pool, tr, kt, qkv, go, inv1, fg, dg, tg, delta, dqt, kpat, qpat,
        acc_u, acc_h, acc_p, given, sem_in, sem_q, sem_dx,
    ) = take(23)
    if fast:
        (
            got_u, got_h, got_p, first_in, fin_u, fin_h, fin_p, r_send, r_recv, r_local, credit,
            sv_held, sv_got, v_send, v_recv,
        ) = take(15)
        pos = here()
        core = pos["c"]
        small = sv_held.at[0]
        scatter = Scatter(
            pos, (acc_u, acc_h, acc_p), (got_u, got_h, got_p), given, first_in, (fin_u, fin_h, fin_p),
            gu_out, gwp_out, r_send, r_recv, r_local, credit,
        )
        late, early = (
            VectorSum(pos, rows, sv_held, sv_got, v_send.at[i], v_recv.at[i])
            for i, rows in enumerate((slice(0, 32), slice(32, 88)))
        )
    else:
        sem_out = take(1)[0]
        core = lax.axis_index("dp") % 2
        small = sg
        holder = Scatter(None, (acc_u, acc_h, acc_p), *[None] * 10)

    def load(i, src, dst):
        copy = pltpu.make_async_copy(src, dst, sem_in.at[i])
        copy.start()
        return copy

    def run(*steps):
        if fast:
            for i, s in steps:
                if i == "e":
                    early.step(s)
                elif i == "l":
                    late.step(s)
                elif s < 0:
                    scatter.begin(i)
                else:
                    scatter.step(i, s)

    def columns(h):
        return pl.ds(pl.multiple_of(384 * h, 128), 384)

    def plain_copy(i, mine):
        kind, u = R_PARTS[i]
        which = core if mine else 1 - core
        full = (slice(None),) * 4
        if mine:
            src = holder.held(holder.acc, i, full)
        else:
            src = given.at[(i % 2,) + full + holder.trim(i)]
        if kind == "p":
            dst = gwp_out.at[full + (slice(None), columns(which))]
        elif kind == "h":
            dst = gu_out.at[(u,) + full + (slice(None), columns(which))]
        else:
            dst = gu_out.at[u + which]
        return pltpu.make_async_copy(src, dst, sem_out.at[i, 1 if mine else 0])

    def make(i, mine, left, right):
        if not mine:
            if fast:
                scatter.reuse(i)
            elif i >= 2:
                plain_copy(i - 2, False).wait()
        value = mm(left[...], right[...]).astype(BF16).reshape(CUBE + (48, D))
        if mine:
            acc_u[i] = value
        else:
            given[i % 2] = value
        if fast:
            if not mine:
                scatter.offer(i)
        else:
            plain_copy(i, mine).start()

    def make_both(i, left, right):
        kind = R_PARTS[i][0]
        rows = 32 if kind == "p" else 48
        if fast:
            scatter.reuse(i)
        elif i >= 2:
            plain_copy(i - 2, False).wait()

        def action(c):
            @pl.loop(0, 2)
            def _(y):
                value = mm(left[span_of(y, 8 * rows), :], right[...]).astype(BF16)
                mine = value[:, half(c)].reshape(2, 2, 2, rows, 384)
                given[(i % 2, y) + (slice(None),) * 3 + (slice(0, rows), slice(0, 384))] = value[
                    :, half(1 - c)
                ].reshape(2, 2, 2, rows, 384)
                if kind == "p":
                    acc_p[y] = mine
                else:
                    acc_h[i - 4, y] = mine

        by_core(dict(c=core), action)
        if fast:
            scatter.offer(i)
        else:
            plain_copy(i, False).start()
            plain_copy(i, True).start()

    def quarter(k):
        s = k % 2
        q = 2 * (k // 2) + (core if k % 2 else 1 - core)
        pairs = [
            (active_hbm.at[q], pool.at[s]),
            (wg_hbm.at[8 + q], wbuf.at[s]),
            (gp_hbm.at[q], pool.at[2 + s]),
            (wg_hbm.at[4 + q], wbuf.at[2 + s]),
        ]
        return q, [
            pltpu.make_async_copy(src, dst, sem_q.at[s, i]) for i, (src, dst) in enumerate(pairs)
        ]

    dgt, flt, ig = tr.at[0], tr.at[1], pool.at[4]
    if fast:
        greet(pos)
    c_dgt = load(0, dgt_hbm, dgt)
    for copy in quarter(0)[1]:
        copy.start()
    c_dg = load(1, dg_hbm, dg)

    width = cfg_ref[0, 0]
    count = 1.0 / width.astype(F32)
    small[...] = sg_in[...]
    fill_patterns(seg_ref, kpat, qpat)
    c_dgt.wait()
    if fast:
        meet()
    events = {(1, 0): [(0, -1)], (1, 2): [(1, -1)], (3, 0): [(2, -1)], (3, 2): [(3, -1)]}
    for k in range(4):
        s = k % 2
        mine = bool(k % 2)
        q, copies = quarter(k)
        at = lambda n: run(*events.get((k, n), []))
        copies[0].wait()
        if k == 0:
            c_flt = load(2, flt_hbm, flt)
            c_d2 = load(3, d2_hbm, fg)
        make(2 * (k // 2), mine, dgt, pool.at[s])
        at(0)
        if k == 0:
            c_dg.wait()
            for copy in quarter(1)[1]:
                copy.start()
        if k == 1:
            c_xh1 = load(4, xh1_hbm, go)
            c_inv1 = load(5, inv1_hbm, inv1)
            c_mixed = load(6, mixed_hbm, pool.at[5])
        if k == 2:
            c_qkv = load(9, qkv_hbm, qkv)
            c_kt = load(10, kt_hbm, kt)
        if k == 3:
            c_wp = load(15, wp_hbm, wp)
            c_feat = load(16, feat_hbm, feat)
        copies[1].wait()
        copies[2].wait()

        def inner(t, bias, q=q, s=s):
            rows = pl.ds(0, LEN)
            low = (
                mm(dg[rows, :], square(wbuf, s))
                * pool[2 + s, rows, :].astype(F32)
                * keep_row(D, cfg_ref[0, 2] - q * D)
            ).astype(BF16)
            ig[rows, :] = low
            return bias + col_sum(low.astype(F32))

        put(small, "b1", inner(0, jnp.zeros((1, D), F32)), q * D)
        at(1)
        if k == 0:
            c_flt.wait()
            c_d2.wait()
        make(2 * (k // 2) + 1, mine, flt, ig)
        at(2)
        copies[3].wait()

        fg[...] += mm_nt(ig[...], square(wbuf, 2 + s))
        at(3)
        if k < 2:
            for copy in quarter(k + 2)[1]:
                copy.start()
        if k == 2:
            c_wo = load(8, wg_hbm.at[3], wbuf.at[0])
            c_wa = [load(12, wg_hbm.at[0], wbuf.at[2])]

    mixedt, hlt, mixed = tr.at[0], tr.at[1], pool.at[5]
    c_mixedt = load(7, mixedt_hbm, mixedt)
    c_hlt = load(11, hlt_hbm, hlt)
    c_wa.append(load(13, wg_hbm.at[1], wbuf.at[1]))
    c_wa.append(load(14, wg_hbm.at[2], wbuf.at[3]))
    wa_slot = (2, 1, 3)
    for copy in (c_xh1, c_inv1, c_mixed, c_wo):
        copy.wait()
    zero = jnp.zeros((1, D), F32)

    def middle(t, sums):
        gain_sum, shift_sum, bias_sum = sums
        rows = span_of(t, 512)
        keep = keep_row(D, width)
        hat = go[rows, :].astype(F32)
        g = fg[rows, :] * keep
        gain_sum = gain_sum + col_sum(g * hat)
        shift_sum = shift_sum + col_sum(g)
        a = g * piece(svec, "g1")
        d1 = inv1[rows, 0:1] * (a - keep * (row_sum(a) * count) - hat * (row_sum(a * hat) * count))
        fg[rows, :] = d1
        low = d1.astype(BF16)
        dg[rows, :] = low
        mg = mm_nt(low, square(wbuf, 0)).astype(BF16)
        go[rows, :] = mg
        product = mg.astype(F32) * mixed[rows, :].astype(F32)
        high = product.astype(BF16)
        rest = (product - high.astype(F32)).astype(BF16)
        lane = lax.broadcasted_iota(jnp.int32, (16, D), 1)
        head = lax.broadcasted_iota(jnp.int32, (16, D), 0)
        pick = ((lane >= head * HDIM) & (lane < head * HDIM + HDIM)).astype(F32).astype(BF16)
        delta[:, rows] = mm_nt(pick, high) + mm_nt(pick, rest)
        return gain_sum, shift_sum, bias_sum + col_sum(low.astype(F32))

    gain_sum, shift_sum, bias_sum = lax.fori_loop(0, LEN // 512, middle, (zero, zero, zero))
    put(small, "g1", gain_sum)
    put(small, "c1", shift_sum)
    put(small, "bo", bias_sum)
    if fast:
        early.start()
    run((0, 0))
    c_mixedt.wait()
    make_both(4, mixedt, dg)

    c_qkv.wait()
    c_kt.wait()
    c_hlt.wait()
    for copy in c_wa:
        copy.wait()
    slots = [
        [[], [(1, 0)], [(4, -1), ("e", 0)], []],
        [[], [(4, 0), (3, 0), (1, 1), (5, -1)], [("e", 2)], []],
        [[], [(3, 1), (6, -1)], [(1, 2), (4, 2)], []],
    ]
    after_loop = [[], [], [(5, 1)]]
    after_make = [[("e", 1), (0, 1), (2, 0)], [(4, 1), (2, 1)], []]
    after_back = [[], [(5, 0), (0, 2)], [(6, 0), (2, 2)]]

    def chunk(n):
        return n // 3, slice(256 * (n % 3), 256 * (n % 3) + 256)

    for j in range(3):

        def at_slot(pp, e, j=j):
            if fast:
                for i in range(2):
                    steps = slots[j][2 * i + e]
                    if steps:

                        @pl.when(pp == i)
                        def _(steps=steps):
                            run(*steps)

        @pl.loop(0, 2)
        def _(pp, j=j):
            p = j * 2 + pp
            lanes = lanes_of(p)
            for e in range(2):
                at_slot(pp, e)
                kaug = qkv[1, :, lanes] * half_mask(e) + kpat[e]
                head_rows = pl.ds(pl.multiple_of(p * 128 + 64 * e, 64), 64)
                for b in range(NT):
                    lo, hi = KEY_RANGE[b]
                    cols = slice(b * TILE, (b + 1) * TILE)
                    qaug = qkv[0, cols, lanes] * (half_mask(e) * 0.125) + qpat[e, cols, :]
                    st = mm_nt(kaug[lo:hi], qaug)
                    weights = jnp.exp(st - lse[pl.ds(2 * p + e, 1), cols])
                    n, span = chunk(4 * e + b)
                    pool[n, lo:hi, span] = weights.astype(BF16)
                    goe = go[cols, lanes] * half_mask(e)
                    dp = mm_nt(qkv[2, lo:hi, lanes], goe)
                    ds = (weights * (dp - delta[pl.ds(2 * p + e, 1), cols])).astype(BF16)
                    n, span = chunk(8 + 4 * e + b)
                    pool[n, lo:hi, span] = ds
                    dqt[64 * e : 64 * e + 64, cols] = mm(kt[head_rows, lo:hi], ds)
            keep = keep_row(128, cfg_ref[0, 1] * HDIM - p * 128)
            for t in range(NT):
                rows = slice(t * TILE, (t + 1) * TILE)
                dk = jnp.zeros((TILE, 128), F32)
                dv = jnp.zeros((TILE, 128), F32)
                for b in range(NT):
                    if not KEY_RANGE[b][0] <= t * TILE < KEY_RANGE[b][1]:
                        continue
                    cols = slice(b * TILE, (b + 1) * TILE)
                    for e in range(2):
                        n, span = chunk(8 + 4 * e + b)
                        dk = dk + mm(pool[n, rows, span], qkv[0, cols, lanes] * half_mask(e))
                        n, span = chunk(4 * e + b)
                        dv = dv + mm(pool[n, rows, span], go[cols, lanes] * half_mask(e))
                dq = dqt[:, rows].T
                for i, value in enumerate((dq * (keep * 0.125), dk * (keep * 0.125), dv * keep)):
                    tg[rows, pl.ds(pl.multiple_of(256 * i + pp * 128, 128), 128)] = value.astype(BF16)

        run(*after_loop[j])
        make_both(5 + j, hlt, tg)
        run(*after_make[j])

        fg[...] += mm_nt(tg[...], square(wbuf, wa_slot[j]))
        bias = lax.fori_loop(
            0, NT, lambda t, total: total + col_sum(tg[rows_of(t), :].astype(F32)), zero
        )
        put(small, "bq", bias[:, 0:256], 256 * j)
        put(small, "bv", bias[:, 512:768], 256 * j)
        run(*after_back[j])

    c_wp.wait()
    c_feat.wait()
    zero_feat = jnp.zeros((1, FEAT), F32)
    nrmt = tr.at[0]

    def first(t, bias_sum):
        rows = rows_of(t)
        nrmt[0:FEAT, rows] = norm0(feat, svec, rows)[2].T
        low = (fg[rows, :] * keep_row(D, width)).astype(BF16)
        dg[rows, :] = low
        return bias_sum + col_sum(low.astype(F32))

    put(small, "bp", lax.fori_loop(0, NT, first, zero))
    run((7, -1))
    make_both(8, nrmt, dg)

    def second(t, sums):
        gain_sum, shift_sum = sums
        rows = span_of(t, 512)
        hat, inv, _ = norm0(feat, svec, rows)
        g = mm_nt(dg[rows, :], wp[...].reshape(FEAT, D))
        gain_sum = gain_sum + col_sum(g * hat)
        shift_sum = shift_sum + col_sum(g)
        a = g * piece(svec, "g0")
        dx = inv * (a - row_sum(a) * (1.0 / FEAT) - hat * (row_sum(a * hat) * (1.0 / FEAT)))
        fg[rows, 0:FEAT] = 0.1 * dx
        return gain_sum, shift_sum

    gain_sum, shift_sum = lax.fori_loop(0, LEN // 512, second, (zero_feat, zero_feat))
    put(small, "g0", gain_sum)
    put(small, "b0", shift_sum)
    c_dx = pltpu.make_async_copy(fg.at[:, 0:FEAT], dx_out, sem_dx)
    c_dx.start()
    if fast:
        late.start()
        run((3, 2), (5, 2), (8, -1), (6, 1), ("l", 0), (7, 0), (8, 0), (6, 2), ("l", 1), (8, 1), (7, 1), ("l", 2))
        sg[...] = sv_held[3]
        early.finish()
        late.finish()
        scatter.finish()
    else:
        for i in range(len(R_PARTS)):
            plain_copy(i, True).wait()
        for i in range(len(R_PARTS) - 2, len(R_PARTS)):
            plain_copy(i, False).wait()
    c_dx.wait()


def adam_rule(weight, moment, square_in, grad, rate):
    moment_new = BETA_ONE * moment + (1.0 - BETA_ONE) * grad
    square_new = BETA_TWO * square_in + (1.0 - BETA_TWO) * grad * grad
    fix_one = 1.0 - BETA_ONE**STEP
    fix_two = 1.0 - BETA_TWO**STEP
    direction = moment_new / fix_one / (jnp.sqrt(square_new / fix_two) + ADAM_EPS)
    return (moment_new, square_new, weight - rate * (direction + DECAY * weight))


def adam_kernel(*refs):
    gu_hbm, gp_hbm, act_hbm, dx_hbm = refs[0:4]
    ins, act_out, dx_out, outs = refs[4:16], refs[16], refs[17], refs[18:34]
    gu, gp, act, dx = refs[34:38]
    held, new = refs[38:50], refs[50:62]
    sem_in, sem_out = refs[62:]
    sources = (gu_hbm,) + tuple(ins[9:12]) + (act_hbm, dx_hbm, gp_hbm) + tuple(ins[0:9])
    places = (gu,) + tuple(held[9:12]) + (act, dx, gp) + tuple(held[0:9])
    loads = [
        pltpu.make_async_copy(src, dst, sem_in.at[i]) for i, (src, dst) in enumerate(zip(sources, places))
    ]
    for copy in loads:
        copy.start()
    stores = []

    def store(src, dst):
        copy = pltpu.make_async_copy(src, dst, sem_out.at[len(stores)])
        copy.start()
        stores.append(copy)

    def update(k, pieces):
        w, m, v = held[3 * k : 3 * k + 3]
        for index, grad in pieces:
            done = adam_rule(w[index], m[index], v[index], grad(), RATE)
            for ref, value in zip(new[3 * k : 3 * k + 3], done):
                ref[index] = value
            m[index] = grad()
        for src, dst in zip((m,) + tuple(new[3 * k : 3 * k + 3]), outs[4 * k : 4 * k + 4]):
            store(src, dst)

    everything = (slice(None), slice(None))
    for copy in loads[0:4]:
        copy.wait()
    update(
        3,
        [
            ((i, slice(None), slice(D * q, D * q + D)), lambda i=i, q=q: gu[4 + 4 * i + q])
            for i in range(2) for q in range(4)
        ],
    )
    for copy in loads[4:6]:
        copy.wait()
    store(act, act_out)
    store(dx, dx_out)
    for copy in loads[6:16]:
        copy.wait()
    update(
        1,
        [
            ((i, slice(None), slice(256 * j, 256 * j + 256)), lambda i=i, j=j: gu[j, :, 256 * i : 256 * i + 256])
            for i in range(3) for j in range(3)
        ],
    )
    update(2, [(everything, lambda: gu[3])])
    update(0, [(everything, lambda: gp[...])])
    for copy in stores:
        copy.wait()


def adam_call(gu, gp, act, dx, state):
    shape = jax.ShapeDtypeStruct
    f32 = lambda s: pltpu.VMEM(s, F32)
    outs = [shape((LEN, D), BF16), shape((LEN, FEAT), F32)]
    outs += [shape(state[3 * k].shape, F32) for k in range(4) for _ in range(4)]
    scratch = [f32(gu.shape), f32(gp.shape), pltpu.VMEM((LEN, D), BF16), f32((LEN, FEAT))]
    scratch += [f32(x.shape) for x in state] * 2
    scratch += [pltpu.SemaphoreType.DMA((16,)), pltpu.SemaphoreType.DMA((18,))]
    return pl.pallas_call(
        adam_kernel,
        out_shape=outs,
        in_specs=[any_spec()] * 16,
        out_specs=[any_spec()] * 18,
        scratch_shapes=scratch,
        compiler_params=pltpu.CompilerParams(vmem_limit_bytes=VMEM_LIMIT),
        name="adam",
    )(gu, gp, act, dx, *state)


def any_spec():
    return pl.BlockSpec(memory_space=pl.ANY)


def vmem_spec():
    return pl.BlockSpec(memory_space=pltpu.VMEM)


def smem_spec():
    return pl.BlockSpec(memory_space=pltpu.SMEM)


def forward_call(fast, seg, cfg, feat, cot, weights):
    shape = jax.ShapeDtypeStruct
    outs = [
        (shape((LEN, D), BF16), any_spec()),
        (shape((D, LEN), BF16), any_spec()),
        (shape((3, LEN, D), BF16), any_spec()),
        (shape((D, LEN), BF16), any_spec()),
        (shape((LEN, D), BF16), any_spec()),
        (shape((D, LEN), BF16), any_spec()),
        (shape((LEN, D), BF16), any_spec()),
        (shape((LEN, 128), F32), vmem_spec()),
        (shape((D, LEN), BF16), any_spec()),
        (shape((4, LEN, D), BF16), any_spec()),
        (shape((4, LEN, D), BF16), any_spec()),
        (shape((LEN, D), F32), any_spec()),
        (shape((LEN, D), BF16), any_spec()),
        (shape((D, LEN), BF16), any_spec()),
        (shape((16, LEN), F32), vmem_spec()),
        (shape((88, 128), F32), vmem_spec()),
    ]
    if fast:
        outs += [
            (shape((12,) + CUBE + (48, D), BF16), any_spec()),
            (shape(CUBE + (32, D), BF16), any_spec()),
            (shape((1, VEC), F32), vmem_spec()),
        ]
    bf = lambda *s: pltpu.VMEM(s, BF16)
    f32 = lambda *s: pltpu.VMEM(s, F32)
    dma = lambda *s: pltpu.SemaphoreType.DMA(s)
    scratch = [
        bf(LEN, FEAT), bf(LEN, D), bf(12, *CUBE, 48, D), bf(*CUBE, 32, D), f32(LEN, D),
        bf(LEN, D), bf(D, LEN), bf(3, LEN, D), bf(D, LEN), bf(D, LEN), bf(LEN, D), bf(D, LEN),
        bf(LEN, D), bf(LEN, D), bf(D, LEN), bf(4, LEN, D), bf(4, LEN, D), bf(LEN, D), bf(D, LEN),
        bf(2, LEN, 128), bf(2, LEN, 128), dma(15), dma(32),
    ]
    if fast:
        scratch += [
            f32(16, D), f32(3, 24, D), f32(24, D), f32(2, 24, FF), f32(12, 48, D), f32(32, D), dma(5),
            dma(len(PARTS), 11), dma(len(PARTS), 11), f32(4, 88, 128), f32(7, 88, 128), dma(7), dma(7),
        ]
        specs = [any_spec()] * len(weights)
        params = dict(collective_id=0, has_side_effects=True)
    else:
        specs = [any_spec()] * 2 + [vmem_spec()]
        params = {}
    return pl.pallas_call(
        functools.partial(forward_kernel, fast),
        out_shape=[o[0] for o in outs],
        in_specs=[smem_spec(), smem_spec()] + [any_spec()] * 2 + specs,
        out_specs=[o[1] for o in outs],
        scratch_shapes=scratch,
        compiler_params=pltpu.CompilerParams(vmem_limit_bytes=VMEM_LIMIT, **params),
        name="forward",
    )(seg, cfg, feat, cot, *weights)


def backward_call(fast, seg, cfg, feat, wg, wp, svec, saved):
    shape = jax.ShapeDtypeStruct
    bf = lambda *s: pltpu.VMEM(s, BF16)
    f32 = lambda *s: pltpu.VMEM(s, F32)
    dma = lambda *s: pltpu.SemaphoreType.DMA(s)
    n = len(R_PARTS)
    scratch = [
        bf(LEN, FEAT), bf(4, *CUBE, 48, D), bf(*CUBE, 32, D), bf(6, LEN, D), bf(2, D, LEN), bf(D, LEN),
        bf(3, LEN, D), bf(LEN, D), f32(LEN, 128), f32(LEN, D), bf(LEN, D), bf(LEN, D), f32(16, LEN),
        f32(128, LEN), bf(2, LEN, 128), bf(2, LEN, 128),
        bf(4, *CUBE, 48, D), bf(4, *CUBE, 48, 384), bf(*CUBE, 32, 384), bf(2, *CUBE, 48, D),
        dma(17), dma(2, 4), pltpu.SemaphoreType.DMA,
    ]
    if fast:
        scratch += [
            bf(4, *CUBE, 48, D), bf(4, *CUBE, 48, 384), bf(*CUBE, 32, 384), bf(2, *CUBE, 48, D),
            f32(4, 48, D), f32(4, 48, 384), f32(32, 384), dma(n, 8), dma(n, 8), dma(n),
            pltpu.SemaphoreType.REGULAR, f32(4, 88, 128), f32(7, 88, 128), dma(2, 7), dma(2, 7),
        ]
        grads = [shape((12, 24, D), F32), shape((16, D), F32)]
        params = dict(collective_id=1, has_side_effects=True)
    else:
        scratch += [dma(n, 2)]
        grads = [shape((12,) + CUBE + (48, D), BF16), shape(CUBE + (32, D), BF16)]
        params = {}
    return pl.pallas_call(
        functools.partial(backward_kernel, fast),
        out_shape=[shape((LEN, FEAT), F32)] + grads + [shape((88, 128), F32)],
        in_specs=[smem_spec(), smem_spec()] + [any_spec()] * 3 + [vmem_spec()]
        + [any_spec()] * 13 + [vmem_spec()] * 2,
        out_specs=[any_spec()] * 3 + [vmem_spec()],
        scratch_shapes=scratch,
        compiler_params=pltpu.CompilerParams(vmem_limit_bytes=VMEM_LIMIT, **params),
        name="backward",
    )(seg, cfg, feat, wg, wp, svec, *saved)


AXES = ("grp", "dp")


def gathered(projection_weight, attention_weight, output_weight, feedforward_weight, small_params):
    gather = lambda w, axis: lax.all_gather(w.astype(BF16), AXES, axis=axis, tiled=True)
    wp = gather(projection_weight, 0)
    wa = gather(attention_weight, 1)
    wo = gather(output_weight, 0)
    wf = gather(feedforward_weight, 1)
    svec = gather(small_params, 0).astype(F32).reshape(1, VEC)
    return units(wp, wa, wo, wf) + (svec,)


def units(wp, wa, wo, wf):
    groups = wa.reshape(3, D, 3, 256).transpose(2, 1, 0, 3).reshape(3, D, D)
    quarters = wf.reshape(2, D, 4, D).transpose(0, 2, 1, 3).reshape(8, D, D)
    wg = jnp.concatenate([groups, wo[None], quarters], 0)
    return wg.reshape((12,) + CUBE + (48, D)), wp.reshape(CUBE + (32, D))


def layer(fast, features, lengths, config, cotangent, weights):
    feat = features.reshape(LEN, FEAT)
    cot = cotangent.reshape(LEN, D)
    saved = forward_call(fast, lengths, config, feat, cot, weights)
    activations = saved[0]
    wg, wp, svec = saved[16:] if fast else weights
    dx, gu, gwp, sg = backward_call(fast, lengths, config, feat, wg, wp, svec, saved[1:16])
    return activations, dx, gu, gwp, sg


def per_device(
    fast,
    features, segment_lengths, subnet_config, cotangent,
    projection_weight, projection_moment, projection_square,
    attention_weight, attention_moment, attention_square,
    output_weight, output_moment, output_square,
    feedforward_weight, feedforward_moment, feedforward_square,
    small_params, small_moment, small_square,
):
    weights = (projection_weight, attention_weight, output_weight, feedforward_weight)
    if fast:
        me = lax.axis_index(AXES)
        low = lax.reduce_precision(small_params, 8, 7)
        placed = lax.dynamic_update_slice(jnp.zeros((88 * 128,), F32), low, (me * low.shape[0],))
        weights = weights + (placed.reshape(88, 128),)
    else:
        weights = gathered(*weights, small_params)
    activations, dx, gu, gwp, sg = layer(
        fast, features, segment_lengths, subnet_config, cotangent, weights
    )
    state = (
        projection_weight, projection_moment, projection_square,
        attention_weight, attention_moment, attention_square,
        output_weight, output_moment, output_square,
        feedforward_weight, feedforward_moment, feedforward_square,
        small_params[None], small_moment[None], small_square[None],
    )
    out = [activations.reshape(1, LEN, D), dx.reshape(1, LEN, FEAT)]
    vec = sg.reshape(88 * 128)
    if fast:
        gs = lax.dynamic_slice(vec, (me * small_params.shape[0],), small_params.shape)
        done = adam_call(gu, gwp, activations, dx, state[:12])
        return (
            (done[0].reshape(1, LEN, D), done[1].reshape(1, LEN, FEAT))
            + tuple(done[2:18])
            + (gs,) + adam_rule(small_params, small_moment, small_square, gs, SMALL_RATE)
        )
    gu = gu.reshape(12, D, D).astype(F32)
    scatter = lambda g, dim: lax.psum_scatter(g, AXES, scatter_dimension=dim, tiled=True)
    ga = gu[0:3].reshape(3, D, 3, 256).transpose(2, 1, 0, 3).reshape(3, D, D)
    gf = gu[4:12].reshape(2, 4, D, D).transpose(0, 2, 1, 3).reshape(2, D, FF)
    sums = (
        scatter(gwp.reshape(FEAT, D).astype(F32), 0), scatter(ga, 1), scatter(gu[3], 0), scatter(gf, 1),
        scatter(vec[:VEC], 0)[None],
    )
    for k, g in enumerate(sums):
        new = (g,) + adam_rule(*state[3 * k : 3 * k + 3], g, RATE if k < 4 else SMALL_RATE)
        out.extend(x[0] if k == 4 else x for x in new)
    return tuple(out)


def solution(mesh):
    rows3, rows2, stacked, flat = (
        P(AXES, None, None), P(AXES, None), P(None, AXES, None), P(AXES),
    )
    return jax.shard_map(
        functools.partial(per_device, dict(mesh.shape) == dict(grp=4, dp=8)),
        mesh=mesh,
        in_specs=(
            rows3, rows2, P("grp", None), rows3, rows2, rows2, rows2, stacked, stacked, stacked,
            rows2, rows2, rows2, stacked, stacked, stacked, flat, flat, flat,
        ),
        out_specs=(rows3, rows3) + (rows2,) * 4 + (stacked,) * 4 + (rows2,) * 4 + (stacked,) * 4 + (flat,) * 4,
        check_vma=False,
    )
```
